32 devices in a mesh: wide: 8 (over z, y), narrow: 4 (over x, core).
Axes of the slice: x: 2, y: 2, z: 4, core: 2. Of those that a mesh axis runs over, the one named last changes fastest.
Arguments:
- features: float32 [8192, 602], P(('wide', 'narrow')), may hold values from -6 to 6
- adjacency: int32 [8192, 8192], P('wide', 'narrow'), may hold values from 0 to 1, as said below
- labels: int32 [8192, 121], P(('wide', 'narrow')), may hold values 0 or 1
- labelled: int32 [8192], P(('wide', 'narrow')), may hold values from 0 to 1, as said below
- node_count: int32 [8192], P(('wide', 'narrow')), may hold values from 1 to 8
- w_in: float32 [602, 512], P(None, ('wide', 'narrow')), may hold values from -0.25 to 0.25
- w_side: float32 [3, 1024, 512], P(None, ('wide', 'narrow')), may hold values from -0.25 to 0.25
- w_proj: float32 [3, 1024, 512], P(None, ('wide', 'narrow')), may hold values from -0.1875 to 0.1875
- w_out: float32 [512, 121], P(('wide', 'narrow')), may hold values from -0.25 to 0.25
- row_in: float32 [602], replicated, may hold values from 8.5449216e-08 to 3.4179686e-07
- col_in: float32 [512], P(('wide', 'narrow')), may hold values from 8.5449216e-08 to 3.4179686e-07
- row_side: float32 [3, 1024], P(None, ('wide', 'narrow')), may hold values from 1.8310547e-07 to 7.324219e-07
- col_side: float32 [3, 512], replicated, may hold values from 1.8310547e-07 to 7.324219e-07
- row_proj: float32 [3, 1024], P(None, ('wide', 'narrow')), may hold values from 6.1035155e-07 to 2.4414062e-06
- col_proj: float32 [3, 512], replicated, may hold values from 6.1035155e-07 to 2.4414062e-06
- row_out: float32 [512], P(('wide', 'narrow')), may hold values from 2.4414063e-05 to 9.765625e-05
- col_out: float32 [121], replicated, may hold values from 2.4414063e-05 to 9.765625e-05
Outputs:
- loss_sum: float32 [], replicated
- label_count: float32 [], replicated
- grad_in: float32 [602, 512], P(None, ('wide', 'narrow'))
- grad_side: float32 [3, 1024, 512], P(None, ('wide', 'narrow'))
- grad_proj: float32 [3, 1024, 512], P(None, ('wide', 'narrow'))
- grad_out: float32 [512, 121], P(('wide', 'narrow'))
- new_in: float32 [602, 512], P(None, ('wide', 'narrow'))
- new_side: float32 [3, 1024, 512], P(None, ('wide', 'narrow'))
- new_proj: float32 [3, 1024, 512], P(None, ('wide', 'narrow'))
- new_out: float32 [512, 121], P(('wide', 'narrow'))
- new_row_in: float32 [602], replicated
- new_col_in: float32 [512], P(('wide', 'narrow'))
- new_row_side: float32 [3, 1024], P(None, ('wide', 'narrow'))
- new_col_side: float32 [3, 512], replicated
- new_row_proj: float32 [3, 1024], P(None, ('wide', 'narrow'))
- new_col_proj: float32 [3, 512], replicated
- new_row_out: float32 [512], P(('wide', 'narrow'))
- new_col_out: float32 [121], replicated
The draws below stay inside these ranges and needn't reach their ends.
Inputs may be any that keep to these rules, and one draw needn't show every extreme that they name: `adjacency`: each row has a drawn edge density; every row and column of a block may hold edges. The last node is labelled.
All inputs are finite; a program needn't handle non-finite values. No bound on the sum of `labels` on one device may be relied on, other than what follows from the above.
Results may differ from the reference program's by a relative error of at most 0.0003.
Values sent between devices are 32-bit elements; how exact they have to be, the bound alone decides.
A program may use at most 192 MiB of HBM per device.

```python
import math
import jax
import jax.numpy as jnp
from jax import lax

F_IN = 602
HID = 512
CLS = 121
LAYERS = 3
TOK_DEV = 256
NODES = 8192
N_WIDE = 8
N_NARROW = 4


def draw_adjacency(key, part):
    key = jax.random.fold_in(key, 11)
    rate_key, edge_key = jax.random.split(key)
    level = jax.random.randint(rate_key, (NODES,), 0, 65)
    density = 8 + level * level * level // 2000
    picks = jax.random.randint(edge_key, (NODES, NODES), 0, 4096)
    return (picks < density[:, None]).astype(jnp.int32)


def draw_labelled(key, part):
    key = jax.random.fold_in(key, 23)
    index = jnp.arange(NODES)
    device = index // TOK_DEV
    wide_pos = device // N_NARROW
    narrow_pos = device % N_NARROW
    level = 250 + 250 * wide_pos // max(N_WIDE - 1, 1) + 250 * narrow_pos // max(N_NARROW - 1, 1)
    picks = jax.random.randint(key, (NODES,), 0, 1000)
    marked = (picks < level).astype(jnp.int32)
    return jnp.where(index == NODES - 1, 1, marked).astype(jnp.int32)


def with_ends(entries, own_key, least, largest):
    shape = entries.shape
    place = [jax.random.randint(jax.random.fold_in(own_key, axis), (), 0, shape[axis]) for axis in range(len(shape))]
    entries = entries.at[tuple(place)].set(least)
    longest = shape.index(max(shape))
    place[longest] = (place[longest] + 1) % shape[longest]
    return entries.at[tuple(place)].set(largest)


def block_levels(stream_key, extent, shards, least, high):
    level, own = 1.0, jax.random.fold_in(stream_key, 6)
    for dim, shards_of in shards:
        draws = jnp.exp(jax.random.uniform(jax.random.fold_in(own, dim), (shards_of,), jnp.float32, least / len(shards), high / len(shards)))
        level = level * jnp.repeat(draws, extent[dim] // shards_of).reshape([-1 if axis == dim else 1 for axis in range(len(extent))])
    return level


def normal_values(stream_key, shape, scale, limit, cuts=(), kind=jnp.bfloat16):
    loudness = block_levels(stream_key, shape, cuts, -0.22, 0.18) if cuts else 1.0
    result = jax.random.normal(stream_key, shape, jnp.float32) * scale * loudness
    return jnp.minimum(jnp.maximum(result, -limit), limit).astype(kind)


def setup_inputs(seed: int = 0) -> dict:
    seeds = jax.random.split(jax.random.key(seed), 18)
    features = normal_values(seeds[0], (NODES, F_IN), 1.0, 6.0, ((0, 32),), jnp.float32)
    adjacency = draw_adjacency(jax.random.fold_in(seeds[17], 71), 0)
    labels = with_ends((jax.random.randint(seeds[2], (NODES, CLS), 0, 2) < 1).astype(jnp.int32), jax.random.fold_in(seeds[2], 1), 0, 1)
    labelled = draw_labelled(jax.random.fold_in(seeds[17], 71), 0)
    node_count = with_ends(jax.random.randint(seeds[4], (NODES,), 1, 9), jax.random.fold_in(seeds[4], 1), 1, 8).astype(jnp.int32)
    w_in = normal_values(seeds[5], (F_IN, HID), F_IN ** -0.5, 0.25, ((1, 32),), jnp.float32)
    w_side = normal_values(seeds[6], (LAYERS, 2 * HID, HID), HID ** -0.5, 0.25, ((1, 32),), jnp.float32)
    w_proj = normal_values(seeds[7], (LAYERS, 2 * HID, HID), (2 * HID) ** -0.5, 0.1875, ((1, 32),), jnp.float32)
    w_out = normal_values(seeds[8], (HID, CLS), HID ** -0.5, 0.25, ((0, 32),), jnp.float32)
    row_in = jnp.clip(jnp.exp(jax.random.uniform(seeds[9], (F_IN,), jnp.float32, math.log(8.544921570319275e-08), math.log(3.41796862812771e-07))), 8.544921570319275e-08, 3.41796862812771e-07)
    col_in = jnp.clip(jnp.exp(math.log(3.41796862812771e-07) - 1.3862944 * jax.random.uniform(seeds[10], (HID,), jnp.float32) ** block_levels(seeds[10], (HID,), ((0, 32),), -0.2, 0.2)), 8.544921570319275e-08, 3.41796862812771e-07)
    row_side = jnp.clip(jnp.exp(math.log(7.324218813664629e-07) - 1.3862944 * jax.random.uniform(seeds[11], (LAYERS, 2 * HID), jnp.float32) ** block_levels(seeds[11], (LAYERS, 2 * HID), ((1, 32),), -0.2, 0.2)), 1.8310547034161573e-07, 7.324218813664629e-07)
    col_side = jnp.clip(jnp.exp(jax.random.uniform(seeds[12], (LAYERS, HID), jnp.float32, math.log(1.8310547034161573e-07), math.log(7.324218813664629e-07))), 1.8310547034161573e-07, 7.324218813664629e-07)
    row_proj = jnp.clip(jnp.exp(math.log(2.441406195430318e-06) - 1.3862944 * jax.random.uniform(seeds[13], (LAYERS, 2 * HID), jnp.float32) ** block_levels(seeds[13], (LAYERS, 2 * HID), ((1, 32),), -0.2, 0.2)), 6.103515488575795e-07, 2.441406195430318e-06)
    col_proj = jnp.clip(jnp.exp(jax.random.uniform(seeds[14], (LAYERS, HID), jnp.float32, math.log(6.103515488575795e-07), math.log(2.441406195430318e-06))), 6.103515488575795e-07, 2.441406195430318e-06)
    row_out = jnp.clip(jnp.exp(math.log(9.765625145519152e-05) - 1.3862944 * jax.random.uniform(seeds[15], (HID,), jnp.float32) ** block_levels(seeds[15], (HID,), ((0, 32),), -0.2, 0.2)), 2.441406286379788e-05, 9.765625145519152e-05)
    col_out = jnp.clip(jnp.exp(jax.random.uniform(seeds[16], (CLS,), jnp.float32, math.log(2.441406286379788e-05), math.log(9.765625145519152e-05))), 2.441406286379788e-05, 9.765625145519152e-05)
    return {"features": features, "adjacency": adjacency, "labels": labels, "labelled": labelled, "node_count": node_count, "w_in": w_in, "w_side": w_side, "w_proj": w_proj, "w_out": w_out, "row_in": row_in, "col_in": col_in, "row_side": row_side, "col_side": col_side, "row_proj": row_proj, "col_proj": col_proj, "row_out": row_out, "col_out": col_out}


@jax.custom_vjp
def low(v):
    return lax.optimization_barrier(v.astype(jnp.bfloat16)).astype(jnp.float32)

@jax.custom_vjp
def low_back(v):
    return v

def low_keep(v):
    return (low(v), None)

def low_pass(kept, grad):
    return (grad,)

def back_keep(v):
    return (v, None)

def back_low(kept, grad):
    return (low(grad),)
low.defvjp(low_keep, low_pass)
low_back.defvjp(back_keep, back_low)
norm_eps = 1e-06
stat_eps = 1e-30
clip_level = 0.5
step_rate = 0.04

def matmul(left, right):
    return jnp.dot(left, right, precision=lax.Precision.HIGHEST, preferred_element_type=jnp.float32)

def column_order(values):
    width = values.shape[1]
    blocks = values.reshape(N_WIDE, N_NARROW, TOK_DEV, width)
    return jnp.transpose(blocks, (1, 0, 2, 3)).reshape(NODES, width)

def factored(grad, row_old, col_old):
    square = grad * grad
    row_new = 0.5 * row_old + 0.5 * (lax.optimization_barrier(jnp.mean(square, -1)) + stat_eps)
    col_new = 0.5 * col_old + 0.5 * (lax.optimization_barrier(jnp.mean(square, -2)) + stat_eps)
    row_mean = lax.optimization_barrier(jnp.mean(row_new, -1))
    vhat = row_new[..., :, None] * col_new[..., None, :] / row_mean[..., None, None]
    update = grad * lax.rsqrt(vhat)
    rms = jnp.sqrt(lax.optimization_barrier(jnp.mean(update * update, (-2, -1))))
    factor = 1.0 / jnp.maximum(1.0, rms / clip_level)
    return (update * factor[..., None, None], row_new, col_new)

def reference(features, adjacency, labels, labelled, node_count, w_in, w_side, w_proj, w_out, row_in, col_in, row_side, col_side, row_proj, col_proj, row_out, col_out):
    adj_float = adjacency.astype(jnp.float32)
    degree = 1.0 + lax.optimization_barrier(jnp.sum(adj_float, 1))
    counts = node_count.astype(jnp.float32)
    alpha = 2.0 / (1.0 + counts)
    lam = lax.rsqrt(counts)
    target = labels.astype(jnp.float32)
    weight_mask = labelled.astype(jnp.float32)
    label_count = jnp.sum(weight_mask)

    def loss_fn(p_in, p_side, p_proj, p_out):
        hidden = matmul(features, p_in)
        for layer in range(LAYERS):
            side = p_side[layer]
            proj = p_proj[layer]
            agg = matmul(adj_float, column_order(alpha[:, None] * hidden)) / degree[:, None]
            joined = jnp.concatenate([matmul(hidden, side[:HID]), matmul(agg, side[HID:])], 1)
            act = jax.nn.silu(matmul(joined, proj))
            hidden = act * lax.rsqrt(lax.optimization_barrier(jnp.mean(act * act, -1, keepdims=True)) + norm_eps)
        logits = matmul(hidden, p_out)
        per = lax.optimization_barrier(jnp.sum(jax.nn.softplus(logits) - target * logits, -1))
        total = jnp.sum(weight_mask * lam * per)
        return (total / label_count, total)
    loss, pullback, loss_sum = jax.vjp(loss_fn, w_in, w_side, w_proj, w_out, has_aux=True)
    grad_in, grad_side, grad_proj, grad_out = pullback(jnp.ones((), jnp.float32))
    up_in, new_row_in, new_col_in = factored(grad_in, row_in, col_in)
    up_side, new_row_side, new_col_side = factored(grad_side, row_side, col_side)
    up_proj, new_row_proj, new_col_proj = factored(grad_proj, row_proj, col_proj)
    up_out, new_row_out, new_col_out = factored(grad_out, row_out, col_out)
    return (loss_sum, label_count, grad_in, grad_side, grad_proj, grad_out, w_in - step_rate * up_in, w_side - step_rate * up_side, w_proj - step_rate * up_proj, w_out - step_rate * up_out, new_row_in, new_col_in, new_row_side, new_col_side, new_row_proj, new_col_proj, new_row_out, new_col_out)
```

```python
import functools
import jax
import jax.numpy as jnp
from jax import lax
from jax.experimental import pallas as pl
from jax.experimental.pallas import tpu as pltpu
from jax.sharding import PartitionSpec as P

MESH = pl.DeviceIdType.MESH
LANES = 128
CORES = 2
f32 = jnp.float32
bf16 = jnp.bfloat16


def grid_of(mesh):
    wide, narrow = mesh.shape["wide"], mesh.shape["narrow"]
    far = 4 if wide % 4 == 0 else wide
    return far, wide // far, narrow // CORES, CORES


def place(dims):
    far, near, across, cores = dims
    wide, narrow = lax.axis_index("wide"), lax.axis_index("narrow")
    return wide // near, lax.rem(wide, near), narrow // cores, lax.rem(narrow, cores)


def device(dims, far_at, near_at, across_at, core_at):
    return (far_at * dims[1] + near_at, across_at * dims[3] + core_at)


def send(src, dst, send_sem, recv_sem, target):
    pltpu.make_async_remote_copy(
        src_ref=src,
        dst_ref=dst,
        send_sem=send_sem,
        recv_sem=recv_sem,
        device_id=target,
        device_id_type=MESH,
    ).start()


def arrived(dst, recv_sem):
    pltpu.make_async_copy(dst, dst, recv_sem).wait()


def left_source(src, send_sem):
    pltpu.make_async_copy(src, src, send_sem).wait()


def halves(value):
    high = value.astype(bf16)
    return high, (value - high.astype(f32)).astype(bf16)


def neighbours(dims, at):
    far, near, across, cores = dims
    p, q, x, c = at
    always = [(p, lax.rem(q + step, near), x, c) for step in range(1, near)]
    always += [(p, q, lax.rem(x + step, across), c) for step in range(1, across)]
    always += [(p, q, x, 1 - c)]
    return always


def entry_barrier(dims, at):
    far, near, across, cores = dims
    p, q, x, c = at
    barrier = pltpu.get_barrier_semaphore()
    steady = neighbours(dims, at)
    for other in steady:
        pl.semaphore_signal(barrier, inc=1, device_id=device(dims, *other), device_id_type=MESH)

    @pl.when(p > 0)
    def _():
        pl.semaphore_signal(barrier, inc=1, device_id=device(dims, p - 1, q, x, c), device_id_type=MESH)

    @pl.when(p < far - 1)
    def _():
        pl.semaphore_signal(barrier, inc=1, device_id=device(dims, p + 1, q, x, c), device_id_type=MESH)

    ends = jnp.where(p > 0, 1, 0) + jnp.where(p < far - 1, 1, 0)
    pl.semaphore_wait(barrier, len(steady) + ends)


def chunk(ref, k):
    return ref.at[:, pl.ds(k * LANES, LANES)]


def forward_kernel(dims, chunks, adj, sent, out, gathered, pair, part, from_core, from_across, to_right, to_left, to_near, came, core_sems, across_out, across_in):
    far, near, across, cores = dims
    p, q, x, c = at = place(dims)
    nodes = sent.shape[0]
    early = chunks - 1
    right, left = device(dims, p + 1, q, x, c), device(dims, p - 1, q, x, c)
    others = [lax.rem(q + step, near) for step in range(1, near)]
    entry_barrier(dims, at)

    def go_right(k, pp, qq, src):
        @pl.when(p < far - 1)
        def _():
            send(src, gathered.at[k, pp, qq], to_right.at[k, pp, qq], came.at[k, pp, qq], right)

    def go_left(k, pp, qq, src):
        @pl.when(p > 0)
        def _():
            send(src, gathered.at[k, pp, qq], to_left.at[k, pp, qq], came.at[k, pp, qq], left)

    def go_near(k, pp, src):
        for step, qq in enumerate(others):
            send(src, gathered.at[k, pp, q], to_near.at[k, pp, step], came.at[k, pp, q], device(dims, p, qq, x, c))

    for k in [early] + list(range(chunks - 1)):
        src = chunk(sent, k)
        go_near(k, p, src)
        go_right(k, p, q, src)
        go_left(k, p, q, src)
    for k in range(chunks):
        gathered[k, p, q] = sent[:, k * LANES : (k + 1) * LANES]
    for qq in others:
        arrived(gathered.at[early, p, qq], came.at[early, p, qq])
        go_right(early, p, qq, gathered.at[early, p, qq])
        go_left(early, p, qq, gathered.at[early, p, qq])
    for step in range(1, far):
        for k in range(chunks):
            for side in range(2):
                pp = p - step if side == 0 else p + step
                onward = go_right if side == 0 else go_left

                @pl.when(pp >= 0 if side == 0 else pp < far)
                def _(k=k, pp=pp, onward=onward):
                    for qq in [q] + (others if k == early else []):
                        block = gathered.at[k, pp, qq]
                        arrived(block, came.at[k, pp, qq])
                        onward(k, pp, qq, block)
                    if k != early:
                        go_near(k, pp, gathered.at[k, pp, q])

    def reduce_across(k):
        arrived(from_core.at[k], core_sems.at[1, k])
        for step in range(1, across):
            xx = lax.rem(x + step, across)
            part[k, c, xx] = part[k, c, xx] + from_core[k, xx]
            send(part.at[k, c, xx], from_across.at[k, x], across_out.at[k, xx], across_in.at[k, x], device(dims, p, q, xx, c))

    def finish(k):
        total = part[k, c, x] + from_core[k, x]
        for step in range(1, across):
            xx = lax.rem(x + step, across)
            arrived(from_across.at[k, xx], across_in.at[k, xx])
            total = total + from_across[k, xx]
        out[:, k * LANES : (k + 1) * LANES] = total

    for k in range(chunks):
        if k != early:
            for pp in range(far):
                for qq in others:
                    arrived(gathered.at[k, pp, qq], came.at[k, pp, qq])
        high, low = halves(gathered[k].reshape(far * near * nodes, LANES))
        pair[:, :LANES] = high
        pair[:, LANES:] = low

        def product(index, carry, k=k):
            cc = lax.rem(index // across + 1 + c, cores)
            xx = lax.rem(index, across)
            rows = pl.multiple_of((xx * cores + cc) * nodes, nodes)
            both = jnp.dot(adj[pl.ds(rows, nodes), :], pair[...], preferred_element_type=f32)
            part[k, cc, xx] = both[:, :LANES] + both[:, LANES:]

            @pl.when(index == across - 1)
            def _():
                send(part.at[k, 1 - c], from_core.at[k], core_sems.at[0, k], core_sems.at[1, k], device(dims, p, q, x, 1 - c))

            return carry

        lax.fori_loop(0, cores * across, product, 0)
        if k >= 1:
            reduce_across(k - 1)
        if k >= 2:
            finish(k - 2)
    reduce_across(chunks - 1)
    if chunks >= 2:
        finish(chunks - 2)
    finish(chunks - 1)

    for k in range(chunks):
        left_source(part.at[k, 1 - c], core_sems.at[0, k])
        for step in range(1, across):
            xx = lax.rem(x + step, across)
            left_source(part.at[k, c, xx], across_out.at[k, xx])
        for pp in range(far):
            for qq in [q] + (others if k == early else []):
                block = gathered.at[k, pp, qq]

                @pl.when(jnp.logical_and(p < far - 1, pp <= p))
                def _(k=k, pp=pp, qq=qq, block=block):
                    left_source(block, to_right.at[k, pp, qq])

                @pl.when(jnp.logical_and(p > 0, pp >= p))
                def _(k=k, pp=pp, qq=qq, block=block):
                    left_source(block, to_left.at[k, pp, qq])

            def near_sent(k=k, pp=pp):
                for step in range(near - 1):
                    left_source(gathered.at[k, pp, q], to_near.at[k, pp, step])

            if k == early:
                pl.when(pp == p)(near_sent)
            else:
                near_sent()


def forward_aggregate(dims, name_id, adj, sent):
    far, near, across, cores = dims
    nodes, width = sent.shape
    chunks = width // LANES
    dma = pltpu.SemaphoreType.DMA
    return pl.pallas_call(
        functools.partial(forward_kernel, dims, chunks),
        out_shape=jax.ShapeDtypeStruct((nodes, width), f32),
        in_specs=[pl.BlockSpec(memory_space=pltpu.VMEM)] * 2,
        out_specs=pl.BlockSpec(memory_space=pltpu.VMEM),
        scratch_shapes=[
            pltpu.VMEM((chunks, far, near, nodes, LANES), f32),
            pltpu.VMEM((far * near * nodes, 2 * LANES), bf16),
            pltpu.VMEM((chunks, cores, across, nodes, LANES), f32),
            pltpu.VMEM((chunks, across, nodes, LANES), f32),
            pltpu.VMEM((chunks, across, nodes, LANES), f32),
            dma((chunks, far, near)),
            dma((chunks, far, near)),
            dma((chunks, far, near)),
            dma((chunks, far, near)),
            dma((2, chunks)),
            dma((chunks, across)),
            dma((chunks, across)),
        ],
        compiler_params=pltpu.CompilerParams(
            collective_id=name_id, has_side_effects=True, vmem_limit_bytes=60 * 2**20
        ),
    )(adj, sent)


def backward_kernel(dims, chunks, adj, sent, out, rows, pair, part, from_near, from_left, from_right, final, row_out, row_in, near_out, near_in, right_out, left_out, left_in, right_in):
    far, near, across, cores = dims
    p, q, x, c = at = place(dims)
    nodes = sent.shape[0]
    early = 0
    right, left = device(dims, p + 1, q, x, c), device(dims, p - 1, q, x, c)
    others = [lax.rem(q + step, near) for step in range(1, near)]
    crossing = [lax.rem(x + step, across) for step in range(1, across)]
    entry_barrier(dims, at)

    for k in range(chunks):
        src = chunk(sent, k)
        for xx in crossing:
            send(src, rows.at[k, x, c], row_out.at[k, xx], row_in.at[k, x, c], device(dims, p, q, xx, c))
        send(src, rows.at[k, x, c], row_out.at[k, across + x], row_in.at[k, x, c], device(dims, p, q, x, 1 - c))
    for k in range(chunks):
        rows[k, x, c] = sent[:, k * LANES : (k + 1) * LANES]

    def dest(i):
        rights = far - 1 - p
        low = jnp.where(i < rights, far - 1 - i, jnp.where(i < far - 1, i - rights, p))
        high = jnp.where(i < p, i, jnp.where(i < far - 1, far - 1 - (i - p), p))
        return jnp.where(p < far // 2, low, high)

    def along(k, pp, qq):
        @pl.when(pp > p)
        def _():
            @pl.when(p > 0)
            def _():
                arrived(from_left.at[k, pp, qq], left_in.at[k, pp, qq])
                part[k, pp, qq] = part[k, pp, qq] + from_left[k, pp, qq]

            send(part.at[k, pp, qq], from_left.at[k, pp, qq], right_out.at[k, pp, qq], left_in.at[k, pp, qq], right)

        @pl.when(pp < p)
        def _():
            @pl.when(p < far - 1)
            def _():
                arrived(from_right.at[k, pp, qq], right_in.at[k, pp, qq])
                part[k, pp, qq] = part[k, pp, qq] + from_right[k, pp, qq]

            send(part.at[k, pp, qq], from_right.at[k, pp, qq], left_out.at[k, pp, qq], right_in.at[k, pp, qq], left)

    def settle(k, qq):
        @pl.when(p > 0)
        def _():
            arrived(from_left.at[k, p, qq], left_in.at[k, p, qq])
            part[k, p, qq] = part[k, p, qq] + from_left[k, p, qq]

        @pl.when(p < far - 1)
        def _():
            arrived(from_right.at[k, p, qq], right_in.at[k, p, qq])
            part[k, p, qq] = part[k, p, qq] + from_right[k, p, qq]

    def line(k):
        def step(i, carry):
            pp = dest(i)
            if k == early:
                for qq in others + [q]:
                    along(k, pp, qq)
            else:
                for qq in others:
                    arrived(from_near.at[k, pp, qq], near_in.at[k, pp, qq])
                    part[k, pp, q] = part[k, pp, q] + from_near[k, pp, qq]
                along(k, pp, q)
            return carry

        lax.fori_loop(0, far, step, 0)

    def early_end():
        for step, qq in enumerate(others):
            settle(early, qq)
            send(part.at[early, p, qq], from_near.at[early, p, q], near_out.at[early, p, step], near_in.at[early, p, q], device(dims, p, qq, x, c))

    for k in range(chunks):
        for xx in crossing:
            arrived(rows.at[k, xx, c], row_in.at[k, xx, c])
            send(rows.at[k, xx, c], rows.at[k, xx, c], row_out.at[k, across + xx], row_in.at[k, xx, c], device(dims, p, q, x, 1 - c))
        for xx in range(across):
            arrived(rows.at[k, xx, 1 - c], row_in.at[k, xx, 1 - c])
        high, low = halves(rows[k].reshape(across * cores * nodes, LANES))
        pair[:, :LANES] = high
        pair[:, LANES:] = low

        def product(i, carry, k=k):
            pp = dest(i // near)
            qq = lax.rem(q + 1 + lax.rem(i, near), near)
            start = pl.multiple_of((pp * near + qq) * nodes, nodes)
            both = lax.dot_general(adj[:, pl.ds(start, nodes)], pair[...], (((0,), (0,)), ((), ())), preferred_element_type=f32)
            part[k, pp, qq] = both[:, :LANES] + both[:, LANES:]
            if k != early:
                @pl.when(qq != q)
                def _():
                    send(part.at[k, pp, qq], from_near.at[k, pp, q], near_out.at[k, pp, lax.rem(qq - q - 1 + near, near)], near_in.at[k, pp, q], device(dims, p, qq, x, c))

            return carry

        lax.fori_loop(0, far * near, product, 0)
        if k >= 1:
            line(k - 1)
    early_end()
    line(chunks - 1)
    for k in range(chunks):
        settle(k, q)
        total = part[k, p, q]
        if k == early:
            for qq in others:
                arrived(from_near.at[k, p, qq], near_in.at[k, p, qq])
                total = total + from_near[k, p, qq]
        out[:, k * LANES : (k + 1) * LANES] = total

    for k in range(chunks):
        for xx in crossing:
            left_source(rows.at[k, x, c], row_out.at[k, xx])
        for xx in range(across):
            left_source(rows.at[k, xx, c], row_out.at[k, across + xx])
        for pp in range(far):
            for qq in [q] + (others if k == early else []):
                @pl.when(pp > p)
                def _(k=k, pp=pp, qq=qq):
                    left_source(part.at[k, pp, qq], right_out.at[k, pp, qq])

                @pl.when(pp < p)
                def _(k=k, pp=pp, qq=qq):
                    left_source(part.at[k, pp, qq], left_out.at[k, pp, qq])

            def near_sent(k=k, pp=pp):
                for step in range(near - 1):
                    left_source(part.at[k, pp, q], near_out.at[k, pp, step])

            if k == early:
                pl.when(pp == p)(near_sent)
            else:
                near_sent()


def backward_aggregate(dims, name_id, adj, sent):
    far, near, across, cores = dims
    nodes, width = sent.shape
    chunks = width // LANES
    dma = pltpu.SemaphoreType.DMA
    blocks = pltpu.VMEM((chunks, far, near, nodes, LANES), f32)
    return pl.pallas_call(
        functools.partial(backward_kernel, dims, chunks),
        out_shape=jax.ShapeDtypeStruct((nodes, width), f32),
        in_specs=[pl.BlockSpec(memory_space=pltpu.VMEM)] * 2,
        out_specs=pl.BlockSpec(memory_space=pltpu.VMEM),
        scratch_shapes=[
            pltpu.VMEM((chunks, across, cores, nodes, LANES), f32),
            pltpu.VMEM((across * cores * nodes, 2 * LANES), bf16),
            blocks,
            blocks,
            blocks,
            blocks,
            pltpu.VMEM((8, LANES), f32),
            dma((chunks, 2 * across)),
            dma((chunks, across, cores)),
        ]
        + [dma((chunks, far, near))] * 6,
        compiler_params=pltpu.CompilerParams(
            collective_id=name_id, has_side_effects=True, vmem_limit_bytes=60 * 2**20
        ),
    )(adj, sent)


norm_eps = 1e-06
stat_eps = 1e-30
clip_level = 0.5
step_rate = 0.04


def dot(left, right, over=((1,), (0,))):
    return lax.dot_general(
        left, right, (over, ((), ())), precision=lax.Precision.HIGH, preferred_element_type=f32
    )


def left_t(left, right):
    return dot(left, right, ((0,), (0,)))


def right_t(left, right):
    return dot(left, right, ((1,), (1,)))


def step_on_device(
    dims,
    features,
    adjacency,
    labels,
    labelled,
    node_count,
    w_in,
    w_side,
    w_proj,
    w_out,
    row_in,
    col_in,
    row_side,
    col_side,
    row_proj,
    col_proj,
    row_out,
    col_out,
):
    layers = w_side.shape[0]
    width = w_side.shape[2]
    in_width = features.shape[1]
    classes = w_out.shape[1]
    nodes = features.shape[0]
    both = ("wide", "narrow")
    adj = adjacency.astype(bf16)
    counts = node_count.astype(f32)
    alpha = 2.0 / (1.0 + counts)
    lam = lax.rsqrt(counts)
    target = labels.astype(f32)
    weight_mask = labelled.astype(f32)

    spare = -(in_width + 1) % LANES
    sent = jnp.concatenate(
        [alpha[:, None] * features, jnp.ones((nodes, 1), f32), jnp.zeros((nodes, spare), f32)], 1
    )
    summed = forward_aggregate(dims, 1, adj, sent)
    inverse = 1.0 / (1.0 + summed[:, in_width : in_width + 1])
    agg_features = summed[:, :in_width] * inverse

    full_in, full_side, full_proj, full_out = (
        lax.all_gather(w_in, both, axis=1, tiled=True),
        lax.all_gather(w_side, both, axis=1, tiled=True),
        lax.all_gather(w_proj, both, axis=1, tiled=True),
        lax.all_gather(w_out, both, axis=0, tiled=True),
    )
    mix_self = [dot(full_side[l, :width], full_proj[l, :width]) for l in range(layers)]
    mix_neigh = [dot(full_side[l, width:], full_proj[l, width:]) for l in range(layers)]

    kept = []
    hidden = dot(features, full_in)
    agg = dot(agg_features, full_in)
    for layer in range(layers):
        if layer > 0:
            agg = forward_aggregate(dims, 1 + layer, adj, alpha[:, None] * hidden) * inverse
        pre_act = dot(hidden, mix_self[layer]) + dot(agg, mix_neigh[layer])
        kept.append((hidden, agg, pre_act))
        act = jax.nn.silu(pre_act)
        hidden = act * lax.rsqrt(jnp.mean(act * act, -1, keepdims=True) + norm_eps)

    logits = dot(hidden, full_out)
    per = jnp.sum(jax.nn.softplus(logits) - target * logits, -1)
    loss_sum, label_count = lax.psum(
        (jnp.sum(weight_mask * lam * per), jnp.sum(weight_mask)), both
    )
    d_logits = (weight_mask * lam / label_count)[:, None] * (jax.nn.sigmoid(logits) - target)
    g_out = left_t(hidden, d_logits)
    d_out = right_t(d_logits, full_out)
    side_grads = [None] * layers
    proj_grads = [None] * layers
    for layer in reversed(range(layers)):
        hidden, agg, pre_act = kept[layer]
        sig = jax.nn.sigmoid(pre_act)
        act = pre_act * sig
        scale = lax.rsqrt(jnp.mean(act * act, -1, keepdims=True) + norm_eps)
        normed = act * scale
        d_act = scale * (d_out - normed * jnp.mean(d_out * normed, -1, keepdims=True))
        d_pre = d_act * sig * (1.0 + pre_act * (1.0 - sig))
        outer_self = left_t(hidden, d_pre)
        outer_neigh = left_t(agg, d_pre)
        side, proj = full_side[layer], full_proj[layer]
        side_grads[layer] = jnp.concatenate(
            [right_t(outer_self, proj[:width]), right_t(outer_neigh, proj[width:])], 0
        )
        proj_grads[layer] = jnp.concatenate(
            [left_t(side[:width], outer_self), left_t(side[width:], outer_neigh)], 0
        )
        d_self = right_t(d_pre, mix_self[layer])
        if layer > 0:
            back = backward_aggregate(dims, 3 + layer, adj, d_pre * inverse)
            d_out = d_self + right_t(alpha[:, None] * back, mix_neigh[layer])
        else:
            g_in = left_t(features, d_self) + left_t(agg_features, right_t(d_pre, mix_neigh[layer]))
    red_in, red_side, red_proj, red_out = (
        lax.psum_scatter(g_in, both, scatter_dimension=1, tiled=True),
        lax.psum_scatter(jnp.stack(side_grads), both, scatter_dimension=1, tiled=True),
        lax.psum_scatter(jnp.stack(proj_grads), both, scatter_dimension=1, tiled=True),
        lax.psum_scatter(g_out, both, scatter_dimension=0, tiled=True),
    )
    sq_in = red_in * red_in
    sq_side = red_side * red_side
    sq_proj = red_proj * red_proj
    sq_out = red_out * red_out
    new_col_in = 0.5 * col_in + 0.5 * (jnp.mean(sq_in, 0) + stat_eps)
    new_row_side = 0.5 * row_side + 0.5 * (jnp.mean(sq_side, 2) + stat_eps)
    new_row_proj = 0.5 * row_proj + 0.5 * (jnp.mean(sq_proj, 2) + stat_eps)
    new_row_out = 0.5 * row_out + 0.5 * (jnp.mean(sq_out, 1) + stat_eps)
    (
        sum_row_in,
        sum_col_side,
        sum_col_proj,
        sum_col_out,
        total_side,
        total_proj,
        total_out,
        over_in,
        over_side,
        over_proj,
        over_out,
    ) = lax.psum(
        (
            jnp.sum(sq_in, 1),
            jnp.sum(sq_side, 1),
            jnp.sum(sq_proj, 1),
            jnp.sum(sq_out, 0),
            jnp.sum(new_row_side, 1),
            jnp.sum(new_row_proj, 1),
            jnp.sum(new_row_out),
            jnp.sum(sq_in / new_col_in[None, :], 1),
            jnp.sum(sq_side / new_row_side[:, :, None], 1),
            jnp.sum(sq_proj / new_row_proj[:, :, None], 1),
            jnp.sum(sq_out / new_row_out[:, None], 0),
        ),
        both,
    )
    new_row_in = 0.5 * row_in + 0.5 * (sum_row_in / width + stat_eps)
    new_col_side = 0.5 * col_side + 0.5 * (sum_col_side / (2 * width) + stat_eps)
    new_col_proj = 0.5 * col_proj + 0.5 * (sum_col_proj / (2 * width) + stat_eps)
    new_col_out = 0.5 * col_out + 0.5 * (sum_col_out / width + stat_eps)
    mean_in = jnp.mean(new_row_in)
    mean_side = total_side / (2 * width)
    mean_proj = total_proj / (2 * width)
    mean_out = total_out / width
    up_in = red_in * lax.rsqrt(new_row_in[:, None] * new_col_in[None, :] / mean_in)
    up_side = red_side * lax.rsqrt(
        new_row_side[:, :, None] * new_col_side[:, None, :] / mean_side[:, None, None]
    )
    up_proj = red_proj * lax.rsqrt(
        new_row_proj[:, :, None] * new_col_proj[:, None, :] / mean_proj[:, None, None]
    )
    up_out = red_out * lax.rsqrt(new_row_out[:, None] * new_col_out[None, :] / mean_out)
    ms_in = mean_in * jnp.sum(over_in / new_row_in) / (in_width * width)
    ms_side = mean_side * jnp.sum(over_side / new_col_side, 1) / (2 * width * width)
    ms_proj = mean_proj * jnp.sum(over_proj / new_col_proj, 1) / (2 * width * width)
    ms_out = mean_out * jnp.sum(over_out / new_col_out) / (width * classes)
    fac_in = 1.0 / jnp.maximum(1.0, jnp.sqrt(ms_in) / clip_level)
    fac_side = 1.0 / jnp.maximum(1.0, jnp.sqrt(ms_side) / clip_level)
    fac_proj = 1.0 / jnp.maximum(1.0, jnp.sqrt(ms_proj) / clip_level)
    fac_out = 1.0 / jnp.maximum(1.0, jnp.sqrt(ms_out) / clip_level)
    new_in = w_in - step_rate * (up_in * fac_in)
    new_side = w_side - step_rate * (up_side * fac_side[:, None, None])
    new_proj = w_proj - step_rate * (up_proj * fac_proj[:, None, None])
    new_out = w_out - step_rate * (up_out * fac_out)
    return (
        loss_sum,
        label_count,
        red_in,
        red_side,
        red_proj,
        red_out,
        new_in,
        new_side,
        new_proj,
        new_out,
        new_row_in,
        new_col_in,
        new_row_side,
        new_col_side,
        new_row_proj,
        new_col_proj,
        new_row_out,
        new_col_out,
    )


def solution(mesh):
    in_specs = (
        P(("wide", "narrow"), None),
        P("wide", "narrow"),
        P(("wide", "narrow"), None),
        P(("wide", "narrow")),
        P(("wide", "narrow")),
        P(None, ("wide", "narrow")),
        P(None, ("wide", "narrow"), None),
        P(None, ("wide", "narrow"), None),
        P(("wide", "narrow"), None),
        P(),
        P(("wide", "narrow")),
        P(None, ("wide", "narrow")),
        P(),
        P(None, ("wide", "narrow")),
        P(),
        P(("wide", "narrow")),
        P(),
    )
    out_specs = (
        P(),
        P(),
        P(None, ("wide", "narrow")),
        P(None, ("wide", "narrow"), None),
        P(None, ("wide", "narrow"), None),
        P(("wide", "narrow"), None),
        P(None, ("wide", "narrow")),
        P(None, ("wide", "narrow"), None),
        P(None, ("wide", "narrow"), None),
        P(("wide", "narrow"), None),
        P(),
        P(("wide", "narrow")),
        P(None, ("wide", "narrow")),
        P(),
        P(None, ("wide", "narrow")),
        P(),
        P(("wide", "narrow")),
        P(),
    )
    shards = functools.partial(step_on_device, grid_of(mesh))
    return jax.shard_map(shards, mesh=mesh, in_specs=in_specs, out_specs=out_specs, check_vma=False)
```

```python
import functools
import jax
import jax.numpy as jnp
from jax import lax
from jax.experimental import pallas as pl
from jax.experimental.pallas import tpu as pltpu
from jax.sharding import PartitionSpec as P

MESH = pl.DeviceIdType.MESH
LANES = 128
CORES = 2
f32 = jnp.float32
bf16 = jnp.bfloat16


norm_eps = 1e-06
stat_eps = 1e-30
clip_level = 0.5
step_rate = 0.04


def grid_of(mesh):
    wide, narrow = mesh.shape["wide"], mesh.shape["narrow"]
    far = 4 if wide % 4 == 0 else wide
    return far, wide // far, narrow // CORES, CORES


def place(dims):
    far, near, across, cores = dims
    wide, narrow = lax.axis_index("wide"), lax.axis_index("narrow")
    return wide // near, lax.rem(wide, near), narrow // cores, lax.rem(narrow, cores)


def device(dims, far_at, near_at, across_at, core_at):
    return (far_at * dims[1] + near_at, across_at * dims[3] + core_at)


def send(src, dst, send_sem, recv_sem, target):
    pltpu.make_async_remote_copy(
        src_ref=src,
        dst_ref=dst,
        send_sem=send_sem,
        recv_sem=recv_sem,
        device_id=target,
        device_id_type=MESH,
    ).start()


def arrived(dst, recv_sem):
    pltpu.make_async_copy(dst, dst, recv_sem).wait()


def left_source(src, send_sem):
    pltpu.make_async_copy(src, src, send_sem).wait()


def halves(value):
    high = value.astype(bf16)
    return high, (value - high.astype(f32)).astype(bf16)


def neighbours(dims, at):
    far, near, across, cores = dims
    p, q, x, c = at
    always = [(p, lax.rem(q + step, near), x, c) for step in range(1, near)]
    always += [(p, q, lax.rem(x + step, across), c) for step in range(1, across)]
    always += [(p, q, x, 1 - c)]
    return always


def entry_barrier(dims, at):
    barrier = pltpu.get_barrier_semaphore()
    announce(dims, at, barrier)
    await_all(dims, at, barrier)


def chunk(ref, k):
    return ref.at[:, pl.ds(k * LANES, LANES)]


class SpreadAll:
    def __init__(self, dims, at, own, every, right_out, left_out, near_out, across_out, core_out, came):
        self.dims, self.at, self.own, self.every = dims, at, own, every
        self.right_out, self.left_out, self.near_out = right_out, left_out, near_out
        self.across_out, self.core_out, self.came = across_out, core_out, came

    def away(self, distance):
        far, p = self.dims[0], self.at[0]
        if distance == 0:
            return [(p, None)]
        return [(p - distance, p >= distance), (p + distance, p + distance < far)]

    def when(self, flag, act):
        if flag is None:
            act()
        else:
            pl.when(flag)(act)

    def on_line(self, pp, src):
        far, near, across, cores = self.dims
        p, q, x, c = self.at
        dst = self.every.at[pp, q, x, c]
        sem = self.came.at[pp, q, x, c]

        @pl.when(jnp.logical_and(p < far - 1, pp <= p))
        def _():
            send(src, dst, self.right_out.at[pp], sem, device(self.dims, p + 1, q, x, c))

        @pl.when(jnp.logical_and(p > 0, pp >= p))
        def _():
            send(src, dst, self.left_out.at[pp], sem, device(self.dims, p - 1, q, x, c))

        for step in range(1, near):
            send(src, dst, self.near_out.at[pp, step - 1], sem, device(self.dims, p, lax.rem(q + step, near), x, c))

    def on_plane(self, pp, qq, src):
        far, near, across, cores = self.dims
        p, q, x, c = self.at
        dst, sem = self.every.at[pp, qq, x, c], self.came.at[pp, qq, x, c]
        for step in range(1, across):
            send(src, dst, self.across_out.at[pp, qq, step - 1], sem, device(self.dims, p, q, lax.rem(x + step, across), c))
        self.to_core(pp, qq, x, src)

    def to_core(self, pp, qq, xx, src):
        p, q, x, c = self.at
        send(src, self.every.at[pp, qq, xx, c], self.core_out.at[pp, qq, xx], self.came.at[pp, qq, xx, c], device(self.dims, p, q, x, 1 - c))

    def wait(self, *where):
        arrived(self.every.at[where], self.came.at[where])

    def begin(self):
        p, q, x, c = self.at
        self.on_line(p, self.own)
        self.on_plane(p, q, self.own)
        self.every[p, q, x, c] = self.own[...]

    def from_line(self, distance):
        p, q, x, c = self.at
        for pp, flag in self.away(distance):
            def act(pp=pp):
                self.wait(pp, q, x, c)
                self.on_line(pp, self.every.at[pp, q, x, c])
                self.on_plane(pp, q, self.every.at[pp, q, x, c])
            self.when(flag, act)

    def from_near(self, distance):
        far, near, across, cores = self.dims
        p, q, x, c = self.at
        for pp, flag in self.away(distance):
            def act(pp=pp):
                for step in range(1, near):
                    qq = lax.rem(q + step, near)
                    self.wait(pp, qq, x, c)
                    self.on_plane(pp, qq, self.every.at[pp, qq, x, c])
            self.when(flag, act)

    def from_across(self, distance):
        far, near, across, cores = self.dims
        p, q, x, c = self.at
        for pp, flag in self.away(distance):
            def act(pp=pp):
                for qq in range(near):
                    for step in range(1, across):
                        xx = lax.rem(x + step, across)
                        self.wait(pp, qq, xx, c)
                        self.to_core(pp, qq, xx, self.every.at[pp, qq, xx, c])
            self.when(flag, act)

    def step(self, distance):
        self.from_line(distance)
        self.from_near(distance - 1)
        if distance >= 2:
            self.from_across(distance - 2)

    def drain(self):
        far = self.dims[0]
        self.from_near(far - 1)
        if far >= 2:
            self.from_across(far - 2)

    def end(self):
        far, near, across, cores = self.dims
        p, q, x, c = self.at
        self.from_across(far - 1)
        for pp in range(far):
            for qq in range(near):
                for xx in range(across):
                    self.wait(pp, qq, xx, 1 - c)
        for pp in range(far):
            block = self.every.at[pp, q, x, c]

            @pl.when(jnp.logical_and(p < far - 1, pp <= p))
            def _(pp=pp, block=block):
                left_source(block, self.right_out.at[pp])

            @pl.when(jnp.logical_and(p > 0, pp >= p))
            def _(pp=pp, block=block):
                left_source(block, self.left_out.at[pp])

            for step in range(1, near):
                left_source(block, self.near_out.at[pp, step - 1])
            for qq in range(near):
                for step in range(1, across):
                    left_source(block, self.across_out.at[pp, qq, step - 1])
                for xx in range(across):
                    left_source(block, self.core_out.at[pp, qq, xx])


def spread_sems(dims):
    far, near, across, cores = dims
    dma = pltpu.SemaphoreType.DMA
    return [
        dma((far,)),
        dma((far,)),
        dma((far, max(near - 1, 1))),
        dma((far, near, max(across - 1, 1))),
        dma((far, near, across)),
        dma((far, near, across, cores)),
    ]


class Blocks:
    def __init__(self, pool, base, *shape):
        self.pool, self.base, self.shape = pool, base, shape

    @property
    def count(self):
        total = 1
        for size in self.shape:
            total *= size
        return total

    def flat(self, where):
        index = 0
        for size, at in zip(self.shape, where):
            index = index * size + at
        left = 1
        for size in self.shape[len(where) :]:
            left *= size
        return self.base + index * left, left

    def ref(self, *where):
        start, _ = self.flat(where)
        return self.pool.at[start]

    def run(self, *where):
        start, left = self.flat(where)
        return self.pool.at[pl.ds(start, left)]

    def add(self, where, other):
        ref = self.ref(*where)
        ref[...] = ref[...] + other[...]


def take(pool, *shapes):
    base, made = 0, []
    for shape in shapes:
        made.append(Blocks(pool, base, *shape))
        base += made[-1].count
    return made


def forward_blocks(dims, chunks):
    far, near, across, cores = dims
    return (
        (chunks, far, near),
        (chunks, cores, across),
        (chunks, across),
        (chunks, across),
    )


def backward_blocks(dims, chunks):
    far, near, across, cores = dims
    return (
        (chunks, across, cores),
        (chunks, far, near),
        (far, near),
        (chunks, far),
        (near,),
        (chunks,),
        (chunks, far, near),
    )


def blocks_of(shapes):
    total = 0
    for shape in shapes:
        size = 1
        for extent in shape:
            size *= extent
        total += size
    return total


def counted(dims, at):
    p, far = at[0], dims[0]
    ends = jnp.where(p > 0, 1, 0) + jnp.where(p < far - 1, 1, 0)
    return len(neighbours(dims, at)) + ends


def announce(dims, at, sem):
    far = dims[0]
    p, q, x, c = at
    for other in neighbours(dims, at):
        pl.semaphore_signal(sem, inc=1, device_id=device(dims, *other), device_id_type=MESH)

    @pl.when(p > 0)
    def _():
        pl.semaphore_signal(sem, inc=1, device_id=device(dims, p - 1, q, x, c), device_id_type=MESH)

    @pl.when(p < far - 1)
    def _():
        pl.semaphore_signal(sem, inc=1, device_id=device(dims, p + 1, q, x, c), device_id_type=MESH)


def await_all(dims, at, sem):
    pl.semaphore_wait(sem, counted(dims, at))


class Hooks:
    def __init__(self, **acts):
        self.acts = acts

    def run(self, name):
        for act in self.acts.get(name, ()):
            act()


def forward_pass(dims, at, chunks, adj, sent, out, pair, pool, sems, hooks):
    to_right, to_left, to_near, came, core_sems, across_out, across_in = sems
    gathered, part, from_core, from_across = take(pool, *forward_blocks(dims, chunks))
    far, near, across, cores = dims
    p, q, x, c = at
    nodes = sent.shape[0]
    early = chunks - 1
    right, left = device(dims, p + 1, q, x, c), device(dims, p - 1, q, x, c)
    others = [lax.rem(q + step, near) for step in range(1, near)]

    def go_right(k, pp, qq, src):
        @pl.when(p < far - 1)
        def _():
            send(src, gathered.ref(k, pp, qq), to_right.at[k, pp, qq], came.at[k, pp, qq], right)

    def go_left(k, pp, qq, src):
        @pl.when(p > 0)
        def _():
            send(src, gathered.ref(k, pp, qq), to_left.at[k, pp, qq], came.at[k, pp, qq], left)

    def go_near(k, pp, src):
        for step, qq in enumerate(others):
            send(src, gathered.ref(k, pp, q), to_near.at[k, pp, step], came.at[k, pp, q], device(dims, p, qq, x, c))

    hooks.run("begin")
    for k in [early] + list(range(chunks - 1)):
        src = chunk(sent, k)
        go_near(k, p, src)
        go_right(k, p, q, src)
        go_left(k, p, q, src)
    for k in range(chunks):
        gathered.ref(k, p, q)[...] = sent[:, k * LANES : (k + 1) * LANES]
    hooks.run("sent")
    for qq in others:
        arrived(gathered.ref(early, p, qq), came.at[early, p, qq])
        go_right(early, p, qq, gathered.ref(early, p, qq))
        go_left(early, p, qq, gathered.ref(early, p, qq))
    for step in range(1, far):
        hooks.run("step%d" % step)
        for k in range(chunks):
            for side in range(2):
                pp = p - step if side == 0 else p + step
                onward = go_right if side == 0 else go_left

                @pl.when(pp >= 0 if side == 0 else pp < far)
                def _(k=k, pp=pp, onward=onward):
                    for qq in [q] + (others if k == early else []):
                        block = gathered.ref(k, pp, qq)
                        arrived(block, came.at[k, pp, qq])
                        onward(k, pp, qq, block)
                    if k != early:
                        go_near(k, pp, gathered.ref(k, pp, q))

    hooks.run("drain")

    def reduce_across(k):
        arrived(from_core.run(k), core_sems.at[1, k])
        for step in range(1, across):
            xx = lax.rem(x + step, across)
            part.add((k, c, xx), from_core.ref(k, xx))
            send(part.ref(k, c, xx), from_across.ref(k, x), across_out.at[k, xx], across_in.at[k, x], device(dims, p, q, xx, c))

    def finish(k):
        total = part.ref(k, c, x)[...] + from_core.ref(k, x)[...]
        for step in range(1, across):
            xx = lax.rem(x + step, across)
            arrived(from_across.ref(k, xx), across_in.at[k, xx])
            total = total + from_across.ref(k, xx)[...]
        out[:, k * LANES : (k + 1) * LANES] = total

    for k in range(chunks):
        if k != early:
            for pp in range(far):
                for qq in others:
                    arrived(gathered.ref(k, pp, qq), came.at[k, pp, qq])
        high, low = halves(gathered.run(k)[...].reshape(far * near * nodes, LANES))
        pair[: far * near * nodes, :LANES] = high
        pair[: far * near * nodes, LANES:] = low

        def product(index, carry, k=k):
            cc = lax.rem(index // across + 1 + c, cores)
            xx = lax.rem(index, across)
            rows = pl.multiple_of((xx * cores + cc) * nodes, nodes)
            both = jnp.dot(adj[pl.ds(rows, nodes), :], pair[: far * near * nodes, :], preferred_element_type=f32)
            part.ref(k, cc, xx)[...] = both[:, :LANES] + both[:, LANES:]

            @pl.when(index == across - 1)
            def _():
                send(part.run(k, 1 - c), from_core.run(k), core_sems.at[0, k], core_sems.at[1, k], device(dims, p, q, x, 1 - c))

            return carry

        lax.fori_loop(0, cores * across, product, 0)
        if k >= 1:
            reduce_across(k - 1)
        if k >= 2:
            finish(k - 2)
    reduce_across(chunks - 1)
    if chunks >= 2:
        finish(chunks - 2)
    finish(chunks - 1)

    for k in range(chunks):
        left_source(part.run(k, 1 - c), core_sems.at[0, k])
        for step in range(1, across):
            xx = lax.rem(x + step, across)
            left_source(part.ref(k, c, xx), across_out.at[k, xx])
        for pp in range(far):
            for qq in [q] + (others if k == early else []):
                block = gathered.ref(k, pp, qq)

                @pl.when(jnp.logical_and(p < far - 1, pp <= p))
                def _(k=k, pp=pp, qq=qq, block=block):
                    left_source(block, to_right.at[k, pp, qq])

                @pl.when(jnp.logical_and(p > 0, pp >= p))
                def _(k=k, pp=pp, qq=qq, block=block):
                    left_source(block, to_left.at[k, pp, qq])

            def near_sent(k=k, pp=pp):
                for step in range(near - 1):
                    left_source(gathered.ref(k, pp, q), to_near.at[k, pp, step])

            if k == early:
                pl.when(pp == p)(near_sent)
            else:
                near_sent()


def forward_sems(dims, chunks):
    far, near, across, cores = dims
    dma = pltpu.SemaphoreType.DMA
    return [dma((chunks, far, near))] * 4 + [dma((2, chunks)), dma((chunks, across)), dma((chunks, across))]


def backward_pass(dims, at, chunks, adj, sent, out, pair, pool, sems, hooks):
    row_out, row_in, near_out, near_in, right_out, left_out, left_in, right_in = sems
    rows, part, line_early, line_rest, right_early, right_rest, from_near = take(
        pool, *backward_blocks(dims, chunks)
    )
    far, near, across, cores = dims
    p, q, x, c = at
    nodes = sent.shape[0]
    total_rows = across * cores * nodes
    early = 0
    right, left = device(dims, p + 1, q, x, c), device(dims, p - 1, q, x, c)
    others = [lax.rem(q + step, near) for step in range(1, near)]
    crossing = [lax.rem(x + step, across) for step in range(1, across)]

    def on_line(k, pp, qq):
        return line_early.ref(pp, qq) if k == early else line_rest.ref(k, pp)

    def from_right_own(k, qq):
        return right_early.ref(qq) if k == early else right_rest.ref(k)

    for k in range(chunks):
        src = chunk(sent, k)
        for xx in crossing:
            send(src, rows.ref(k, x, c), row_out.at[k, xx], row_in.at[k, x, c], device(dims, p, q, xx, c))
        send(src, rows.ref(k, x, c), row_out.at[k, across + x], row_in.at[k, x, c], device(dims, p, q, x, 1 - c))
    for k in range(chunks):
        rows.ref(k, x, c)[...] = sent[:, k * LANES : (k + 1) * LANES]
    hooks.run("sent")

    def dest(i):
        rights = far - 1 - p
        low = jnp.where(i < rights, far - 1 - i, jnp.where(i < far - 1, i - rights, p))
        high = jnp.where(i < p, i, jnp.where(i < far - 1, far - 1 - (i - p), p))
        return jnp.where(p < far // 2, low, high)

    def along(k, pp, qq):
        @pl.when(pp > p)
        def _():
            @pl.when(p > 0)
            def _():
                arrived(on_line(k, pp, qq), left_in.at[k, pp, qq])
                part.add((k, pp, qq), on_line(k, pp, qq))

            send(part.ref(k, pp, qq), on_line(k, pp, qq), right_out.at[k, pp, qq], left_in.at[k, pp, qq], right)

        @pl.when(pp < p)
        def _():
            @pl.when(p < far - 1)
            def _():
                arrived(on_line(k, pp, qq), right_in.at[k, pp, qq])
                part.add((k, pp, qq), on_line(k, pp, qq))

            @pl.when(pp < p - 1)
            def _():
                send(part.ref(k, pp, qq), on_line(k, pp, qq), left_out.at[k, pp, qq], right_in.at[k, pp, qq], left)

            @pl.when(pp == p - 1)
            def _():
                send(part.ref(k, pp, qq), from_right_own(k, qq), left_out.at[k, pp, qq], right_in.at[k, pp, qq], left)

    def settle(k, qq):
        @pl.when(p > 0)
        def _():
            arrived(on_line(k, p, qq), left_in.at[k, p, qq])
            part.add((k, p, qq), on_line(k, p, qq))

        @pl.when(p < far - 1)
        def _():
            arrived(from_right_own(k, qq), right_in.at[k, p, qq])
            part.add((k, p, qq), from_right_own(k, qq))

    def line(k):
        def step(i, carry):
            pp = dest(i)
            if k == early:
                for qq in others + [q]:
                    along(k, pp, qq)
            else:
                for qq in others:
                    arrived(from_near.ref(k, pp, qq), near_in.at[k, pp, qq])
                    part.add((k, pp, q), from_near.ref(k, pp, qq))
                along(k, pp, q)
            return carry

        lax.fori_loop(0, far, step, 0)

    def early_end():
        for step, qq in enumerate(others):
            settle(early, qq)
            send(part.ref(early, p, qq), from_near.ref(early, p, q), near_out.at[early, p, step], near_in.at[early, p, q], device(dims, p, qq, x, c))

    for k in range(chunks):
        for xx in crossing:
            arrived(rows.ref(k, xx, c), row_in.at[k, xx, c])
            send(rows.ref(k, xx, c), rows.ref(k, xx, c), row_out.at[k, across + xx], row_in.at[k, xx, c], device(dims, p, q, x, 1 - c))
        for xx in range(across):
            arrived(rows.ref(k, xx, 1 - c), row_in.at[k, xx, 1 - c])
        high, low = halves(rows.run(k)[...].reshape(total_rows, LANES))
        pair[:total_rows, :LANES] = high
        pair[:total_rows, LANES:] = low

        def product(i, carry, k=k):
            pp = dest(i // near)
            qq = lax.rem(q + 1 + lax.rem(i, near), near)
            start = pl.multiple_of((pp * near + qq) * nodes, nodes)
            both = lax.dot_general(adj[:, pl.ds(start, nodes)], pair[:total_rows, :], (((0,), (0,)), ((), ())), preferred_element_type=f32)
            part.ref(k, pp, qq)[...] = both[:, :LANES] + both[:, LANES:]
            if k != early:
                @pl.when(qq != q)
                def _():
                    send(part.ref(k, pp, qq), from_near.ref(k, pp, q), near_out.at[k, pp, lax.rem(qq - q - 1 + near, near)], near_in.at[k, pp, q], device(dims, p, qq, x, c))

            return carry

        lax.fori_loop(0, far * near, product, 0)
        if k >= 1:
            line(k - 1)
        hooks.run("chunk%d" % k)
    early_end()
    hooks.run("early")
    line(chunks - 1)
    hooks.run("line")
    for k in range(chunks):
        settle(k, q)
        total = part.ref(k, p, q)[...]
        if k == early:
            for qq in others:
                arrived(from_near.ref(k, p, qq), near_in.at[k, p, qq])
                total = total + from_near.ref(k, p, qq)[...]
        out[:, k * LANES : (k + 1) * LANES] = total

    for k in range(chunks):
        for xx in crossing:
            left_source(rows.ref(k, x, c), row_out.at[k, xx])
        for xx in range(across):
            left_source(rows.ref(k, xx, c), row_out.at[k, across + xx])
        for pp in range(far):
            for qq in [q] + (others if k == early else []):
                @pl.when(pp > p)
                def _(k=k, pp=pp, qq=qq):
                    left_source(part.ref(k, pp, qq), right_out.at[k, pp, qq])

                @pl.when(pp < p)
                def _(k=k, pp=pp, qq=qq):
                    left_source(part.ref(k, pp, qq), left_out.at[k, pp, qq])

            def near_sent(k=k, pp=pp):
                for step in range(near - 1):
                    left_source(part.ref(k, pp, q), near_out.at[k, pp, step])

            if k == early:
                pl.when(pp == p)(near_sent)
            else:
                near_sent()


def backward_sems(dims, chunks):
    far, near, across, cores = dims
    dma = pltpu.SemaphoreType.DMA
    return [dma((chunks, 2 * across)), dma((chunks, across, cores))] + [dma((chunks, far, near))] * 6


class ReduceAll:
    def __init__(self, dims, at, own, first_rows, out, bufs, sems):
        self.dims, self.at, self.own, self.first_rows, self.out = dims, at, own, first_rows, out
        self.halfway, self.from_across, self.from_near, self.from_left, self.from_right = bufs
        self.core_sems, self.across_out, self.across_in, self.near_out, self.near_in = sems[:5]
        self.right_out, self.left_out, self.left_in, self.right_in = sems[5:]
        self.depth = self.halfway.shape[4]

    def rows(self, j):
        return pl.ds(self.first_rows[j], self.depth)

    def core_stage(self, j):
        p, q, x, c = self.at
        send(self.own.at[:, :, :, 1 - c, self.rows(j)], self.halfway.at[j], self.core_sems.at[0, j], self.core_sems.at[1, j], device(self.dims, p, q, x, 1 - c))

    def across_stage(self, j):
        far, near, across, cores = self.dims
        p, q, x, c = self.at
        arrived(self.halfway.at[j], self.core_sems.at[1, j])
        self.halfway[j] = self.halfway[j] + self.own[:, :, :, c, self.rows(j)]
        for step in range(1, across):
            xx = lax.rem(x + step, across)
            send(self.halfway.at[j, :, :, xx], self.from_across.at[j, step - 1], self.across_out.at[j, step - 1], self.across_in.at[j, step - 1], device(self.dims, p, q, xx, c))

    def near_stage(self, j):
        far, near, across, cores = self.dims
        p, q, x, c = self.at
        for step in range(1, across):
            arrived(self.from_across.at[j, step - 1], self.across_in.at[j, step - 1])
            self.halfway[j, :, :, x] = self.halfway[j, :, :, x] + self.from_across[j, step - 1]
        for step in range(1, near):
            qq = lax.rem(q + step, near)
            send(self.halfway.at[j, :, qq, x], self.from_near.at[j, step - 1], self.near_out.at[j, step - 1], self.near_in.at[j, step - 1], device(self.dims, p, qq, x, c))

    def line_stage(self, j):
        far, near, across, cores = self.dims
        p, q, x, c = self.at
        for step in range(1, near):
            arrived(self.from_near.at[j, step - 1], self.near_in.at[j, step - 1])
            self.halfway[j, :, q, x] = self.halfway[j, :, q, x] + self.from_near[j, step - 1]
        for distance in range(far - 1, 0, -1):
            pp = p + distance

            @pl.when(pp < far)
            def _(pp=pp):
                @pl.when(p > 0)
                def _():
                    arrived(self.from_left.at[j, pp], self.left_in.at[j, pp])
                    self.halfway[j, pp, q, x] = self.halfway[j, pp, q, x] + self.from_left[j, pp]

                send(self.halfway.at[j, pp, q, x], self.from_left.at[j, pp], self.right_out.at[j, pp], self.left_in.at[j, pp], device(self.dims, p + 1, q, x, c))

            pm = p - distance

            @pl.when(pm >= 0)
            def _(pm=pm):
                @pl.when(p < far - 1)
                def _():
                    arrived(self.from_right.at[j, pm], self.right_in.at[j, pm])
                    self.halfway[j, pm, q, x] = self.halfway[j, pm, q, x] + self.from_right[j, pm]

                send(self.halfway.at[j, pm, q, x], self.from_right.at[j, pm], self.left_out.at[j, pm], self.right_in.at[j, pm], device(self.dims, p - 1, q, x, c))

    def last_stage(self, j, out_row):
        far, near, across, cores = self.dims
        p, q, x, c = self.at
        into = self.out.at[pl.ds(out_row, self.depth)]
        into[...] = self.halfway[j, p, q, x]

        @pl.when(p > 0)
        def _():
            arrived(self.from_left.at[j, p], self.left_in.at[j, p])
            into[...] = into[...] + self.from_left[j, p]

        @pl.when(p < far - 1)
        def _():
            arrived(self.from_right.at[j, p], self.right_in.at[j, p])
            into[...] = into[...] + self.from_right[j, p]

    def end(self, j):
        far, near, across, cores = self.dims
        p, q, x, c = self.at
        left_source(self.own.at[:, :, :, 1 - c, self.rows(j)], self.core_sems.at[0, j])
        for step in range(1, across):
            left_source(self.from_across.at[j, step - 1], self.across_out.at[j, step - 1])
        for step in range(1, near):
            left_source(self.from_near.at[j, step - 1], self.near_out.at[j, step - 1])
        for pp in range(far):
            @pl.when(pp > p)
            def _(pp=pp):
                left_source(self.from_left.at[j, pp], self.right_out.at[j, pp])

            @pl.when(pp < p)
            def _(pp=pp):
                left_source(self.from_right.at[j, pp], self.left_out.at[j, pp])


def reduce_scratch(dims, pieces, depth, width):
    far, near, across, cores = dims
    dma = pltpu.SemaphoreType.DMA
    bufs = [
        pltpu.VMEM((pieces, far, near, across, depth, width), f32),
        pltpu.VMEM((pieces, max(across - 1, 1), far, near, depth, width), f32),
        pltpu.VMEM((pieces, max(near - 1, 1), far, depth, width), f32),
        pltpu.VMEM((pieces, far, depth, width), f32),
        pltpu.VMEM((pieces, far, depth, width), f32),
    ]
    sems = [
        dma((2, pieces)),
        dma((pieces, max(across - 1, 1))),
        dma((pieces, max(across - 1, 1))),
        dma((pieces, max(near - 1, 1))),
        dma((pieces, max(near - 1, 1))),
    ] + [dma((pieces, far))] * 4
    return bufs, sems


def forward_kernel(dims, chunks, adj, sent, out, pair, pool, *sems):
    at = place(dims)
    entry_barrier(dims, at)
    forward_pass(dims, at, chunks, adj, sent, out, pair, pool, sems, Hooks())


def backward_kernel(dims, chunks, adj, sent, out, pair, pool, *sems):
    at = place(dims)
    entry_barrier(dims, at)
    backward_pass(dims, at, chunks, adj, sent, out, pair, pool, sems, Hooks())


def aggregate(dims, name_id, adj, sent, backward=False):
    far, near, across, cores = dims
    nodes, width = sent.shape
    chunks = width // LANES
    kernel = backward_kernel if backward else forward_kernel
    blocks = backward_blocks if backward else forward_blocks
    sems = backward_sems if backward else forward_sems
    depth = (across * cores if backward else far * near) * nodes
    return pl.pallas_call(
        functools.partial(kernel, dims, chunks),
        out_shape=jax.ShapeDtypeStruct((nodes, width), f32),
        in_specs=[pl.BlockSpec(memory_space=pltpu.VMEM)] * 2,
        out_specs=pl.BlockSpec(memory_space=pltpu.VMEM),
        scratch_shapes=[
            pltpu.VMEM((depth, 2 * LANES), bf16),
            pltpu.VMEM((blocks_of(blocks(dims, chunks)), nodes, LANES), f32),
        ]
        + sems(dims, chunks),
        compiler_params=pltpu.CompilerParams(
            collective_id=name_id, has_side_effects=True, vmem_limit_bytes=60 * 2**20
        ),
    )(adj, sent)


def contract(left, right, over):
    first, second = halves(left), halves(right)

    def go(a, b):
        return lax.dot_general(a, b, (over, ((), ())), preferred_element_type=f32)

    return go(first[0], second[0]) + (go(first[0], second[1]) + go(first[1], second[0]))


def plain(left, right):
    return contract(left, right, ((1,), (0,)))


def left_flip(left, right):
    return contract(left, right, ((0,), (0,)))


def right_flip(left, right):
    return contract(left, right, ((1,), (1,)))


def rows_of(every, half, start, size):
    far = every.shape[0]
    value = every[half * (far // 2) : (half + 1) * (far // 2), :, :, :, start : start + size, :]
    return value.reshape(-1, value.shape[-1])


def put_rows(every, half, start, size, value):
    far = every.shape[0]
    shape = (far // 2,) + every.shape[1:4] + (size, value.shape[-1])
    every[half * (far // 2) : (half + 1) * (far // 2), :, :, :, start : start + size, :] = value.reshape(shape)


def activation(pre_act):
    sig = jax.nn.sigmoid(pre_act)
    act = pre_act * sig
    return sig, act, lax.rsqrt(jnp.mean(act * act, -1, keepdims=True) + norm_eps)


def train_kernel(dims, in_width, classes, adj_hbm, feats, info, target, own0, own1, own2, red, notes, refs):
    far, near, across, cores = dims
    at = place(dims)
    nodes, wide_in = feats.shape
    width = own0.shape[1]
    block = own1.shape[0] // 2
    owns = (own0, own1, own2)
    layers = len(owns)
    every = (refs["every0"], refs["every1"], refs["every2"])
    adj, stage, stage_sems = refs["adj"], refs["stage"], refs["stage_sems"]
    pair, pool, sent = refs["pair"], refs["pool"], refs["sent"]
    raw, inverse, mix, direct, back = refs["raw"], refs["inverse"], refs["mix"], refs["direct"], refs["back"]
    agg, hid, pre, outer, ready = refs["agg"], refs["hid"], refs["pre"], refs["outer"], refs["ready"]
    in_chunks, chunks = wide_in // LANES, width // LANES
    head = 2 * block

    strip = stage.shape[1]

    def strip_copy(i):
        return pltpu.make_async_copy(adj_hbm.at[pl.ds(i * strip, strip)], stage.at[i % 2], stage_sems.at[i % 2])

    strips = adj.shape[0] // strip
    strip_copy(0).start()
    strip_copy(1).start()
    entry_barrier(dims, at)
    alpha = info[:, 0:1]
    weight = info[:, 1:2]
    lane = lax.broadcasted_iota(jnp.int32, (nodes, wide_in), 1)
    sent[...] = jnp.where(lane == in_width, 1.0, feats[...] * alpha)

    def load_adjacency():
        for i in range(strips):
            strip_copy(i).wait()
            adj[i * strip : (i + 1) * strip, :] = stage[i % 2].astype(f32).astype(bf16)
            if i + 2 < strips:
                strip_copy(i + 2).start()

    spreads = [SpreadAll(dims, at, owns[l], every[l], *refs["spread%d" % l]) for l in range(layers)]

    def mixing(layer):
        for half in range(2):
            side = rows_of(every[layer], half, 0, block)
            proj = rows_of(every[layer], half, block, block)
            mix[layer % 2, half] = plain(side, proj)

    def input_weights():
        def both(start):
            return jnp.concatenate([rows_of(every[0], half, start, block // 2) for half in range(2)], 0)

        first, second = both(head), both(head + block // 2)
        return jnp.concatenate([first, second[:, : wide_in - width]], 1)

    def ahead(layer):
        def act():
            spreads[layer].drain()
            spreads[layer].end()
            mixing(layer)
            if layer == 0:
                hid[0] = right_flip(feats[...], input_weights())
            direct[...] = plain(hid[layer], mix[layer % 2, 0])
            if layer + 1 < layers:
                spreads[layer + 1].begin()

        return act

    rounds = iter(range(ready.shape[0]))
    for layer in range(layers):
        acts = {"drain": [ahead(layer)]}
        for step in range(1, far):
            acts["step%d" % step] = [functools.partial(spreads[layer].step, step)]
        if layer == 0:
            acts["begin"] = [spreads[0].begin]
            acts["sent"] = [load_adjacency]
            forward_pass(dims, at, in_chunks, adj, sent, raw, pair, pool, refs["forward"], Hooks(**acts))
            turn = ready.at[next(rounds)]
            announce(dims, at, turn)
            inverse[...] = jnp.broadcast_to(1.0 / (1.0 + raw[:, in_width : in_width + 1]), inverse.shape)
            raw[...] = raw[...] * inverse[:, 0:1]
            agg[0] = right_flip(raw[...], input_weights())
        else:
            forward_pass(dims, at, chunks, adj, sent, agg.at[layer], pair, pool, refs["forward"], Hooks(**acts))
            turn = ready.at[next(rounds)]
            announce(dims, at, turn)
            agg[layer] = agg[layer] * inverse[:, 0:1]
        pre_act = direct[...] + plain(agg[layer], mix[layer % 2, 1])
        pre[layer] = pre_act
        _, act, scale = activation(pre_act)
        after = act * scale
        hid[layer + 1] = after
        if layer + 1 < layers:
            sent[:, :width] = after * alpha
        await_all(dims, at, turn)

    def output_weights():
        at_lane = wide_in - width
        return jnp.concatenate(
            [rows_of(every[0], half, head + block // 2, block // 2)[:, at_lane : at_lane + LANES] for half in range(2)], 0
        )

    tail = wide_in - width + LANES
    labelled = jnp.sum(every[0][:, :, :, :, head + block // 2 : head + block // 2 + 8, tail : tail + LANES].reshape(-1, 8, LANES), 0)[0:1, 0:1]
    notes[...] = jnp.broadcast_to(labelled, notes.shape)
    head_weights = output_weights()
    logits = plain(hid[layers], head_weights)
    column = lax.broadcasted_iota(jnp.int32, logits.shape, 1)
    soft = jnp.maximum(logits, 0.0) + jnp.log(1.0 + jnp.exp(-jnp.abs(logits)))
    each = jnp.where(column < classes, soft - target[...] * logits, 0.0)
    loss = jnp.sum(weight * jnp.sum(each, -1, keepdims=True), 0, keepdims=True)
    d_logits = jnp.where(column < classes, (weight / labelled) * (jax.nn.sigmoid(logits) - target[...]), 0.0)
    g_out = left_flip(hid[layers], d_logits)
    d_out = right_flip(d_logits, head_weights)
    start = head + block // 2
    half_rows = width // 2
    for half in range(2):
        piece = jnp.concatenate(
            [
                jnp.zeros((half_rows, wide_in - width), f32),
                g_out[half * half_rows : (half + 1) * half_rows],
                jnp.broadcast_to(loss, (half_rows, width - tail)),
            ],
            1,
        )
        put_rows(every[0], half, start, block // 2, piece)

    reduces = [
        ReduceAll(dims, at, every[l], [0, block, head], red, refs["reduce_bufs"], refs["reduce_sems"]) for l in range(layers)
    ]

    def slope(layer, d_out):
        pre_act = pre[layer]
        sig, act, scale = activation(pre_act)
        normed = act * scale
        d_act = scale * (d_out - normed * jnp.mean(d_out * normed, -1, keepdims=True))
        return d_act * sig * (1.0 + pre_act * (1.0 - sig))

    def outers(layer, d_pre):
        outer[0] = left_flip(hid[layer], d_pre)
        outer[1] = left_flip(agg[layer], d_pre)

    def weight_grads(layer, half):
        side = rows_of(every[layer], half, 0, block)
        proj = rows_of(every[layer], half, block, block)
        g_side = right_flip(outer[half], proj)
        g_proj = left_flip(side, outer[half])
        put_rows(every[layer], half, 0, block, g_side)
        put_rows(every[layer], half, block, block, g_proj)

    base = [0, 3 * block, 5 * block]

    def finish_reduce(layer, pieces):
        for j in pieces:
            reduces[layer].last_stage(j, base[layer] + j * block)
        for j in pieces:
            reduces[layer].end(j)

    d_pre_ref = refs["d_pre"]
    carried, freed = [], []
    for layer in range(layers - 1, 0, -1):
        d_pre_ref[...] = slope(layer, d_out)
        sent[:, :width] = d_pre_ref[...] * inverse[:, 0:1]

        def grads(layer=layer):
            outers(layer, d_pre_ref[...])
            for half in range(2):
                weight_grads(layer, half)
            if freed:
                await_all(dims, at, freed.pop())
            for j in range(2):
                reduces[layer].core_stage(j)

        def direct_part(layer=layer):
            direct[...] = right_flip(d_pre_ref[...], mix[layer % 2, 0])

        def stage(name, layer=layer):
            for j in range(2):
                getattr(reduces[layer], name)(j)

        acts = {
            "chunk0": carried[:1],
            "chunk1": carried[1:] + [direct_part],
            "chunk2": [grads],
            "chunk3": [functools.partial(stage, "across_stage")],
            "early": [functools.partial(mixing, 0)] if layer == 1 else [],
            "line": [functools.partial(stage, "near_stage")],
        }
        backward_pass(dims, at, chunks, adj, sent, back, pair, pool, refs["backward"], Hooks(**acts))
        if layer > 1:
            turn = ready.at[next(rounds)]
            announce(dims, at, turn)
        d_out = direct[...] + right_flip(back[...] * alpha, mix[layer % 2, 1])
        if layer > 1:
            await_all(dims, at, turn)

        def close(layer=layer):
            finish_reduce(layer, range(2))
            freed.append(ready.at[next(rounds)])
            announce(dims, at, freed[0])

        carried = [functools.partial(stage, "line_stage"), close]

    d_pre = slope(0, d_out)
    d_pre_ref[...] = d_pre
    carried[0]()
    d_self = right_flip(d_pre, mix[0, 0])
    d_neigh = right_flip(d_pre, mix[0, 1])
    g_in = left_flip(d_self, feats[...]) + left_flip(d_neigh, raw[...])
    for half in range(2):
        top = slice(half * half_rows, (half + 1) * half_rows)
        put_rows(every[0], half, head, block // 2, g_in[top, :width])
        where = (slice(half * (far // 2), (half + 1) * (far // 2)),) + (slice(None),) * 3
        value = g_in[top, width:]
        every[0][where + (slice(head + block // 2, head + block), slice(0, wide_in - width))] = value.reshape(
            (far // 2, near, across, cores, block // 2, wide_in - width)
        )
    carried[1]()
    await_all(dims, at, freed.pop())
    final = reduces[0]
    final.core_stage(2)
    outers(0, d_pre)
    for half in range(2):
        weight_grads(0, half)
    final.core_stage(0)
    final.core_stage(1)
    for name in ("across_stage", "near_stage", "line_stage"):
        for j in (2, 0, 1):
            getattr(final, name)(j)
    finish_reduce(0, (2, 0, 1))


def train_on_device(dims, name_id, in_width, classes, adjacency, feats, info, target, owns):
    far, near, across, cores = dims
    nodes, wide_in = feats.shape
    width = owns[0].shape[1]
    block = owns[1].shape[0] // 2
    in_chunks, chunks = wide_in // LANES, width // LANES
    layers = len(owns)
    dma = pltpu.SemaphoreType.DMA
    pool = max(blocks_of(forward_blocks(dims, in_chunks)), blocks_of(backward_blocks(dims, chunks)))
    bufs, sems = reduce_scratch(dims, 3, block, width)
    strip = 128
    vmem = pl.BlockSpec(memory_space=pltpu.VMEM)
    refs = {
        "adj": pltpu.VMEM(adjacency.shape, bf16),
        "stage": pltpu.VMEM((2, strip, adjacency.shape[1]), jnp.int32),
        "stage_sems": dma((2,)),
        "pair": pltpu.VMEM((max(far * near, across * cores) * nodes, 2 * LANES), bf16),
        "pool": pltpu.VMEM((pool, nodes, LANES), f32),
        "sent": pltpu.VMEM((nodes, wide_in), f32),
        "raw": pltpu.VMEM((nodes, wide_in), f32),
        "inverse": pltpu.VMEM((nodes, LANES), f32),
        "mix": pltpu.VMEM((2, 2, width, width), f32),
        "direct": pltpu.VMEM((nodes, width), f32),
        "back": pltpu.VMEM((nodes, width), f32),
        "d_pre": pltpu.VMEM((nodes, width), f32),
        "agg": pltpu.VMEM((layers, nodes, width), f32),
        "hid": pltpu.VMEM((layers + 1, nodes, width), f32),
        "pre": pltpu.VMEM((layers, nodes, width), f32),
        "outer": pltpu.VMEM((2, width, width), f32),
        "ready": pltpu.SemaphoreType.REGULAR((3 * layers - 3,)),
        "forward": forward_sems(dims, in_chunks),
        "backward": backward_sems(dims, chunks),
        "reduce_bufs": bufs,
        "reduce_sems": sems,
    }
    for layer in range(layers):
        refs["every%d" % layer] = pltpu.VMEM(dims + owns[layer].shape, f32)
        refs["spread%d" % layer] = spread_sems(dims)
    return pl.pallas_call(
        functools.partial(train_kernel, dims, in_width, classes),
        out_shape=(
            jax.ShapeDtypeStruct((7 * block, width), f32),
            jax.ShapeDtypeStruct((8, LANES), f32),
        ),
        in_specs=[pl.BlockSpec(memory_space=pl.ANY)] + [vmem] * (3 + layers),
        out_specs=(vmem, vmem),
        scratch_shapes=[refs],
        compiler_params=pltpu.CompilerParams(
            collective_id=name_id, has_side_effects=True, vmem_limit_bytes=63 * 2**20
        ),
    )(adjacency, feats, info, target, *owns)


def dot(left, right, over=((1,), (0,))):
    return lax.dot_general(
        left, right, (over, ((), ())), precision=lax.Precision.HIGH, preferred_element_type=f32
    )


def left_t(left, right):
    return dot(left, right, ((0,), (0,)))


def right_t(left, right):
    return dot(left, right, ((1,), (1,)))


def pad_lanes(value, lanes):
    return jnp.pad(value, ((0, 0), (0, lanes - value.shape[1])))


def fits_on_chip(adjacency):
    return 2 * adjacency.shape[0] * adjacency.shape[1] <= 4 * 2**20


def gradients_fused(dims, features, adjacency, labels, labelled, node_count, w_in, w_side, w_proj, w_out):
    layers, block, width = w_side.shape
    nodes, in_width = features.shape
    classes = w_out.shape[1]
    wide_in = -(-(in_width + 1) // LANES) * LANES
    counts = node_count.astype(f32)
    alpha = 2.0 / (1.0 + counts)
    weight_mask = labelled.astype(f32)
    feats = pad_lanes(features, wide_in)
    info = pad_lanes(jnp.stack([alpha, weight_mask * lax.rsqrt(counts)], 1), LANES)
    target = pad_lanes(labels.astype(f32), LANES)
    w_in_t = pad_lanes(w_in.T, wide_in)
    tail = width - (wide_in - width) - LANES
    count = jnp.broadcast_to(jnp.sum(weight_mask), (block // 2, tail))
    head = jnp.concatenate(
        [w_in_t[:, :width], jnp.concatenate([w_in_t[:, width:], pad_lanes(w_out, LANES), count], 1)], 0
    )
    owns = [
        jnp.concatenate([w_side[l], w_proj[l]] + ([head] if l == 0 else []), 0) for l in range(layers)
    ]
    red, notes = train_on_device(dims, 1, in_width, classes, adjacency, feats, info, target, owns)
    start = [0, 3 * block, 5 * block]
    red_side = jnp.stack([red[at : at + block] for at in start])
    red_proj = jnp.stack([red[at + block : at + 2 * block] for at in start])
    first, second = red[2 * block : 2 * block + block // 2], red[2 * block + block // 2 : 3 * block]
    red_in = jnp.concatenate([first, second[:, : in_width - width]], 1).T
    at_lane = wide_in - width
    red_out = second[:, at_lane : at_lane + classes]
    return second[0, at_lane + LANES], notes[0, 0], red_in, red_side, red_proj, red_out


def gradients_apart(
    dims,
    features,
    adjacency,
    labels,
    labelled,
    node_count,
    w_in,
    w_side,
    w_proj,
    w_out,
):
    layers = w_side.shape[0]
    width = w_side.shape[2]
    in_width = features.shape[1]
    nodes = features.shape[0]
    both = ("wide", "narrow")
    adj = adjacency.astype(bf16)
    counts = node_count.astype(f32)
    alpha = 2.0 / (1.0 + counts)
    lam = lax.rsqrt(counts)
    target = labels.astype(f32)
    weight_mask = labelled.astype(f32)

    spare = -(in_width + 1) % LANES
    sent = jnp.concatenate(
        [alpha[:, None] * features, jnp.ones((nodes, 1), f32), jnp.zeros((nodes, spare), f32)], 1
    )
    summed = aggregate(dims, 1, adj, sent)
    inverse = 1.0 / (1.0 + summed[:, in_width : in_width + 1])
    agg_features = summed[:, :in_width] * inverse

    full_in, full_side, full_proj, full_out = (
        lax.all_gather(w_in, both, axis=1, tiled=True),
        lax.all_gather(w_side, both, axis=1, tiled=True),
        lax.all_gather(w_proj, both, axis=1, tiled=True),
        lax.all_gather(w_out, both, axis=0, tiled=True),
    )
    mix_self = [dot(full_side[l, :width], full_proj[l, :width]) for l in range(layers)]
    mix_neigh = [dot(full_side[l, width:], full_proj[l, width:]) for l in range(layers)]

    kept = []
    hidden = dot(features, full_in)
    agg = dot(agg_features, full_in)
    for layer in range(layers):
        if layer > 0:
            agg = aggregate(dims, 1 + layer, adj, alpha[:, None] * hidden) * inverse
        pre_act = dot(hidden, mix_self[layer]) + dot(agg, mix_neigh[layer])
        kept.append((hidden, agg, pre_act))
        act = jax.nn.silu(pre_act)
        hidden = act * lax.rsqrt(jnp.mean(act * act, -1, keepdims=True) + norm_eps)

    logits = dot(hidden, full_out)
    per = jnp.sum(jax.nn.softplus(logits) - target * logits, -1)
    loss_sum, label_count = lax.psum(
        (jnp.sum(weight_mask * lam * per), jnp.sum(weight_mask)), both
    )
    d_logits = (weight_mask * lam / label_count)[:, None] * (jax.nn.sigmoid(logits) - target)
    g_out = left_t(hidden, d_logits)
    d_out = right_t(d_logits, full_out)
    side_grads = [None] * layers
    proj_grads = [None] * layers
    for layer in reversed(range(layers)):
        hidden, agg, pre_act = kept[layer]
        sig = jax.nn.sigmoid(pre_act)
        act = pre_act * sig
        scale = lax.rsqrt(jnp.mean(act * act, -1, keepdims=True) + norm_eps)
        normed = act * scale
        d_act = scale * (d_out - normed * jnp.mean(d_out * normed, -1, keepdims=True))
        d_pre = d_act * sig * (1.0 + pre_act * (1.0 - sig))
        outer_self = left_t(hidden, d_pre)
        outer_neigh = left_t(agg, d_pre)
        side, proj = full_side[layer], full_proj[layer]
        side_grads[layer] = jnp.concatenate(
            [right_t(outer_self, proj[:width]), right_t(outer_neigh, proj[width:])], 0
        )
        proj_grads[layer] = jnp.concatenate(
            [left_t(side[:width], outer_self), left_t(side[width:], outer_neigh)], 0
        )
        d_self = right_t(d_pre, mix_self[layer])
        if layer > 0:
            back = aggregate(dims, 3 + layer, adj, d_pre * inverse, backward=True)
            d_out = d_self + right_t(alpha[:, None] * back, mix_neigh[layer])
        else:
            g_in = left_t(features, d_self) + left_t(agg_features, right_t(d_pre, mix_neigh[layer]))
    red_in, red_side, red_proj, red_out = (
        lax.psum_scatter(g_in, both, scatter_dimension=1, tiled=True),
        lax.psum_scatter(jnp.stack(side_grads), both, scatter_dimension=1, tiled=True),
        lax.psum_scatter(jnp.stack(proj_grads), both, scatter_dimension=1, tiled=True),
        lax.psum_scatter(g_out, both, scatter_dimension=0, tiled=True),
    )
    return loss_sum, label_count, red_in, red_side, red_proj, red_out


def step_on_device(
    dims,
    features,
    adjacency,
    labels,
    labelled,
    node_count,
    w_in,
    w_side,
    w_proj,
    w_out,
    row_in,
    col_in,
    row_side,
    col_side,
    row_proj,
    col_proj,
    row_out,
    col_out,
):
    width = w_side.shape[2]
    in_width = features.shape[1]
    classes = w_out.shape[1]
    both = ("wide", "narrow")
    gradients = gradients_fused if fits_on_chip(adjacency) else gradients_apart
    loss_sum, label_count, red_in, red_side, red_proj, red_out = gradients(
        dims, features, adjacency, labels, labelled, node_count, w_in, w_side, w_proj, w_out
    )
    sq_in = red_in * red_in
    sq_side = red_side * red_side
    sq_proj = red_proj * red_proj
    sq_out = red_out * red_out
    new_col_in = 0.5 * col_in + 0.5 * (jnp.mean(sq_in, 0) + stat_eps)
    new_row_side = 0.5 * row_side + 0.5 * (jnp.mean(sq_side, 2) + stat_eps)
    new_row_proj = 0.5 * row_proj + 0.5 * (jnp.mean(sq_proj, 2) + stat_eps)
    new_row_out = 0.5 * row_out + 0.5 * (jnp.mean(sq_out, 1) + stat_eps)
    (
        sum_row_in,
        sum_col_side,
        sum_col_proj,
        sum_col_out,
        total_side,
        total_proj,
        total_out,
        over_in,
        over_side,
        over_proj,
        over_out,
    ) = lax.psum(
        (
            jnp.sum(sq_in, 1),
            jnp.sum(sq_side, 1),
            jnp.sum(sq_proj, 1),
            jnp.sum(sq_out, 0),
            jnp.sum(new_row_side, 1),
            jnp.sum(new_row_proj, 1),
            jnp.sum(new_row_out),
            jnp.sum(sq_in / new_col_in[None, :], 1),
            jnp.sum(sq_side / new_row_side[:, :, None], 1),
            jnp.sum(sq_proj / new_row_proj[:, :, None], 1),
            jnp.sum(sq_out / new_row_out[:, None], 0),
        ),
        both,
    )
    new_row_in = 0.5 * row_in + 0.5 * (sum_row_in / width + stat_eps)
    new_col_side = 0.5 * col_side + 0.5 * (sum_col_side / (2 * width) + stat_eps)
    new_col_proj = 0.5 * col_proj + 0.5 * (sum_col_proj / (2 * width) + stat_eps)
    new_col_out = 0.5 * col_out + 0.5 * (sum_col_out / width + stat_eps)
    mean_in = jnp.mean(new_row_in)
    mean_side = total_side / (2 * width)
    mean_proj = total_proj / (2 * width)
    mean_out = total_out / width
    up_in = red_in * lax.rsqrt(new_row_in[:, None] * new_col_in[None, :] / mean_in)
    up_side = red_side * lax.rsqrt(
        new_row_side[:, :, None] * new_col_side[:, None, :] / mean_side[:, None, None]
    )
    up_proj = red_proj * lax.rsqrt(
        new_row_proj[:, :, None] * new_col_proj[:, None, :] / mean_proj[:, None, None]
    )
    up_out = red_out * lax.rsqrt(new_row_out[:, None] * new_col_out[None, :] / mean_out)
    ms_in = mean_in * jnp.sum(over_in / new_row_in) / (in_width * width)
    ms_side = mean_side * jnp.sum(over_side / new_col_side, 1) / (2 * width * width)
    ms_proj = mean_proj * jnp.sum(over_proj / new_col_proj, 1) / (2 * width * width)
    ms_out = mean_out * jnp.sum(over_out / new_col_out) / (width * classes)
    fac_in = 1.0 / jnp.maximum(1.0, jnp.sqrt(ms_in) / clip_level)
    fac_side = 1.0 / jnp.maximum(1.0, jnp.sqrt(ms_side) / clip_level)
    fac_proj = 1.0 / jnp.maximum(1.0, jnp.sqrt(ms_proj) / clip_level)
    fac_out = 1.0 / jnp.maximum(1.0, jnp.sqrt(ms_out) / clip_level)
    new_in = w_in - step_rate * (up_in * fac_in)
    new_side = w_side - step_rate * (up_side * fac_side[:, None, None])
    new_proj = w_proj - step_rate * (up_proj * fac_proj[:, None, None])
    new_out = w_out - step_rate * (up_out * fac_out)
    return (
        loss_sum,
        label_count,
        red_in,
        red_side,
        red_proj,
        red_out,
        new_in,
        new_side,
        new_proj,
        new_out,
        new_row_in,
        new_col_in,
        new_row_side,
        new_col_side,
        new_row_proj,
        new_col_proj,
        new_row_out,
        new_col_out,
    )


def solution(mesh):
    in_specs = (
        P(("wide", "narrow"), None),
        P("wide", "narrow"),
        P(("wide", "narrow"), None),
        P(("wide", "narrow")),
        P(("wide", "narrow")),
        P(None, ("wide", "narrow")),
        P(None, ("wide", "narrow"), None),
        P(None, ("wide", "narrow"), None),
        P(("wide", "narrow"), None),
        P(),
        P(("wide", "narrow")),
        P(None, ("wide", "narrow")),
        P(),
        P(None, ("wide", "narrow")),
        P(),
        P(("wide", "narrow")),
        P(),
    )
    out_specs = (
        P(),
        P(),
        P(None, ("wide", "narrow")),
        P(None, ("wide", "narrow"), None),
        P(None, ("wide", "narrow"), None),
        P(("wide", "narrow"), None),
        P(None, ("wide", "narrow")),
        P(None, ("wide", "narrow"), None),
        P(None, ("wide", "narrow"), None),
        P(("wide", "narrow"), None),
        P(),
        P(("wide", "narrow")),
        P(None, ("wide", "narrow")),
        P(),
        P(None, ("wide", "narrow")),
        P(),
        P(("wide", "narrow")),
        P(),
    )
    shards = functools.partial(step_on_device, grid_of(mesh))
    return jax.shard_map(shards, mesh=mesh, in_specs=in_specs, out_specs=out_specs, check_vma=False)
```

```python
import functools
import jax
import jax.numpy as jnp
from jax import lax
from jax.experimental import pallas as pl
from jax.experimental.pallas import tpu as pltpu
from jax.sharding import PartitionSpec as P

MESH = pl.DeviceIdType.MESH
LANES = 128
CORES = 2
f32 = jnp.float32
bf16 = jnp.bfloat16


norm_eps = 1e-06
stat_eps = 1e-30
clip_level = 0.5
step_rate = 0.04


def grid_of(mesh):
    wide, narrow = mesh.shape["wide"], mesh.shape["narrow"]
    far = 4 if wide % 4 == 0 else wide
    return far, wide // far, narrow // CORES, CORES


def place(dims):
    far, near, across, cores = dims
    wide, narrow = lax.axis_index("wide"), lax.axis_index("narrow")
    return wide // near, lax.rem(wide, near), narrow // cores, lax.rem(narrow, cores)


def device(dims, far_at, near_at, across_at, core_at):
    return (far_at * dims[1] + near_at, across_at * dims[3] + core_at)


def send(src, dst, send_sem, recv_sem, target):
    pltpu.make_async_remote_copy(
        src_ref=src,
        dst_ref=dst,
        send_sem=send_sem,
        recv_sem=recv_sem,
        device_id=target,
        device_id_type=MESH,
    ).start()


def arrived(dst, recv_sem):
    pltpu.make_async_copy(dst, dst, recv_sem).wait()


def left_source(src, send_sem):
    pltpu.make_async_copy(src, src, send_sem).wait()


def halves(value):
    high = value.astype(bf16)
    return high, (value - high.astype(f32)).astype(bf16)


def neighbours(dims, at):
    far, near, across, cores = dims
    p, q, x, c = at
    always = [(p, lax.rem(q + step, near), x, c) for step in range(1, near)]
    always += [(p, q, lax.rem(x + step, across), c) for step in range(1, across)]
    always += [(p, q, x, 1 - c)]
    return always


def line_peers(dims, at):
    far = dims[0]
    p, q, x, c = at
    return [(lax.rem(p + step, far), q, x, c) for step in range(1, far)]


def entry_barrier(dims, at):
    barrier = pltpu.get_barrier_semaphore()
    everyone = neighbours(dims, at) + line_peers(dims, at)
    for other in everyone:
        pl.semaphore_signal(barrier, inc=1, device_id=device(dims, *other), device_id_type=MESH)
    pl.semaphore_wait(barrier, len(everyone))


def chunk(ref, k):
    return ref.at[:, pl.ds(k * LANES, LANES)]


class SpreadAll:
    def __init__(self, dims, at, every, right_out, left_out, near_out, across_out, core_out, came):
        self.dims, self.at, self.every = dims, at, every
        self.right_out, self.left_out, self.near_out = right_out, left_out, near_out
        self.across_out, self.core_out, self.came = across_out, core_out, came

    def away(self, distance):
        far, p = self.dims[0], self.at[0]
        if distance == 0:
            return [(p, None)]
        return [(p - distance, p >= distance), (p + distance, p + distance < far)]

    def when(self, flag, act):
        if flag is None:
            act()
        else:
            pl.when(flag)(act)

    def on_line(self, pp, src):
        far, near, across, cores = self.dims
        p, q, x, c = self.at
        dst = self.every.at[pp, q, x, c]
        sem = self.came.at[pp, q, x, c]

        @pl.when(jnp.logical_and(p < far - 1, pp <= p))
        def _():
            send(src, dst, self.right_out.at[pp], sem, device(self.dims, p + 1, q, x, c))

        @pl.when(jnp.logical_and(p > 0, pp >= p))
        def _():
            send(src, dst, self.left_out.at[pp], sem, device(self.dims, p - 1, q, x, c))

        for step in range(1, near):
            send(src, dst, self.near_out.at[pp, step - 1], sem, device(self.dims, p, lax.rem(q + step, near), x, c))

    def on_plane(self, pp, qq, src):
        far, near, across, cores = self.dims
        p, q, x, c = self.at
        dst, sem = self.every.at[pp, qq, x, c], self.came.at[pp, qq, x, c]
        for step in range(1, across):
            send(src, dst, self.across_out.at[pp, qq, step - 1], sem, device(self.dims, p, q, lax.rem(x + step, across), c))
        self.to_core(pp, qq, x, src)

    def to_core(self, pp, qq, xx, src):
        p, q, x, c = self.at
        send(src, self.every.at[pp, qq, xx, c], self.core_out.at[pp, qq, xx], self.came.at[pp, qq, xx, c], device(self.dims, p, q, x, 1 - c))

    def wait(self, *where):
        arrived(self.every.at[where], self.came.at[where])

    def begin(self):
        p, q, x, c = self.at
        own = self.every.at[p, q, x, c]
        self.on_line(p, own)
        self.on_plane(p, q, own)

    def from_line(self, distance):
        p, q, x, c = self.at
        for pp, flag in self.away(distance):
            def act(pp=pp):
                self.wait(pp, q, x, c)
                self.on_line(pp, self.every.at[pp, q, x, c])
                self.on_plane(pp, q, self.every.at[pp, q, x, c])
            self.when(flag, act)

    def from_near(self, distance):
        far, near, across, cores = self.dims
        p, q, x, c = self.at
        for pp, flag in self.away(distance):
            def act(pp=pp):
                for step in range(1, near):
                    qq = lax.rem(q + step, near)
                    self.wait(pp, qq, x, c)
                    self.on_plane(pp, qq, self.every.at[pp, qq, x, c])
            self.when(flag, act)

    def from_across(self, distance):
        far, near, across, cores = self.dims
        p, q, x, c = self.at
        for pp, flag in self.away(distance):
            def act(pp=pp):
                for qq in range(near):
                    for step in range(1, across):
                        xx = lax.rem(x + step, across)
                        self.wait(pp, qq, xx, c)
                        self.to_core(pp, qq, xx, self.every.at[pp, qq, xx, c])
            self.when(flag, act)

    def step(self, distance):
        self.from_line(distance)
        self.from_near(distance - 1)
        if distance >= 2:
            self.from_across(distance - 2)

    def drain(self):
        far = self.dims[0]
        self.from_near(far - 1)
        if far >= 2:
            self.from_across(far - 2)

    def end(self):
        far, near, across, cores = self.dims
        p, q, x, c = self.at
        self.from_across(far - 1)
        for pp in range(far):
            for qq in range(near):
                for xx in range(across):
                    self.wait(pp, qq, xx, 1 - c)
        for pp in range(far):
            block = self.every.at[pp, q, x, c]

            @pl.when(jnp.logical_and(p < far - 1, pp <= p))
            def _(pp=pp, block=block):
                left_source(block, self.right_out.at[pp])

            @pl.when(jnp.logical_and(p > 0, pp >= p))
            def _(pp=pp, block=block):
                left_source(block, self.left_out.at[pp])

            for step in range(1, near):
                left_source(block, self.near_out.at[pp, step - 1])
            for qq in range(near):
                for step in range(1, across):
                    left_source(block, self.across_out.at[pp, qq, step - 1])
                for xx in range(across):
                    left_source(block, self.core_out.at[pp, qq, xx])


def spread_sems(dims):
    far, near, across, cores = dims
    dma = pltpu.SemaphoreType.DMA
    return [
        dma((far,)),
        dma((far,)),
        dma((far, max(near - 1, 1))),
        dma((far, near, max(across - 1, 1))),
        dma((far, near, across)),
        dma((far, near, across, cores)),
    ]


class Blocks:
    def __init__(self, pool, base, *shape):
        self.pool, self.base, self.shape = pool, base, shape

    @property
    def count(self):
        total = 1
        for size in self.shape:
            total *= size
        return total

    def flat(self, where):
        index = 0
        for size, at in zip(self.shape, where):
            index = index * size + at
        left = 1
        for size in self.shape[len(where) :]:
            left *= size
        return self.base + index * left, left

    def ref(self, *where):
        start, _ = self.flat(where)
        return self.pool.at[start]

    def run(self, *where):
        start, left = self.flat(where)
        return self.pool.at[pl.ds(start, left)]

    def add(self, where, other):
        ref = self.ref(*where)
        ref[...] = ref[...] + other[...]


def take(pool, *shapes):
    base, made = 0, []
    for shape in shapes:
        made.append(Blocks(pool, base, *shape))
        base += made[-1].count
    return made


def forward_blocks(dims, chunks):
    far, near, across, cores = dims
    return (
        (chunks, far, near),
        (chunks, cores, across),
        (chunks, across),
        (chunks, across),
    )


def backward_blocks(dims, chunks):
    far, near, across, cores = dims
    return (
        (chunks, across, cores),
        (chunks, far, near),
        (far, near),
        (chunks, far),
        (near,),
        (chunks,),
        (chunks, far, near),
    )


def blocks_of(shapes):
    total = 0
    for shape in shapes:
        size = 1
        for extent in shape:
            size *= extent
        total += size
    return total


def counted(dims, at):
    p, far = at[0], dims[0]
    ends = jnp.where(p > 0, 1, 0) + jnp.where(p < far - 1, 1, 0)
    return len(neighbours(dims, at)) + ends


def announce(dims, at, sem):
    far = dims[0]
    p, q, x, c = at
    for other in neighbours(dims, at):
        pl.semaphore_signal(sem, inc=1, device_id=device(dims, *other), device_id_type=MESH)

    @pl.when(p > 0)
    def _():
        pl.semaphore_signal(sem, inc=1, device_id=device(dims, p - 1, q, x, c), device_id_type=MESH)

    @pl.when(p < far - 1)
    def _():
        pl.semaphore_signal(sem, inc=1, device_id=device(dims, p + 1, q, x, c), device_id_type=MESH)


def await_all(dims, at, sem):
    pl.semaphore_wait(sem, counted(dims, at))


class Hooks:
    def __init__(self, **acts):
        self.acts = acts

    def run(self, name):
        for act in self.acts.get(name, ()):
            act()


def forward_pass(dims, at, chunks, adj, sent, out, pair, pool, sems, hooks):
    to_right, to_left, to_near, came, core_sems, across_out, across_in = sems
    gathered, part, from_core, from_across = take(pool, *forward_blocks(dims, chunks))
    far, near, across, cores = dims
    p, q, x, c = at
    nodes = sent.shape[0]
    early = chunks - 1
    right, left = device(dims, p + 1, q, x, c), device(dims, p - 1, q, x, c)
    others = [lax.rem(q + step, near) for step in range(1, near)]

    def go_right(k, pp, qq, src):
        @pl.when(p < far - 1)
        def _():
            send(src, gathered.ref(k, pp, qq), to_right.at[k, pp, qq], came.at[k, pp, qq], right)

    def go_left(k, pp, qq, src):
        @pl.when(p > 0)
        def _():
            send(src, gathered.ref(k, pp, qq), to_left.at[k, pp, qq], came.at[k, pp, qq], left)

    def go_near(k, pp, src):
        for step, qq in enumerate(others):
            send(src, gathered.ref(k, pp, q), to_near.at[k, pp, step], came.at[k, pp, q], device(dims, p, qq, x, c))

    hooks.run("begin")
    for k in [early] + list(range(chunks - 1)):
        src = chunk(sent, k)
        go_near(k, p, src)
        go_right(k, p, q, src)
        go_left(k, p, q, src)
    for k in range(chunks):
        gathered.ref(k, p, q)[...] = sent[:, k * LANES : (k + 1) * LANES]
    hooks.run("sent")
    for qq in others:
        arrived(gathered.ref(early, p, qq), came.at[early, p, qq])
        go_right(early, p, qq, gathered.ref(early, p, qq))
        go_left(early, p, qq, gathered.ref(early, p, qq))
    group = near * nodes

    def accumulate(k, pp, fresh):
        high, low = halves(gathered.run(k, pp)[...].reshape(group, LANES))
        pair[:group, :LANES] = high
        pair[:group, LANES:] = low
        columns = pl.ds(pl.multiple_of(pp * group, group), group)

        def product(index, carry):
            cc = lax.rem(index // across + 1 + c, cores)
            xx = lax.rem(index, across)
            rows = pl.multiple_of((xx * cores + cc) * nodes, nodes)
            both = jnp.dot(adj[pl.ds(rows, nodes), columns], pair[:group, :], preferred_element_type=f32)
            both = both[:, :LANES] + both[:, LANES:]
            into = part.ref(k, cc, xx)
            into[...] = both if fresh else into[...] + both
            return carry

        lax.fori_loop(0, cores * across, product, 0)

    def from_near(k, pp):
        if isinstance(k, int) and k == early:
            return

        def act():
            for qq in others:
                arrived(gathered.ref(k, pp, qq), came.at[k, pp, qq])

        if isinstance(k, int):
            act()
        else:
            pl.when(k != early)(act)

    def sides(distance):
        if distance == 0:
            return [(p, p >= 0)]
        return [(p - distance, p >= distance), (p + distance, p + distance < far)]

    def from_line(step, k):
        for pp, flag in sides(step):

            @pl.when(flag)
            def _(pp=pp):
                for qq in [q] + (others if k == early else []):
                    block = gathered.ref(k, pp, qq)
                    arrived(block, came.at[k, pp, qq])

                    @pl.when(pp < p)
                    def _():
                        go_right(k, pp, qq, block)

                    @pl.when(pp > p)
                    def _():
                        go_left(k, pp, qq, block)

                if k != early:
                    go_near(k, pp, gathered.ref(k, pp, q))

    def take_in(k, distance):
        for pp, flag in sides(distance):

            @pl.when(flag)
            def _(pp=pp):
                from_near(k, pp)
                accumulate(k, pp, distance == 0)

    def every_chunk(distance):
        def act(k, carry):
            take_in(k, distance)
            return carry

        lax.fori_loop(0, chunks, act, 0)

    def reduce_across(k):
        arrived(from_core.run(k), core_sems.at[1, k])
        for step in range(1, across):
            xx = lax.rem(x + step, across)
            part.add((k, c, xx), from_core.ref(k, xx))
            send(part.ref(k, c, xx), from_across.ref(k, x), across_out.at[k, xx], across_in.at[k, x], device(dims, p, q, xx, c))

    def finish(k):
        total = part.ref(k, c, x)[...] + from_core.ref(k, x)[...]
        for step in range(1, across):
            xx = lax.rem(x + step, across)
            arrived(from_across.ref(k, xx), across_in.at[k, xx])
            total = total + from_across.ref(k, xx)[...]
        out[:, k * LANES : (k + 1) * LANES] = total

    for step in range(1, far):
        hooks.run("step%d" % step)
        for k in range(chunks):
            from_line(step, k)
            if step == far - 1 and step >= 2:
                take_in(k, step - 1)
        if step == 1 or step < far - 1:
            every_chunk(step - 1)
    hooks.run("drain")
    order = list(range(chunks))
    for i, k in enumerate(order):
        take_in(k, far - 1)
        send(part.run(k, 1 - c), from_core.run(k), core_sems.at[0, k], core_sems.at[1, k], device(dims, p, q, x, 1 - c))
        if i >= 1:
            reduce_across(order[i - 1])
        if i >= 2:
            finish(order[i - 2])
    hooks.run("product")
    reduce_across(order[-1])
    hooks.run("shadow")
    if chunks >= 2:
        finish(order[-2])
    finish(order[-1])

    for k in range(chunks):
        left_source(part.run(k, 1 - c), core_sems.at[0, k])
        for step in range(1, across):
            xx = lax.rem(x + step, across)
            left_source(part.ref(k, c, xx), across_out.at[k, xx])
        for pp in range(far):
            for qq in [q] + (others if k == early else []):
                block = gathered.ref(k, pp, qq)

                @pl.when(jnp.logical_and(p < far - 1, pp <= p))
                def _(k=k, pp=pp, qq=qq, block=block):
                    left_source(block, to_right.at[k, pp, qq])

                @pl.when(jnp.logical_and(p > 0, pp >= p))
                def _(k=k, pp=pp, qq=qq, block=block):
                    left_source(block, to_left.at[k, pp, qq])

            def near_sent(k=k, pp=pp):
                for step in range(near - 1):
                    left_source(gathered.ref(k, pp, q), to_near.at[k, pp, step])

            if k == early:
                pl.when(pp == p)(near_sent)
            else:
                near_sent()


def forward_sems(dims, chunks):
    far, near, across, cores = dims
    dma = pltpu.SemaphoreType.DMA
    return [dma((chunks, far, near))] * 4 + [dma((2, chunks)), dma((chunks, across)), dma((chunks, across))]


def backward_pass(dims, at, chunks, adj, sent, out, pair, pool, sems, hooks):
    row_out, row_in, near_out, near_in, right_out, left_out, left_in, right_in = sems
    rows, part, line_early, line_rest, right_early, right_rest, from_near = take(
        pool, *backward_blocks(dims, chunks)
    )
    far, near, across, cores = dims
    p, q, x, c = at
    nodes = sent.shape[0]
    total_rows = across * cores * nodes
    early = 0
    right, left = device(dims, p + 1, q, x, c), device(dims, p - 1, q, x, c)
    others = [lax.rem(q + step, near) for step in range(1, near)]
    crossing = [lax.rem(x + step, across) for step in range(1, across)]

    def on_line(k, pp, qq):
        return line_early.ref(pp, qq) if k == early else line_rest.ref(k, pp)

    def from_right_own(k, qq):
        return right_early.ref(qq) if k == early else right_rest.ref(k)

    for k in range(chunks):
        src = chunk(sent, k)
        for xx in crossing:
            send(src, rows.ref(k, x, c), row_out.at[k, xx], row_in.at[k, x, c], device(dims, p, q, xx, c))
        send(src, rows.ref(k, x, c), row_out.at[k, across + x], row_in.at[k, x, c], device(dims, p, q, x, 1 - c))
    for k in range(chunks):
        rows.ref(k, x, c)[...] = sent[:, k * LANES : (k + 1) * LANES]
    hooks.run("sent")

    def dest(i):
        rights = far - 1 - p
        low = jnp.where(i < rights, far - 1 - i, jnp.where(i < far - 1, i - rights, p))
        high = jnp.where(i < p, i, jnp.where(i < far - 1, far - 1 - (i - p), p))
        return jnp.where(p < far // 2, low, high)

    def along(k, pp, qq):
        @pl.when(pp > p)
        def _():
            @pl.when(p > 0)
            def _():
                arrived(on_line(k, pp, qq), left_in.at[k, pp, qq])
                part.add((k, pp, qq), on_line(k, pp, qq))

            send(part.ref(k, pp, qq), on_line(k, pp, qq), right_out.at[k, pp, qq], left_in.at[k, pp, qq], right)

        @pl.when(pp < p)
        def _():
            @pl.when(p < far - 1)
            def _():
                arrived(on_line(k, pp, qq), right_in.at[k, pp, qq])
                part.add((k, pp, qq), on_line(k, pp, qq))

            @pl.when(pp < p - 1)
            def _():
                send(part.ref(k, pp, qq), on_line(k, pp, qq), left_out.at[k, pp, qq], right_in.at[k, pp, qq], left)

            @pl.when(pp == p - 1)
            def _():
                send(part.ref(k, pp, qq), from_right_own(k, qq), left_out.at[k, pp, qq], right_in.at[k, pp, qq], left)

    def settle(k, qq):
        @pl.when(p > 0)
        def _():
            arrived(on_line(k, p, qq), left_in.at[k, p, qq])
            part.add((k, p, qq), on_line(k, p, qq))

        @pl.when(p < far - 1)
        def _():
            arrived(from_right_own(k, qq), right_in.at[k, p, qq])
            part.add((k, p, qq), from_right_own(k, qq))

    def line(k):
        def step(i, carry):
            pp = dest(i)
            if k == early:
                for qq in others + [q]:
                    along(k, pp, qq)
            else:
                for qq in others:
                    arrived(from_near.ref(k, pp, qq), near_in.at[k, pp, qq])
                    part.add((k, pp, q), from_near.ref(k, pp, qq))
                along(k, pp, q)
            return carry

        lax.fori_loop(0, far, step, 0)

    def early_end():
        for step, qq in enumerate(others):
            settle(early, qq)
            send(part.ref(early, p, qq), from_near.ref(early, p, q), near_out.at[early, p, step], near_in.at[early, p, q], device(dims, p, qq, x, c))

    for k in range(chunks):
        for xx in crossing:
            arrived(rows.ref(k, xx, c), row_in.at[k, xx, c])
            send(rows.ref(k, xx, c), rows.ref(k, xx, c), row_out.at[k, across + xx], row_in.at[k, xx, c], device(dims, p, q, x, 1 - c))
        for xx in range(across):
            arrived(rows.ref(k, xx, 1 - c), row_in.at[k, xx, 1 - c])
        high, low = halves(rows.run(k)[...].reshape(total_rows, LANES))
        pair[:total_rows, :LANES] = high
        pair[:total_rows, LANES:] = low

        def product(i, carry, k=k):
            pp = dest(i // near)
            qq = lax.rem(q + 1 + lax.rem(i, near), near)
            start = pl.multiple_of((pp * near + qq) * nodes, nodes)
            both = lax.dot_general(adj[:, pl.ds(start, nodes)], pair[:total_rows, :], (((0,), (0,)), ((), ())), preferred_element_type=f32)
            part.ref(k, pp, qq)[...] = both[:, :LANES] + both[:, LANES:]
            if k != early:
                @pl.when(qq != q)
                def _():
                    send(part.ref(k, pp, qq), from_near.ref(k, pp, q), near_out.at[k, pp, lax.rem(qq - q - 1 + near, near)], near_in.at[k, pp, q], device(dims, p, qq, x, c))

            return carry

        lax.fori_loop(0, far * near, product, 0)
        if k >= 1:
            line(k - 1)
        hooks.run("chunk%d" % k)
    early_end()
    hooks.run("early")
    line(chunks - 1)
    hooks.run("line")
    for k in range(chunks):
        settle(k, q)
        total = part.ref(k, p, q)[...]
        if k == early:
            for qq in others:
                arrived(from_near.ref(k, p, qq), near_in.at[k, p, qq])
                total = total + from_near.ref(k, p, qq)[...]
        out[:, k * LANES : (k + 1) * LANES] = total

    for k in range(chunks):
        for xx in crossing:
            left_source(rows.ref(k, x, c), row_out.at[k, xx])
        for xx in range(across):
            left_source(rows.ref(k, xx, c), row_out.at[k, across + xx])
        for pp in range(far):
            for qq in [q] + (others if k == early else []):
                @pl.when(pp > p)
                def _(k=k, pp=pp, qq=qq):
                    left_source(part.ref(k, pp, qq), right_out.at[k, pp, qq])

                @pl.when(pp < p)
                def _(k=k, pp=pp, qq=qq):
                    left_source(part.ref(k, pp, qq), left_out.at[k, pp, qq])

            def near_sent(k=k, pp=pp):
                for step in range(near - 1):
                    left_source(part.ref(k, pp, q), near_out.at[k, pp, step])

            if k == early:
                pl.when(pp == p)(near_sent)
            else:
                near_sent()


def backward_sems(dims, chunks):
    far, near, across, cores = dims
    dma = pltpu.SemaphoreType.DMA
    return [dma((chunks, 2 * across)), dma((chunks, across, cores))] + [dma((chunks, far, near))] * 6


class ReduceAll:
    def __init__(self, dims, at, own, first_rows, out, bufs, sems):
        self.dims, self.at, self.own, self.first_rows, self.out = dims, at, own, first_rows, out
        self.halfway, self.from_first, self.from_next, self.from_left, self.from_right = bufs
        self.core_sems, self.first_out, self.first_in, self.next_out, self.next_in = sems[:5]
        self.right_out, self.left_out, self.left_in, self.right_in = sems[5:]
        self.depth = self.halfway.shape[4]
        self.turned = [False] * len(first_rows)

    def rows(self, j):
        return pl.ds(self.first_rows[j], self.depth)

    def peers(self, turned):
        far, near, across, cores = self.dims
        p, q, x, c = self.at
        if turned:
            return [(lax.rem(q + step, near), device(self.dims, p, lax.rem(q + step, near), x, c)) for step in range(1, near)]
        return [(lax.rem(x + step, across), device(self.dims, p, q, lax.rem(x + step, across), c)) for step in range(1, across)]

    def core_stage(self, j):
        p, q, x, c = self.at
        send(self.own.at[:, :, :, 1 - c, self.rows(j)], self.halfway.at[j], self.core_sems.at[0, j], self.core_sems.at[1, j], device(self.dims, p, q, x, 1 - c))

    def across_stage(self, j):
        p, q, x, c = self.at
        arrived(self.halfway.at[j], self.core_sems.at[1, j])
        self.halfway[j] = self.halfway[j] + self.own[:, :, :, c, self.rows(j)]
        for i, (other, target) in enumerate(self.peers(self.turned[j])):
            src = self.halfway.at[j, :, other] if self.turned[j] else self.halfway.at[j, :, :, other]
            send(src, self.from_first.at[j, i], self.first_out.at[j, i], self.first_in.at[j, i], target)

    def near_stage(self, j):
        p, q, x, c = self.at
        for i, _ in enumerate(self.peers(self.turned[j])):
            arrived(self.from_first.at[j, i], self.first_in.at[j, i])
            if self.turned[j]:
                self.halfway[j, :, q] = self.halfway[j, :, q] + self.from_first[j, i]
            else:
                self.halfway[j, :, :, x] = self.halfway[j, :, :, x] + self.from_first[j, i]
        for i, (other, target) in enumerate(self.peers(not self.turned[j])):
            src = self.halfway.at[j, :, q, other] if self.turned[j] else self.halfway.at[j, :, other, x]
            send(src, self.from_next.at[j, i], self.next_out.at[j, i], self.next_in.at[j, i], target)

    def line_stage(self, j):
        far, near, across, cores = self.dims
        p, q, x, c = self.at
        for i, _ in enumerate(self.peers(not self.turned[j])):
            arrived(self.from_next.at[j, i], self.next_in.at[j, i])
            self.halfway[j, :, q, x] = self.halfway[j, :, q, x] + self.from_next[j, i]
        for distance in range(far - 1, 0, -1):
            pp = p + distance

            @pl.when(pp < far)
            def _(pp=pp):
                @pl.when(p > 0)
                def _():
                    arrived(self.from_left.at[j, pp], self.left_in.at[j, pp])
                    self.halfway[j, pp, q, x] = self.halfway[j, pp, q, x] + self.from_left[j, pp]

                send(self.halfway.at[j, pp, q, x], self.from_left.at[j, pp], self.right_out.at[j, pp], self.left_in.at[j, pp], device(self.dims, p + 1, q, x, c))

            pm = p - distance

            @pl.when(pm >= 0)
            def _(pm=pm):
                @pl.when(p < far - 1)
                def _():
                    arrived(self.from_right.at[j, pm], self.right_in.at[j, pm])
                    self.halfway[j, pm, q, x] = self.halfway[j, pm, q, x] + self.from_right[j, pm]

                send(self.halfway.at[j, pm, q, x], self.from_right.at[j, pm], self.left_out.at[j, pm], self.right_in.at[j, pm], device(self.dims, p - 1, q, x, c))

    def last_stage(self, j, out_row):
        far, near, across, cores = self.dims
        p, q, x, c = self.at
        into = self.out.at[pl.ds(out_row, self.depth)]
        into[...] = self.halfway[j, p, q, x]

        @pl.when(p > 0)
        def _():
            arrived(self.from_left.at[j, p], self.left_in.at[j, p])
            into[...] = into[...] + self.from_left[j, p]

        @pl.when(p < far - 1)
        def _():
            arrived(self.from_right.at[j, p], self.right_in.at[j, p])
            into[...] = into[...] + self.from_right[j, p]

    def end(self, j):
        far, near, across, cores = self.dims
        p, q, x, c = self.at
        left_source(self.own.at[:, :, :, 1 - c, self.rows(j)], self.core_sems.at[0, j])
        for i, _ in enumerate(self.peers(self.turned[j])):
            left_source(self.from_first.at[j, i], self.first_out.at[j, i])
        for i, _ in enumerate(self.peers(not self.turned[j])):
            left_source(self.from_next.at[j, i], self.next_out.at[j, i])
        for pp in range(far):
            @pl.when(pp > p)
            def _(pp=pp):
                left_source(self.from_left.at[j, pp], self.right_out.at[j, pp])

            @pl.when(pp < p)
            def _(pp=pp):
                left_source(self.from_right.at[j, pp], self.left_out.at[j, pp])


def reduce_scratch(dims, pieces, depth, width):
    far, near, across, cores = dims
    dma = pltpu.SemaphoreType.DMA
    bufs = [
        pltpu.VMEM((pieces, far, near, across, depth, width), f32),
        pltpu.VMEM((pieces, max(across - 1, 1), far, near, depth, width), f32),
        pltpu.VMEM((pieces, max(near - 1, 1), far, depth, width), f32),
        pltpu.VMEM((pieces, far, depth, width), f32),
        pltpu.VMEM((pieces, far, depth, width), f32),
    ]
    sems = [
        dma((2, pieces)),
        dma((pieces, max(across - 1, 1))),
        dma((pieces, max(across - 1, 1))),
        dma((pieces, max(near - 1, 1))),
        dma((pieces, max(near - 1, 1))),
    ] + [dma((pieces, far))] * 4
    return bufs, sems


def forward_kernel(dims, chunks, adj, sent, out, pair, pool, *sems):
    at = place(dims)
    entry_barrier(dims, at)
    forward_pass(dims, at, chunks, adj, sent, out, pair, pool, sems, Hooks())


def backward_kernel(dims, chunks, adj, sent, out, pair, pool, *sems):
    at = place(dims)
    entry_barrier(dims, at)
    backward_pass(dims, at, chunks, adj, sent, out, pair, pool, sems, Hooks())


def aggregate(dims, name_id, adj, sent, backward=False):
    far, near, across, cores = dims
    nodes, width = sent.shape
    chunks = width // LANES
    kernel = backward_kernel if backward else forward_kernel
    blocks = backward_blocks if backward else forward_blocks
    sems = backward_sems if backward else forward_sems
    depth = (across * cores if backward else far * near) * nodes
    return pl.pallas_call(
        functools.partial(kernel, dims, chunks),
        out_shape=jax.ShapeDtypeStruct((nodes, width), f32),
        in_specs=[pl.BlockSpec(memory_space=pltpu.VMEM)] * 2,
        out_specs=pl.BlockSpec(memory_space=pltpu.VMEM),
        scratch_shapes=[
            pltpu.VMEM((depth, 2 * LANES), bf16),
            pltpu.VMEM((blocks_of(blocks(dims, chunks)), nodes, LANES), f32),
        ]
        + sems(dims, chunks),
        compiler_params=pltpu.CompilerParams(
            collective_id=name_id, has_side_effects=True, vmem_limit_bytes=60 * 2**20
        ),
    )(adj, sent)


def contract(left, right, over):
    first, second = halves(left), halves(right)

    def go(a, b):
        return lax.dot_general(a, b, (over, ((), ())), preferred_element_type=f32)

    return go(first[0], second[0]) + (go(first[0], second[1]) + go(first[1], second[0]))


def plain(left, right):
    return contract(left, right, ((1,), (0,)))


def left_flip(left, right):
    return contract(left, right, ((0,), (0,)))


def right_flip(left, right):
    return contract(left, right, ((1,), (1,)))


def rows_of(every, half, start, size):
    far = every.shape[0]
    value = every[half * (far // 2) : (half + 1) * (far // 2), :, :, :, start : start + size, :]
    return value.reshape(-1, value.shape[-1])


def put_rows(every, half, start, size, value):
    far = every.shape[0]
    shape = (far // 2,) + every.shape[1:4] + (size, value.shape[-1])
    every[half * (far // 2) : (half + 1) * (far // 2), :, :, :, start : start + size, :] = value.reshape(shape)


def activation(pre_act):
    sig = jax.nn.sigmoid(pre_act)
    act = pre_act * sig
    return sig, act, lax.rsqrt(jnp.mean(act * act, -1, keepdims=True) + norm_eps)


def column_of(row):
    size = row.shape[1]
    same = lax.broadcasted_iota(jnp.int32, (size, size), 0) == lax.broadcasted_iota(jnp.int32, (size, size), 1)
    return jnp.sum(jnp.where(same, jnp.broadcast_to(row, (size, size)), 0.0), 1, keepdims=True)


def row_of(column):
    size = column.shape[0]
    same = lax.broadcasted_iota(jnp.int32, (size, size), 0) == lax.broadcasted_iota(jnp.int32, (size, size), 1)
    return jnp.sum(jnp.where(same, jnp.broadcast_to(column, (size, size)), 0.0), 0, keepdims=True)


def blend(old, mean_square):
    return 0.5 * old + 0.5 * (mean_square + stat_eps)


def row_statistic(grad, old, count):
    square = grad * grad
    return square, blend(old, jnp.sum(square, 1, keepdims=True) / count)


def train_kernel(dims, in_width, classes, adj_hbm, feats, info, w_in_t, w_side, w_proj, w_out, col_in, row_side, row_proj, row_out, red, stat, refs):
    far, near, across, cores = dims
    at = place(dims)
    nodes, wide_in = feats.shape
    layers, block, width = w_side.shape
    every = [refs["every%d" % layer] for layer in range(layers)]
    adj, stage, stage_sems = refs["adj"], refs["stage"], refs["stage_sems"]
    pair, pool, sent = refs["pair"], refs["pool"], refs["sent"]
    raw, inverse, mix, direct, back = refs["raw"], refs["inverse"], refs["mix"], refs["direct"], refs["back"]
    agg, hid, pre, outer, ready = refs["agg"], refs["hid"], refs["pre"], refs["outer"], refs["ready"]
    in_chunks, chunks = wide_in // LANES, width // LANES
    head = 2 * block
    tail = wide_in - width + LANES

    strip = stage.shape[1]

    def strip_copy(i):
        return pltpu.make_async_copy(adj_hbm.at[pl.ds(i * strip, strip)], stage.at[i % 2], stage_sems.at[i % 2])

    strips = adj.shape[0] // strip
    strip_copy(0).start()
    strip_copy(1).start()
    for layer in range(layers):
        mine = every[layer].at[at]
        mine[:block] = w_side[layer]
        mine[block : 2 * block] = w_proj[layer]
    mine = every[0].at[at]
    mine[head : head + block // 2] = w_in_t[:, :width]
    mine[head + block // 2 : head + block, : wide_in - width] = w_in_t[:, width:]
    mine[head + block // 2 : head + block, wide_in - width : tail] = jnp.zeros((block // 2, LANES), f32)
    mine[head + block // 2 : head + block, wide_in - width : wide_in - width + classes] = w_out[...]
    marked = jnp.sum(info[:, LANES + 2 : LANES + 3], 0, keepdims=True)
    mine[head + block // 2 : head + block, tail:] = jnp.broadcast_to(marked, (block // 2, width - tail))
    entry_barrier(dims, at)
    target = info[:, :LANES]
    alpha = info[:, LANES : LANES + 1]
    weight = info[:, LANES + 1 : LANES + 2]
    lane = lax.broadcasted_iota(jnp.int32, (nodes, wide_in), 1)
    sent[...] = jnp.where(lane == in_width, 1.0, feats[...] * alpha)

    def load_adjacency():
        for i in range(strips):
            strip_copy(i).wait()
            adj[i * strip : (i + 1) * strip, :] = stage[i % 2].astype(f32).astype(bf16)
            if i + 2 < strips:
                strip_copy(i + 2).start()

    spreads = [SpreadAll(dims, at, every[l], *refs["spread%d" % l]) for l in range(layers)]

    def mixing(layer):
        for half in range(2):
            side = rows_of(every[layer], half, 0, block)
            proj = rows_of(every[layer], half, block, block)
            mix[layer % 2, half] = plain(side, proj)

    def input_weights():
        def both(start):
            return jnp.concatenate([rows_of(every[0], half, start, block // 2) for half in range(2)], 0)

        first, second = both(head), both(head + block // 2)
        return jnp.concatenate([first, second[:, : wide_in - width]], 1)

    def onward(layer):
        spreads[layer].drain()
        if layer + 1 < layers:
            spreads[layer + 1].begin()

    def ahead(layer):
        spreads[layer].end()
        mixing(layer)
        if layer == 0:
            hid[0] = right_flip(feats[...], input_weights())
        direct[...] = plain(hid[layer], mix[layer % 2, 0])

    rounds = iter(range(ready.shape[0]))
    for layer in range(layers):
        acts = {"drain": [functools.partial(onward, layer)], "shadow": [functools.partial(ahead, layer)]}
        for step in range(1, far):
            acts["step%d" % step] = [functools.partial(spreads[layer].step, step)]
        if layer == 0:
            acts["begin"] = [spreads[0].begin]
            acts["sent"] = [load_adjacency]
            forward_pass(dims, at, in_chunks, adj, sent, raw, pair, pool, refs["forward"], Hooks(**acts))
            turn = ready.at[next(rounds)]
            announce(dims, at, turn)
            inverse[...] = jnp.broadcast_to(1.0 / (1.0 + raw[:, in_width : in_width + 1]), inverse.shape)
            raw[...] = jnp.where(lane < in_width, raw[...] * inverse[:, 0:1], 0.0)
            agg[0] = right_flip(raw[...], input_weights())
        else:
            forward_pass(dims, at, chunks, adj, sent, agg.at[layer], pair, pool, refs["forward"], Hooks(**acts))
            turn = ready.at[next(rounds)]
            announce(dims, at, turn)
            agg[layer] = agg[layer] * inverse[:, 0:1]
        pre_act = direct[...] + plain(agg[layer], mix[layer % 2, 1])
        pre[layer] = pre_act
        _, act, scale = activation(pre_act)
        after = act * scale
        hid[layer + 1] = after
        if layer + 1 < layers:
            sent[:, :width] = after * alpha
        await_all(dims, at, turn)

    def output_weights():
        at_lane = wide_in - width
        return jnp.concatenate(
            [rows_of(every[0], half, head + block // 2, block // 2)[:, at_lane : at_lane + LANES] for half in range(2)], 0
        )

    labelled = jnp.sum(every[0][:, :, :, :, head + block // 2 : head + block // 2 + 8, tail : tail + LANES].reshape(-1, 8, LANES), 0)[0:1, 0:1]
    refs["marks"][...] = jnp.broadcast_to(labelled, refs["marks"].shape)
    head_weights = output_weights()
    logits = plain(hid[layers], head_weights)
    column = lax.broadcasted_iota(jnp.int32, logits.shape, 1)
    soft = jnp.maximum(logits, 0.0) + jnp.log(1.0 + jnp.exp(-jnp.abs(logits)))
    each = jnp.where(column < classes, soft - target * logits, 0.0)
    loss = jnp.sum(weight * jnp.sum(each, -1, keepdims=True), 0, keepdims=True)
    d_logits = jnp.where(column < classes, (weight / labelled) * (jax.nn.sigmoid(logits) - target), 0.0)
    g_out = left_flip(hid[layers], d_logits)
    d_out = right_flip(d_logits, head_weights)
    start = head + block // 2
    half_rows = width // 2
    for half in range(2):
        piece = jnp.concatenate(
            [
                jnp.zeros((half_rows, wide_in - width), f32),
                g_out[half * half_rows : (half + 1) * half_rows],
                jnp.broadcast_to(loss, (half_rows, width - tail)),
            ],
            1,
        )
        put_rows(every[0], half, start, block // 2, piece)

    reduces = [
        ReduceAll(dims, at, every[l], [0, block, head], red, refs["reduce_bufs"], refs["reduce_sems"]) for l in range(layers)
    ]

    def slope(layer, d_out):
        pre_act = pre[layer]
        sig, act, scale = activation(pre_act)
        normed = act * scale
        d_act = scale * (d_out - normed * jnp.mean(d_out * normed, -1, keepdims=True))
        return d_act * sig * (1.0 + pre_act * (1.0 - sig))

    def outers(layer, d_pre):
        outer[0] = left_flip(hid[layer], d_pre)
        outer[1] = left_flip(agg[layer], d_pre)

    def weight_grads(layer, half):
        side = rows_of(every[layer], half, 0, block)
        proj = rows_of(every[layer], half, block, block)
        g_side = right_flip(outer[half], proj)
        g_proj = left_flip(side, outer[half])
        put_rows(every[layer], half, 0, block, g_side)
        put_rows(every[layer], half, block, block, g_proj)

    base = [0, 3 * block, 5 * block]
    sums = refs["sums"]
    sums[...] = jnp.zeros_like(sums)
    spot = lax.broadcasted_iota(jnp.int32, (1, wide_in), 1)
    slot = 2 * layers

    def note_total(index, new_row):
        total = jnp.sum(new_row, 0, keepdims=True)
        sums[slot + 1 : slot + 2] = sums[slot + 1 : slot + 2] + jnp.where(spot == LANES + index, total, 0.0)

    def note_layer(layer):
        for kind, old in enumerate((row_side, row_proj)):
            start = base[layer] + kind * block
            square, new_row = row_statistic(red[start : start + block], column_of(old[layer : layer + 1]), width)
            index = kind * layers + layer
            sums[index : index + 1, :width] = jnp.sum(square, 0, keepdims=True)
            sums[slot + 2 + index : slot + 3 + index, :width] = jnp.sum(square / new_row, 0, keepdims=True)
            note_total(index, new_row)

    def note_head():
        first, second = red[head : head + block // 2], red[head + block // 2 : head + block]
        square = jnp.concatenate([first * first, second[:, : wide_in - width] * second[:, : wide_in - width]], 1)
        new_col = blend(column_of(col_in[...]), jnp.sum(square, 1, keepdims=True) / in_width)
        sums[slot : slot + 1] = jnp.sum(square, 0, keepdims=True)
        sums[2 * slot + 2 : 2 * slot + 3] = jnp.sum(square / new_col, 0, keepdims=True)
        square, new_row = row_statistic(second[:, wide_in - width : tail], column_of(row_out[...]), classes)
        sums[slot + 1 : slot + 2, :LANES] = jnp.sum(square, 0, keepdims=True)
        sums[2 * slot + 3 : 2 * slot + 4, :LANES] = jnp.sum(square / new_row, 0, keepdims=True)
        note_total(slot, new_row)

    def sum_everywhere(stat):
        far, near, across, cores = dims
        p, q, x, c = at
        came_in, out_sems, in_sems = refs["sum_in"], refs["sum_out"], refs["sum_came"]
        groups = [
            [device(dims, p, q, x, 1 - c)],
            [device(dims, p, q, lax.rem(x + step, across), c) for step in range(1, across)],
            [device(dims, p, lax.rem(q + step, near), x, c) for step in range(1, near)],
            [device(dims, *other) for other in line_peers(dims, at)],
        ]
        base_slot = 0
        for turn, group in enumerate(groups):
            for i, target in enumerate(group):
                at_slot = base_slot + i
                send(sums.at[pl.ds(turn * stat.shape[0], stat.shape[0])], came_in.at[at_slot], out_sems.at[at_slot], in_sems.at[at_slot], target)
            total = sums[turn * stat.shape[0] : (turn + 1) * stat.shape[0]]
            for i in range(len(group)):
                at_slot = base_slot + i
                arrived(came_in.at[at_slot], in_sems.at[at_slot])
                total = total + came_in[at_slot]
            base_slot += len(group)
            if turn + 1 < len(groups):
                sums[(turn + 1) * stat.shape[0] : (turn + 2) * stat.shape[0]] = total
            else:
                stat[...] = total
                stat[2 * slot + 4 : 2 * slot + 5, :LANES] = jnp.broadcast_to(refs["marks"][0:1, 0:1], (1, LANES))
        for at_slot in range(base_slot):
            left_source(came_in.at[at_slot], out_sems.at[at_slot])


    def finish_reduce(layer, pieces):
        for j in pieces:
            reduces[layer].last_stage(j, base[layer] + j * block)
        for j in pieces:
            reduces[layer].end(j)
        note_layer(layer)

    d_pre_ref = refs["d_pre"]
    carried, freed = [], []
    for layer in range(layers - 1, 0, -1):
        d_pre_ref[...] = slope(layer, d_out)
        sent[:, :width] = d_pre_ref[...] * inverse[:, 0:1]

        def grads(layer=layer):
            outers(layer, d_pre_ref[...])
            for half in range(2):
                weight_grads(layer, half)
            if freed:
                await_all(dims, at, freed.pop())
            for j in range(2):
                reduces[layer].core_stage(j)

        def direct_part(layer=layer):
            direct[...] = right_flip(d_pre_ref[...], mix[layer % 2, 0])

        def stage(name, layer=layer):
            for j in range(2):
                getattr(reduces[layer], name)(j)

        acts = {
            "chunk0": carried[:1],
            "chunk1": carried[1:] + [direct_part],
            "chunk2": [grads],
            "chunk3": [functools.partial(stage, "across_stage")],
            "early": [functools.partial(mixing, 0)] if layer == 1 else [],
            "line": [functools.partial(stage, "near_stage")],
        }
        backward_pass(dims, at, chunks, adj, sent, back, pair, pool, refs["backward"], Hooks(**acts))
        if layer > 1:
            turn = ready.at[next(rounds)]
            announce(dims, at, turn)
        d_out = direct[...] + right_flip(back[...] * alpha, mix[layer % 2, 1])
        if layer > 1:
            await_all(dims, at, turn)

        def close(layer=layer):
            finish_reduce(layer, range(2))
            freed.append(ready.at[next(rounds)])
            announce(dims, at, freed[0])

        carried = [functools.partial(stage, "line_stage"), close]

    d_pre = slope(0, d_out)
    d_pre_ref[...] = d_pre
    carried[0]()
    d_self = right_flip(d_pre, mix[0, 0])
    d_neigh = right_flip(d_pre, mix[0, 1])
    g_in = left_flip(d_self, feats[...]) + left_flip(d_neigh, raw[...])
    for half in range(2):
        top = slice(half * half_rows, (half + 1) * half_rows)
        put_rows(every[0], half, head, block // 2, g_in[top, :width])
        where = (slice(half * (far // 2), (half + 1) * (far // 2)),) + (slice(None),) * 3
        value = g_in[top, width:]
        every[0][where + (slice(head + block // 2, head + block), slice(0, wide_in - width))] = value.reshape(
            (far // 2, near, across, cores, block // 2, wide_in - width)
        )
    carried[1]()
    await_all(dims, at, freed.pop())
    final = reduces[0]
    final.turned = [near == across, False, False]
    final.core_stage(2)
    outers(0, d_pre)
    weight_grads(0, 0)
    weight_grads(0, 1)
    final.core_stage(0)
    final.core_stage(1)
    final.across_stage(2)
    final.across_stage(0)
    final.across_stage(1)
    final.near_stage(2)
    final.near_stage(0)
    final.near_stage(1)
    final.line_stage(2)
    final.line_stage(0)
    final.line_stage(1)
    finish_reduce(0, (2, 0, 1))
    note_head()
    sum_everywhere(stat)


def update_kernel(in_width, classes, red, stat, w_in_t, w_side, w_proj, w_out, row_in, col_in, row_side, col_side, row_proj, col_proj, row_out, col_out, loss, count, g_in, g_side, g_proj, g_out, n_in, n_side, n_proj, n_out, s_row_in, s_col_in, s_row_side, s_col_side, s_row_proj, s_col_proj, s_row_out, s_col_out):
    layers, block, width = w_side.shape
    head = 2 * block
    wide_in = w_in_t.shape[1]
    tail = wide_in - width + LANES
    slot = 2 * layers
    base = [0, 3 * block, 5 * block]

    def step_of(weight, grad, new_row, new_col, mean, over, size):
        update = grad * lax.rsqrt(new_row * new_col / mean)
        factor = 1.0 / jnp.maximum(1.0, jnp.sqrt(mean * over / size) / clip_level)
        return weight - step_rate * (update * factor)

    def total_of(index):
        return stat[slot + 1 : slot + 2, LANES + index : LANES + index + 1]

    kinds = (
        (w_side, row_side, col_side, g_side, n_side, s_row_side, s_col_side),
        (w_proj, row_proj, col_proj, g_proj, n_proj, s_row_proj, s_col_proj),
    )
    for layer in range(layers):
        for kind, (weight, row, col, g, n, s_row, s_col) in enumerate(kinds):
            start = base[layer] + kind * block
            index = kind * layers + layer
            grad = red[start : start + block]
            _, new_row = row_statistic(grad, column_of(row[layer : layer + 1]), width)
            new_col = blend(col[layer : layer + 1], stat[index : index + 1, :width] / (2 * width))
            over = jnp.sum(stat[slot + 2 + index : slot + 3 + index, :width] / new_col, 1, keepdims=True)
            g[layer] = grad
            n[layer] = step_of(weight[layer], grad, new_row, new_col, total_of(index) / (2 * width), over, 2 * width * width)
            s_row[layer : layer + 1] = row_of(new_row)
            s_col[layer : layer + 1] = new_col
    first, second = red[head : head + block // 2], red[head + block // 2 : head + block]
    grad = jnp.concatenate([first, second[:, : wide_in - width]], 1)[:, :in_width]
    new_col = blend(column_of(col_in[...]), jnp.sum(grad * grad, 1, keepdims=True) / in_width)
    new_row = blend(row_in[...], stat[slot : slot + 1, :in_width] / width)
    mean = jnp.sum(new_row, 1, keepdims=True) / in_width
    over = jnp.sum(stat[2 * slot + 2 : 2 * slot + 3, :in_width] / new_row, 1, keepdims=True)
    g_in[...] = grad
    n_in[...] = step_of(w_in_t[:, :in_width], grad, new_col, new_row, mean, over, in_width * width)
    s_row_in[...] = new_row
    s_col_in[...] = row_of(new_col)
    grad = second[:, wide_in - width : wide_in - width + classes]
    _, new_row = row_statistic(grad, column_of(row_out[...]), classes)
    new_col = blend(col_out[...], stat[slot + 1 : slot + 2, :classes] / width)
    over = jnp.sum(stat[2 * slot + 3 : 2 * slot + 4, :classes] / new_col, 1, keepdims=True)
    g_out[...] = grad
    n_out[...] = step_of(w_out[...], grad, new_row, new_col, total_of(slot) / width, over, width * classes)
    s_row_out[...] = row_of(new_row)
    s_col_out[...] = new_col
    loss[...] = second[0:1, tail : tail + 1]
    count[...] = stat[2 * slot + 4 : 2 * slot + 5, 0:1]


def train_on_device(dims, name_id, in_width, classes, adjacency, feats, info, w_in_t, w_side, w_proj, w_out, col_in, row_side, row_proj, row_out):
    far, near, across, cores = dims
    nodes, wide_in = feats.shape
    layers, block, width = w_side.shape
    in_chunks, chunks = wide_in // LANES, width // LANES
    dma = pltpu.SemaphoreType.DMA
    pool = max(blocks_of(forward_blocks(dims, in_chunks)), blocks_of(backward_blocks(dims, chunks)))
    bufs, sems = reduce_scratch(dims, 3, block, width)
    strip = 128
    stat_rows = 24
    partners = 1 + (across - 1) + (near - 1) + (far - 1)
    vmem = pl.BlockSpec(memory_space=pltpu.VMEM)
    refs = {
        "adj": pltpu.VMEM(adjacency.shape, bf16),
        "stage": pltpu.VMEM((2, strip, adjacency.shape[1]), jnp.int32),
        "stage_sems": dma((2,)),
        "pair": pltpu.VMEM((max(far * near, across * cores) * nodes, 2 * LANES), bf16),
        "pool": pltpu.VMEM((pool, nodes, LANES), f32),
        "sent": pltpu.VMEM((nodes, wide_in), f32),
        "raw": pltpu.VMEM((nodes, wide_in), f32),
        "inverse": pltpu.VMEM((nodes, LANES), f32),
        "mix": pltpu.VMEM((2, 2, width, width), f32),
        "direct": pltpu.VMEM((nodes, width), f32),
        "back": pltpu.VMEM((nodes, width), f32),
        "d_pre": pltpu.VMEM((nodes, width), f32),
        "agg": pltpu.VMEM((layers, nodes, width), f32),
        "hid": pltpu.VMEM((layers + 1, nodes, width), f32),
        "pre": pltpu.VMEM((layers, nodes, width), f32),
        "outer": pltpu.VMEM((2, width, width), f32),
        "ready": pltpu.SemaphoreType.REGULAR((3 * layers - 3,)),
        "forward": forward_sems(dims, in_chunks),
        "backward": backward_sems(dims, chunks),
        "sums": pltpu.VMEM((4 * stat_rows, wide_in), f32),
        "sum_in": pltpu.VMEM((partners, stat_rows, wide_in), f32),
        "sum_out": dma((partners,)),
        "sum_came": dma((partners,)),
        "marks": pltpu.VMEM((8, LANES), f32),
        "reduce_bufs": bufs,
        "reduce_sems": sems,
    }
    for layer in range(layers):
        refs["every%d" % layer] = pltpu.VMEM(dims + ((3 if layer == 0 else 2) * block, width), f32)
        refs["spread%d" % layer] = spread_sems(dims)
    return pl.pallas_call(
        functools.partial(train_kernel, dims, in_width, classes),
        out_shape=(
            jax.ShapeDtypeStruct((7 * block, width), f32),
            jax.ShapeDtypeStruct((stat_rows, wide_in), f32),
        ),
        in_specs=[pl.BlockSpec(memory_space=pl.ANY)] + [vmem] * 10,
        out_specs=(vmem, vmem),
        scratch_shapes=[refs],
        compiler_params=pltpu.CompilerParams(
            collective_id=name_id, has_side_effects=True, vmem_limit_bytes=63 * 2**20
        ),
    )(adjacency, feats, info, w_in_t, w_side, w_proj, w_out, col_in, row_side, row_proj, row_out)


def update_on_device(in_width, classes, *arrays):
    w_side, w_out = arrays[3], arrays[5]
    layers, block, width = w_side.shape
    shapes = [
        (1, 1),
        (1, 1),
        (block // 2, in_width),
        w_side.shape,
        w_side.shape,
        w_out.shape,
        (block // 2, in_width),
        w_side.shape,
        w_side.shape,
        w_out.shape,
        (1, in_width),
        (1, block // 2),
        (layers, block),
        (layers, width),
        (layers, block),
        (layers, width),
        (1, block // 2),
        (1, classes),
    ]
    vmem = pl.BlockSpec(memory_space=pltpu.VMEM)
    return pl.pallas_call(
        functools.partial(update_kernel, in_width, classes),
        out_shape=[jax.ShapeDtypeStruct(shape, f32) for shape in shapes],
        in_specs=[vmem] * len(arrays),
        out_specs=[vmem] * len(shapes),
    )(*arrays)


def dot(left, right, over=((1,), (0,))):
    return lax.dot_general(
        left, right, (over, ((), ())), precision=lax.Precision.HIGH, preferred_element_type=f32
    )


def left_t(left, right):
    return dot(left, right, ((0,), (0,)))


def right_t(left, right):
    return dot(left, right, ((1,), (1,)))


def pad_lanes(value, lanes):
    return jnp.pad(value, ((0, 0), (0, lanes - value.shape[1])))


def fits_on_chip(adjacency):
    return 2 * adjacency.shape[0] * adjacency.shape[1] <= 4 * 2**20


def step_fused(
    dims,
    features,
    adjacency,
    labels,
    labelled,
    node_count,
    w_in,
    w_side,
    w_proj,
    w_out,
    row_in,
    col_in,
    row_side,
    col_side,
    row_proj,
    col_proj,
    row_out,
    col_out,
):
    nodes, in_width = features.shape
    classes = w_out.shape[1]
    wide_in = -(-(in_width + 1) // LANES) * LANES
    counts = node_count.astype(f32)
    mask = labelled.astype(f32)
    lane = lax.broadcasted_iota(jnp.int32, (nodes, LANES), 1)
    facts = jnp.where(
        lane == 0,
        (2.0 / (1.0 + counts))[:, None],
        jnp.where(lane == 1, (mask * lax.rsqrt(counts))[:, None], jnp.where(lane == 2, mask[:, None], 0.0)),
    )
    info = jnp.concatenate([pad_lanes(labels.astype(f32), LANES), facts], 1)
    w_in_t = pad_lanes(w_in.T, wide_in)
    local = (w_in_t, w_side, w_proj, w_out)
    red, stat = train_on_device(
        dims, 1, in_width, classes, adjacency, pad_lanes(features, wide_in), info, *local,
        col_in[None], row_side, row_proj, row_out[None],
    )
    done = update_on_device(
        in_width, classes, red, stat, *local,
        row_in[None], col_in[None], row_side, col_side, row_proj, col_proj, row_out[None], col_out[None],
    )
    (loss, count, g_in, g_side, g_proj, g_out, n_in, n_side, n_proj, n_out,
     s_row_in, s_col_in, s_row_side, s_col_side, s_row_proj, s_col_proj, s_row_out, s_col_out) = done
    return (
        loss[0, 0],
        count[0, 0],
        g_in.T,
        g_side,
        g_proj,
        g_out,
        n_in.T,
        n_side,
        n_proj,
        n_out,
        s_row_in[0],
        s_col_in[0],
        s_row_side,
        s_col_side,
        s_row_proj,
        s_col_proj,
        s_row_out[0],
        s_col_out[0],
    )


def step_apart(
    dims,
    features,
    adjacency,
    labels,
    labelled,
    node_count,
    w_in,
    w_side,
    w_proj,
    w_out,
    row_in,
    col_in,
    row_side,
    col_side,
    row_proj,
    col_proj,
    row_out,
    col_out,
):
    layers = w_side.shape[0]
    width = w_side.shape[2]
    in_width = features.shape[1]
    classes = w_out.shape[1]
    nodes = features.shape[0]
    both = ("wide", "narrow")
    adj = adjacency.astype(bf16)
    counts = node_count.astype(f32)
    alpha = 2.0 / (1.0 + counts)
    lam = lax.rsqrt(counts)
    target = labels.astype(f32)
    weight_mask = labelled.astype(f32)

    spare = -(in_width + 1) % LANES
    sent = jnp.concatenate(
        [alpha[:, None] * features, jnp.ones((nodes, 1), f32), jnp.zeros((nodes, spare), f32)], 1
    )
    summed = aggregate(dims, 1, adj, sent)
    inverse = 1.0 / (1.0 + summed[:, in_width : in_width + 1])
    agg_features = summed[:, :in_width] * inverse

    full_in, full_side, full_proj, full_out = (
        lax.all_gather(w_in, both, axis=1, tiled=True),
        lax.all_gather(w_side, both, axis=1, tiled=True),
        lax.all_gather(w_proj, both, axis=1, tiled=True),
        lax.all_gather(w_out, both, axis=0, tiled=True),
    )
    mix_self = [dot(full_side[l, :width], full_proj[l, :width]) for l in range(layers)]
    mix_neigh = [dot(full_side[l, width:], full_proj[l, width:]) for l in range(layers)]

    kept = []
    hidden = dot(features, full_in)
    agg = dot(agg_features, full_in)
    for layer in range(layers):
        if layer > 0:
            agg = aggregate(dims, 1 + layer, adj, alpha[:, None] * hidden) * inverse
        pre_act = dot(hidden, mix_self[layer]) + dot(agg, mix_neigh[layer])
        kept.append((hidden, agg, pre_act))
        act = jax.nn.silu(pre_act)
        hidden = act * lax.rsqrt(jnp.mean(act * act, -1, keepdims=True) + norm_eps)

    logits = dot(hidden, full_out)
    per = jnp.sum(jax.nn.softplus(logits) - target * logits, -1)
    loss_sum, label_count = lax.psum(
        (jnp.sum(weight_mask * lam * per), jnp.sum(weight_mask)), both
    )
    d_logits = (weight_mask * lam / label_count)[:, None] * (jax.nn.sigmoid(logits) - target)
    g_out = left_t(hidden, d_logits)
    d_out = right_t(d_logits, full_out)
    side_grads = [None] * layers
    proj_grads = [None] * layers
    for layer in reversed(range(layers)):
        hidden, agg, pre_act = kept[layer]
        sig = jax.nn.sigmoid(pre_act)
        act = pre_act * sig
        scale = lax.rsqrt(jnp.mean(act * act, -1, keepdims=True) + norm_eps)
        normed = act * scale
        d_act = scale * (d_out - normed * jnp.mean(d_out * normed, -1, keepdims=True))
        d_pre = d_act * sig * (1.0 + pre_act * (1.0 - sig))
        outer_self = left_t(hidden, d_pre)
        outer_neigh = left_t(agg, d_pre)
        side, proj = full_side[layer], full_proj[layer]
        side_grads[layer] = jnp.concatenate(
            [right_t(outer_self, proj[:width]), right_t(outer_neigh, proj[width:])], 0
        )
        proj_grads[layer] = jnp.concatenate(
            [left_t(side[:width], outer_self), left_t(side[width:], outer_neigh)], 0
        )
        d_self = right_t(d_pre, mix_self[layer])
        if layer > 0:
            back = aggregate(dims, 3 + layer, adj, d_pre * inverse, backward=True)
            d_out = d_self + right_t(alpha[:, None] * back, mix_neigh[layer])
        else:
            g_in = left_t(features, d_self) + left_t(agg_features, right_t(d_pre, mix_neigh[layer]))
    red_in, red_side, red_proj, red_out = (
        lax.psum_scatter(g_in, both, scatter_dimension=1, tiled=True),
        lax.psum_scatter(jnp.stack(side_grads), both, scatter_dimension=1, tiled=True),
        lax.psum_scatter(jnp.stack(proj_grads), both, scatter_dimension=1, tiled=True),
        lax.psum_scatter(g_out, both, scatter_dimension=0, tiled=True),
    )
    sq_in = red_in * red_in
    sq_side = red_side * red_side
    sq_proj = red_proj * red_proj
    sq_out = red_out * red_out
    new_col_in = 0.5 * col_in + 0.5 * (jnp.mean(sq_in, 0) + stat_eps)
    new_row_side = 0.5 * row_side + 0.5 * (jnp.mean(sq_side, 2) + stat_eps)
    new_row_proj = 0.5 * row_proj + 0.5 * (jnp.mean(sq_proj, 2) + stat_eps)
    new_row_out = 0.5 * row_out + 0.5 * (jnp.mean(sq_out, 1) + stat_eps)
    (
        sum_row_in,
        sum_col_side,
        sum_col_proj,
        sum_col_out,
        total_side,
        total_proj,
        total_out,
        over_in,
        over_side,
        over_proj,
        over_out,
    ) = lax.psum(
        (
            jnp.sum(sq_in, 1),
            jnp.sum(sq_side, 1),
            jnp.sum(sq_proj, 1),
            jnp.sum(sq_out, 0),
            jnp.sum(new_row_side, 1),
            jnp.sum(new_row_proj, 1),
            jnp.sum(new_row_out),
            jnp.sum(sq_in / new_col_in[None, :], 1),
            jnp.sum(sq_side / new_row_side[:, :, None], 1),
            jnp.sum(sq_proj / new_row_proj[:, :, None], 1),
            jnp.sum(sq_out / new_row_out[:, None], 0),
        ),
        both,
    )
    new_row_in = 0.5 * row_in + 0.5 * (sum_row_in / width + stat_eps)
    new_col_side = 0.5 * col_side + 0.5 * (sum_col_side / (2 * width) + stat_eps)
    new_col_proj = 0.5 * col_proj + 0.5 * (sum_col_proj / (2 * width) + stat_eps)
    new_col_out = 0.5 * col_out + 0.5 * (sum_col_out / width + stat_eps)
    mean_in = jnp.mean(new_row_in)
    mean_side = total_side / (2 * width)
    mean_proj = total_proj / (2 * width)
    mean_out = total_out / width
    up_in = red_in * lax.rsqrt(new_row_in[:, None] * new_col_in[None, :] / mean_in)
    up_side = red_side * lax.rsqrt(
        new_row_side[:, :, None] * new_col_side[:, None, :] / mean_side[:, None, None]
    )
    up_proj = red_proj * lax.rsqrt(
        new_row_proj[:, :, None] * new_col_proj[:, None, :] / mean_proj[:, None, None]
    )
    up_out = red_out * lax.rsqrt(new_row_out[:, None] * new_col_out[None, :] / mean_out)
    ms_in = mean_in * jnp.sum(over_in / new_row_in) / (in_width * width)
    ms_side = mean_side * jnp.sum(over_side / new_col_side, 1) / (2 * width * width)
    ms_proj = mean_proj * jnp.sum(over_proj / new_col_proj, 1) / (2 * width * width)
    ms_out = mean_out * jnp.sum(over_out / new_col_out) / (width * classes)
    fac_in = 1.0 / jnp.maximum(1.0, jnp.sqrt(ms_in) / clip_level)
    fac_side = 1.0 / jnp.maximum(1.0, jnp.sqrt(ms_side) / clip_level)
    fac_proj = 1.0 / jnp.maximum(1.0, jnp.sqrt(ms_proj) / clip_level)
    fac_out = 1.0 / jnp.maximum(1.0, jnp.sqrt(ms_out) / clip_level)
    new_in = w_in - step_rate * (up_in * fac_in)
    new_side = w_side - step_rate * (up_side * fac_side[:, None, None])
    new_proj = w_proj - step_rate * (up_proj * fac_proj[:, None, None])
    new_out = w_out - step_rate * (up_out * fac_out)
    return (
        loss_sum,
        label_count,
        red_in,
        red_side,
        red_proj,
        red_out,
        new_in,
        new_side,
        new_proj,
        new_out,
        new_row_in,
        new_col_in,
        new_row_side,
        new_col_side,
        new_row_proj,
        new_col_proj,
        new_row_out,
        new_col_out,
    )


def step_on_device(dims, features, adjacency, *others):
    step = step_fused if fits_on_chip(adjacency) else step_apart
    return step(dims, features, adjacency, *others)


def solution(mesh):
    in_specs = (
        P(("wide", "narrow"), None),
        P("wide", "narrow"),
        P(("wide", "narrow"), None),
        P(("wide", "narrow")),
        P(("wide", "narrow")),
        P(None, ("wide", "narrow")),
        P(None, ("wide", "narrow"), None),
        P(None, ("wide", "narrow"), None),
        P(("wide", "narrow"), None),
        P(),
        P(("wide", "narrow")),
        P(None, ("wide", "narrow")),
        P(),
        P(None, ("wide", "narrow")),
        P(),
        P(("wide", "narrow")),
        P(),
    )
    out_specs = (
        P(),
        P(),
        P(None, ("wide", "narrow")),
        P(None, ("wide", "narrow"), None),
        P(None, ("wide", "narrow"), None),
        P(("wide", "narrow"), None),
        P(None, ("wide", "narrow")),
        P(None, ("wide", "narrow"), None),
        P(None, ("wide", "narrow"), None),
        P(("wide", "narrow"), None),
        P(),
        P(("wide", "narrow")),
        P(None, ("wide", "narrow")),
        P(),
        P(None, ("wide", "narrow")),
        P(),
        P(("wide", "narrow")),
        P(),
    )
    shards = functools.partial(step_on_device, grid_of(mesh))
    return jax.shard_map(shards, mesh=mesh, in_specs=in_specs, out_specs=out_specs, check_vma=False)
```

```python
import functools
import jax
import jax.numpy as jnp
from jax import lax
from jax.experimental import pallas as pl
from jax.experimental.pallas import tpu as pltpu
from jax.sharding import PartitionSpec as P

MESH = pl.DeviceIdType.MESH
LANES = 128
CORES = 2
f32 = jnp.float32
bf16 = jnp.bfloat16


norm_eps = 1e-06
stat_eps = 1e-30
clip_level = 0.5
step_rate = 0.04


def grid_of(mesh):
    wide, narrow = mesh.shape["wide"], mesh.shape["narrow"]
    far = 4 if wide % 4 == 0 else wide
    return far, wide // far, narrow // CORES, CORES


def place(dims):
    far, near, across, cores = dims
    wide, narrow = lax.axis_index("wide"), lax.axis_index("narrow")
    return wide // near, lax.rem(wide, near), narrow // cores, lax.rem(narrow, cores)


def device(dims, far_at, near_at, across_at, core_at):
    return (far_at * dims[1] + near_at, across_at * dims[3] + core_at)


def send(src, dst, send_sem, recv_sem, target):
    pltpu.make_async_remote_copy(
        src_ref=src,
        dst_ref=dst,
        send_sem=send_sem,
        recv_sem=recv_sem,
        device_id=target,
        device_id_type=MESH,
    ).start()


def arrived(dst, recv_sem):
    pltpu.make_async_copy(dst, dst, recv_sem).wait()


def left_source(src, send_sem):
    pltpu.make_async_copy(src, src, send_sem).wait()


def halves(value):
    high = value.astype(bf16)
    return high, (value - high.astype(f32)).astype(bf16)


def neighbours(dims, at):
    far, near, across, cores = dims
    p, q, x, c = at
    always = [(p, lax.rem(q + step, near), x, c) for step in range(1, near)]
    always += [(p, q, lax.rem(x + step, across), c) for step in range(1, across)]
    always += [(p, q, x, 1 - c)]
    return always


def line_peers(dims, at):
    far = dims[0]
    p, q, x, c = at
    return [(lax.rem(p + step, far), q, x, c) for step in range(1, far)]


def entry_barrier(dims, at):
    barrier = pltpu.get_barrier_semaphore()
    everyone = neighbours(dims, at) + line_peers(dims, at)
    for other in everyone:
        pl.semaphore_signal(barrier, inc=1, device_id=device(dims, *other), device_id_type=MESH)
    pl.semaphore_wait(barrier, len(everyone))


def chunk(ref, k):
    return ref.at[:, pl.ds(k * LANES, LANES)]


class SpreadAll:
    def __init__(self, dims, at, every, right_out, left_out, near_out, across_out, core_out, came):
        self.dims, self.at, self.every = dims, at, every
        self.right_out, self.left_out, self.near_out = right_out, left_out, near_out
        self.across_out, self.core_out, self.came = across_out, core_out, came

    def away(self, distance):
        far, p = self.dims[0], self.at[0]
        if distance == 0:
            return [(p, None)]
        return [(p - distance, p >= distance), (p + distance, p + distance < far)]

    def when(self, flag, act):
        if flag is None:
            act()
        else:
            pl.when(flag)(act)

    def on_line(self, pp, src):
        far, near, across, cores = self.dims
        p, q, x, c = self.at
        dst = self.every.at[pp, q, x, c]
        sem = self.came.at[pp, q, x, c]

        @pl.when(jnp.logical_and(p < far - 1, pp <= p))
        def _():
            send(src, dst, self.right_out.at[pp], sem, device(self.dims, p + 1, q, x, c))

        @pl.when(jnp.logical_and(p > 0, pp >= p))
        def _():
            send(src, dst, self.left_out.at[pp], sem, device(self.dims, p - 1, q, x, c))

        for step in range(1, near):
            send(src, dst, self.near_out.at[pp, step - 1], sem, device(self.dims, p, lax.rem(q + step, near), x, c))

    def on_plane(self, pp, qq, src):
        far, near, across, cores = self.dims
        p, q, x, c = self.at
        dst, sem = self.every.at[pp, qq, x, c], self.came.at[pp, qq, x, c]
        for step in range(1, across):
            send(src, dst, self.across_out.at[pp, qq, step - 1], sem, device(self.dims, p, q, lax.rem(x + step, across), c))
        self.to_core(pp, qq, x, src)

    def to_core(self, pp, qq, xx, src):
        p, q, x, c = self.at
        send(src, self.every.at[pp, qq, xx, c], self.core_out.at[pp, qq, xx], self.came.at[pp, qq, xx, c], device(self.dims, p, q, x, 1 - c))

    def wait(self, *where):
        arrived(self.every.at[where], self.came.at[where])

    def begin(self):
        p, q, x, c = self.at
        own = self.every.at[p, q, x, c]
        self.on_line(p, own)
        self.on_plane(p, q, own)

    def from_line(self, distance):
        p, q, x, c = self.at
        for pp, flag in self.away(distance):
            def act(pp=pp):
                self.wait(pp, q, x, c)
                self.on_line(pp, self.every.at[pp, q, x, c])
                self.on_plane(pp, q, self.every.at[pp, q, x, c])
            self.when(flag, act)

    def from_near(self, distance):
        far, near, across, cores = self.dims
        p, q, x, c = self.at
        for pp, flag in self.away(distance):
            def act(pp=pp):
                for step in range(1, near):
                    qq = lax.rem(q + step, near)
                    self.wait(pp, qq, x, c)
                    self.on_plane(pp, qq, self.every.at[pp, qq, x, c])
            self.when(flag, act)

    def from_across(self, distance):
        far, near, across, cores = self.dims
        p, q, x, c = self.at
        for pp, flag in self.away(distance):
            def act(pp=pp):
                for qq in range(near):
                    for step in range(1, across):
                        xx = lax.rem(x + step, across)
                        self.wait(pp, qq, xx, c)
                        self.to_core(pp, qq, xx, self.every.at[pp, qq, xx, c])
            self.when(flag, act)

    def step(self, distance):
        self.from_line(distance)
        self.from_near(distance - 1)
        if distance >= 2:
            self.from_across(distance - 2)

    def drain(self):
        far = self.dims[0]
        self.from_near(far - 1)
        if far >= 2:
            self.from_across(far - 2)

    def end(self):
        far, near, across, cores = self.dims
        p, q, x, c = self.at
        self.from_across(far - 1)
        for pp in range(far):
            for qq in range(near):
                for xx in range(across):
                    self.wait(pp, qq, xx, 1 - c)
        for pp in range(far):
            block = self.every.at[pp, q, x, c]

            @pl.when(jnp.logical_and(p < far - 1, pp <= p))
            def _(pp=pp, block=block):
                left_source(block, self.right_out.at[pp])

            @pl.when(jnp.logical_and(p > 0, pp >= p))
            def _(pp=pp, block=block):
                left_source(block, self.left_out.at[pp])

            for step in range(1, near):
                left_source(block, self.near_out.at[pp, step - 1])
            for qq in range(near):
                for step in range(1, across):
                    left_source(block, self.across_out.at[pp, qq, step - 1])
                for xx in range(across):
                    left_source(block, self.core_out.at[pp, qq, xx])


def spread_sems(dims):
    far, near, across, cores = dims
    dma = pltpu.SemaphoreType.DMA
    return [
        dma((far,)),
        dma((far,)),
        dma((far, max(near - 1, 1))),
        dma((far, near, max(across - 1, 1))),
        dma((far, near, across)),
        dma((far, near, across, cores)),
    ]


class Blocks:
    def __init__(self, pool, base, *shape):
        self.pool, self.base, self.shape = pool, base, shape

    @property
    def count(self):
        total = 1
        for size in self.shape:
            total *= size
        return total

    def flat(self, where):
        index = 0
        for size, at in zip(self.shape, where):
            index = index * size + at
        left = 1
        for size in self.shape[len(where) :]:
            left *= size
        return self.base + index * left, left

    def ref(self, *where):
        start, _ = self.flat(where)
        return self.pool.at[start]

    def run(self, *where):
        start, left = self.flat(where)
        return self.pool.at[pl.ds(start, left)]

    def add(self, where, other):
        ref = self.ref(*where)
        ref[...] = ref[...] + other[...]


def take(pool, *shapes):
    base, made = 0, []
    for shape in shapes:
        made.append(Blocks(pool, base, *shape))
        base += made[-1].count
    return made


def forward_blocks(dims, chunks):
    far, near, across, cores = dims
    return (
        (chunks, far, near),
        (chunks, cores, across),
        (chunks, across),
        (chunks, across),
    )


def backward_blocks(dims, chunks):
    far, near, across, cores = dims
    return (
        (chunks, across, cores),
        (chunks, far, near),
        (far, near),
        (chunks, far),
        (near,),
        (chunks,),
        (chunks, far, near),
    )


def blocks_of(shapes):
    total = 0
    for shape in shapes:
        size = 1
        for extent in shape:
            size *= extent
        total += size
    return total


def counted(dims, at):
    p, far = at[0], dims[0]
    ends = jnp.where(p > 0, 1, 0) + jnp.where(p < far - 1, 1, 0)
    return len(neighbours(dims, at)) + ends


def announce(dims, at, sem):
    far = dims[0]
    p, q, x, c = at
    for other in neighbours(dims, at):
        pl.semaphore_signal(sem, inc=1, device_id=device(dims, *other), device_id_type=MESH)

    @pl.when(p > 0)
    def _():
        pl.semaphore_signal(sem, inc=1, device_id=device(dims, p - 1, q, x, c), device_id_type=MESH)

    @pl.when(p < far - 1)
    def _():
        pl.semaphore_signal(sem, inc=1, device_id=device(dims, p + 1, q, x, c), device_id_type=MESH)


def await_all(dims, at, sem):
    pl.semaphore_wait(sem, counted(dims, at))


class Hooks:
    def __init__(self, **acts):
        self.acts = acts

    def run(self, name):
        for act in self.acts.get(name, ()):
            act()


def forward_pass(dims, at, chunks, adj, sent, out, pair, pool, sems, hooks):
    to_right, to_left, to_near, came, core_sems, across_out, across_in = sems
    gathered, part, from_core, from_across = take(pool, *forward_blocks(dims, chunks))
    far, near, across, cores = dims
    p, q, x, c = at
    nodes = sent.shape[0]
    early = chunks - 1
    right, left = device(dims, p + 1, q, x, c), device(dims, p - 1, q, x, c)
    others = [lax.rem(q + step, near) for step in range(1, near)]

    def go_right(k, pp, qq, src):
        @pl.when(p < far - 1)
        def _():
            send(src, gathered.ref(k, pp, qq), to_right.at[k, pp, qq], came.at[k, pp, qq], right)

    def go_left(k, pp, qq, src):
        @pl.when(p > 0)
        def _():
            send(src, gathered.ref(k, pp, qq), to_left.at[k, pp, qq], came.at[k, pp, qq], left)

    def go_near(k, pp, src):
        for step, qq in enumerate(others):
            send(src, gathered.ref(k, pp, q), to_near.at[k, pp, step], came.at[k, pp, q], device(dims, p, qq, x, c))

    hooks.run("begin")
    for k in [early] + list(range(chunks - 1)):
        src = chunk(sent, k)
        go_near(k, p, src)
        go_right(k, p, q, src)
        go_left(k, p, q, src)
    for k in range(chunks):
        gathered.ref(k, p, q)[...] = sent[:, k * LANES : (k + 1) * LANES]
    hooks.run("sent")
    for qq in others:
        arrived(gathered.ref(early, p, qq), came.at[early, p, qq])
        go_right(early, p, qq, gathered.ref(early, p, qq))
        go_left(early, p, qq, gathered.ref(early, p, qq))
    group = near * nodes

    def accumulate(k, pp, fresh):
        high, low = halves(gathered.run(k, pp)[...].reshape(group, LANES))
        pair[:group, :LANES] = high
        pair[:group, LANES:] = low
        columns = pl.ds(pl.multiple_of(pp * group, group), group)

        def product(index, carry):
            cc = lax.rem(index // across + 1 + c, cores)
            xx = lax.rem(index, across)
            rows = pl.multiple_of((xx * cores + cc) * nodes, nodes)
            both = jnp.dot(adj[pl.ds(rows, nodes), columns], pair[:group, :], preferred_element_type=f32)
            both = both[:, :LANES] + both[:, LANES:]
            into = part.ref(k, cc, xx)
            into[...] = both if fresh else into[...] + both
            return carry

        lax.fori_loop(0, cores * across, product, 0)

    def from_near(k, pp):
        if isinstance(k, int) and k == early:
            return

        def act():
            for qq in others:
                arrived(gathered.ref(k, pp, qq), came.at[k, pp, qq])

        if isinstance(k, int):
            act()
        else:
            pl.when(k != early)(act)

    def sides(distance):
        if distance == 0:
            return [(p, p >= 0)]
        return [(p - distance, p >= distance), (p + distance, p + distance < far)]

    def from_line(step, k):
        for pp, flag in sides(step):

            @pl.when(flag)
            def _(pp=pp):
                for qq in [q] + (others if k == early else []):
                    block = gathered.ref(k, pp, qq)
                    arrived(block, came.at[k, pp, qq])

                    @pl.when(pp < p)
                    def _():
                        go_right(k, pp, qq, block)

                    @pl.when(pp > p)
                    def _():
                        go_left(k, pp, qq, block)

                if k != early:
                    go_near(k, pp, gathered.ref(k, pp, q))

    def take_in(k, distance):
        for pp, flag in sides(distance):

            @pl.when(flag)
            def _(pp=pp):
                from_near(k, pp)
                accumulate(k, pp, distance == 0)

    def every_chunk(distance):
        def act(k, carry):
            take_in(k, distance)
            return carry

        lax.fori_loop(0, chunks, act, 0)

    def reduce_across(k):
        arrived(from_core.run(k), core_sems.at[1, k])
        for step in range(1, across):
            xx = lax.rem(x + step, across)
            part.add((k, c, xx), from_core.ref(k, xx))
            send(part.ref(k, c, xx), from_across.ref(k, x), across_out.at[k, xx], across_in.at[k, x], device(dims, p, q, xx, c))

    def finish(k):
        total = part.ref(k, c, x)[...] + from_core.ref(k, x)[...]
        for step in range(1, across):
            xx = lax.rem(x + step, across)
            arrived(from_across.ref(k, xx), across_in.at[k, xx])
            total = total + from_across.ref(k, xx)[...]
        out[:, k * LANES : (k + 1) * LANES] = total

    def complete(k):
        take_in(k, last)
        send(part.run(k, 1 - c), from_core.run(k), core_sems.at[0, k], core_sems.at[1, k], device(dims, p, q, x, 1 - c))

    last = far - 1
    for step in range(1, last):
        hooks.run("step%d" % step)
        for k in range(chunks):
            from_line(step, k)
        every_chunk(step - 1)
    hooks.run("step%d" % last)
    for k in range(chunks):
        from_line(last, k)
        take_in(k, last - 1)
        if k >= 1:
            complete(k - 1)
        if k >= 2:
            reduce_across(k - 2)
        if k >= 3:
            finish(k - 3)
    hooks.run("drain")
    complete(chunks - 1)
    if chunks >= 2:
        reduce_across(chunks - 2)
    if chunks >= 3:
        finish(chunks - 3)
    hooks.run("product")
    reduce_across(chunks - 1)
    if chunks >= 2:
        finish(chunks - 2)
    hooks.run("shadow")
    finish(chunks - 1)
    hooks.run("last")

    for k in range(chunks):
        left_source(part.run(k, 1 - c), core_sems.at[0, k])
        for step in range(1, across):
            xx = lax.rem(x + step, across)
            left_source(part.ref(k, c, xx), across_out.at[k, xx])
        for pp in range(far):
            for qq in [q] + (others if k == early else []):
                block = gathered.ref(k, pp, qq)

                @pl.when(jnp.logical_and(p < far - 1, pp <= p))
                def _(k=k, pp=pp, qq=qq, block=block):
                    left_source(block, to_right.at[k, pp, qq])

                @pl.when(jnp.logical_and(p > 0, pp >= p))
                def _(k=k, pp=pp, qq=qq, block=block):
                    left_source(block, to_left.at[k, pp, qq])

            def near_sent(k=k, pp=pp):
                for step in range(near - 1):
                    left_source(gathered.ref(k, pp, q), to_near.at[k, pp, step])

            if k == early:
                pl.when(pp == p)(near_sent)
            else:
                near_sent()


def forward_sems(dims, chunks):
    far, near, across, cores = dims
    dma = pltpu.SemaphoreType.DMA
    return [dma((chunks, far, near))] * 4 + [dma((2, chunks)), dma((chunks, across)), dma((chunks, across))]


def backward_pass(dims, at, chunks, adj, sent, out, pair, pool, sems, hooks):
    row_out, row_in, near_out, near_in, right_out, left_out, left_in, right_in = sems
    rows, part, line_early, line_rest, right_early, right_rest, from_near = take(
        pool, *backward_blocks(dims, chunks)
    )
    far, near, across, cores = dims
    p, q, x, c = at
    nodes = sent.shape[0]
    total_rows = across * cores * nodes
    early = 0
    right, left = device(dims, p + 1, q, x, c), device(dims, p - 1, q, x, c)
    others = [lax.rem(q + step, near) for step in range(1, near)]
    crossing = [lax.rem(x + step, across) for step in range(1, across)]

    def on_line(k, pp, qq):
        return line_early.ref(pp, qq) if k == early else line_rest.ref(k, pp)

    def from_right_own(k, qq):
        return right_early.ref(qq) if k == early else right_rest.ref(k)

    for k in range(chunks):
        src = chunk(sent, k)
        for xx in crossing:
            send(src, rows.ref(k, x, c), row_out.at[k, xx], row_in.at[k, x, c], device(dims, p, q, xx, c))
        send(src, rows.ref(k, x, c), row_out.at[k, across + x], row_in.at[k, x, c], device(dims, p, q, x, 1 - c))
    for k in range(chunks):
        rows.ref(k, x, c)[...] = sent[:, k * LANES : (k + 1) * LANES]
    hooks.run("sent")

    def dest(i):
        rights = far - 1 - p
        low = jnp.where(i < rights, far - 1 - i, jnp.where(i < far - 1, i - rights, p))
        high = jnp.where(i < p, i, jnp.where(i < far - 1, far - 1 - (i - p), p))
        return jnp.where(p < far // 2, low, high)

    def along(k, pp, qq):
        @pl.when(pp > p)
        def _():
            @pl.when(p > 0)
            def _():
                arrived(on_line(k, pp, qq), left_in.at[k, pp, qq])
                part.add((k, pp, qq), on_line(k, pp, qq))

            send(part.ref(k, pp, qq), on_line(k, pp, qq), right_out.at[k, pp, qq], left_in.at[k, pp, qq], right)

        @pl.when(pp < p)
        def _():
            @pl.when(p < far - 1)
            def _():
                arrived(on_line(k, pp, qq), right_in.at[k, pp, qq])
                part.add((k, pp, qq), on_line(k, pp, qq))

            @pl.when(pp < p - 1)
            def _():
                send(part.ref(k, pp, qq), on_line(k, pp, qq), left_out.at[k, pp, qq], right_in.at[k, pp, qq], left)

            @pl.when(pp == p - 1)
            def _():
                send(part.ref(k, pp, qq), from_right_own(k, qq), left_out.at[k, pp, qq], right_in.at[k, pp, qq], left)

    def settle(k, qq):
        @pl.when(p > 0)
        def _():
            arrived(on_line(k, p, qq), left_in.at[k, p, qq])
            part.add((k, p, qq), on_line(k, p, qq))

        @pl.when(p < far - 1)
        def _():
            arrived(from_right_own(k, qq), right_in.at[k, p, qq])
            part.add((k, p, qq), from_right_own(k, qq))

    def line(k):
        def step(i, carry):
            pp = dest(i)
            if k == early:
                for qq in others + [q]:
                    along(k, pp, qq)
            else:
                for qq in others:
                    arrived(from_near.ref(k, pp, qq), near_in.at[k, pp, qq])
                    part.add((k, pp, q), from_near.ref(k, pp, qq))
                along(k, pp, q)
            return carry

        lax.fori_loop(0, far, step, 0)

    def early_end():
        for step, qq in enumerate(others):
            settle(early, qq)
            send(part.ref(early, p, qq), from_near.ref(early, p, q), near_out.at[early, p, step], near_in.at[early, p, q], device(dims, p, qq, x, c))

    for k in range(chunks):
        for xx in crossing:
            arrived(rows.ref(k, xx, c), row_in.at[k, xx, c])
            send(rows.ref(k, xx, c), rows.ref(k, xx, c), row_out.at[k, across + xx], row_in.at[k, xx, c], device(dims, p, q, x, 1 - c))
        for xx in range(across):
            arrived(rows.ref(k, xx, 1 - c), row_in.at[k, xx, 1 - c])
        high, low = halves(rows.run(k)[...].reshape(total_rows, LANES))
        pair[:total_rows, :LANES] = high
        pair[:total_rows, LANES:] = low

        def product(i, carry, k=k):
            pp = dest(i // near)
            qq = lax.rem(q + 1 + lax.rem(i, near), near)
            start = pl.multiple_of((pp * near + qq) * nodes, nodes)
            both = lax.dot_general(adj[:, pl.ds(start, nodes)], pair[:total_rows, :], (((0,), (0,)), ((), ())), preferred_element_type=f32)
            part.ref(k, pp, qq)[...] = both[:, :LANES] + both[:, LANES:]
            if k != early:
                @pl.when(qq != q)
                def _():
                    send(part.ref(k, pp, qq), from_near.ref(k, pp, q), near_out.at[k, pp, lax.rem(qq - q - 1 + near, near)], near_in.at[k, pp, q], device(dims, p, qq, x, c))

            return carry

        lax.fori_loop(0, far * near, product, 0)
        if k >= 1:
            line(k - 1)
        hooks.run("chunk%d" % k)
    early_end()
    hooks.run("early")
    line(chunks - 1)
    hooks.run("line")
    for k in range(chunks):
        settle(k, q)
        total = part.ref(k, p, q)[...]
        if k == early:
            for qq in others:
                arrived(from_near.ref(k, p, qq), near_in.at[k, p, qq])
                total = total + from_near.ref(k, p, qq)[...]
        out[:, k * LANES : (k + 1) * LANES] = total

    for k in range(chunks):
        for xx in crossing:
            left_source(rows.ref(k, x, c), row_out.at[k, xx])
        for xx in range(across):
            left_source(rows.ref(k, xx, c), row_out.at[k, across + xx])
        for pp in range(far):
            for qq in [q] + (others if k == early else []):
                @pl.when(pp > p)
                def _(k=k, pp=pp, qq=qq):
                    left_source(part.ref(k, pp, qq), right_out.at[k, pp, qq])

                @pl.when(pp < p)
                def _(k=k, pp=pp, qq=qq):
                    left_source(part.ref(k, pp, qq), left_out.at[k, pp, qq])

            def near_sent(k=k, pp=pp):
                for step in range(near - 1):
                    left_source(part.ref(k, pp, q), near_out.at[k, pp, step])

            if k == early:
                pl.when(pp == p)(near_sent)
            else:
                near_sent()


def backward_sems(dims, chunks):
    far, near, across, cores = dims
    dma = pltpu.SemaphoreType.DMA
    return [dma((chunks, 2 * across)), dma((chunks, across, cores))] + [dma((chunks, far, near))] * 6


class Part:
    def __init__(self, index, piece, offset, depth, own_row, out_row, turned):
        self.index, self.piece, self.offset, self.depth = index, piece, offset, depth
        self.own_row, self.out_row, self.turned = own_row, out_row, turned


class ReduceAll:
    def __init__(self, dims, at, own, out, bufs, sems):
        self.dims, self.at, self.own, self.out = dims, at, own, out
        self.halfway, self.first_buf, self.next_buf, self.left_buf, self.right_buf = bufs
        self.core_sems, self.first_out, self.first_in, self.next_out, self.next_in = sems[:5]
        self.right_out, self.left_out, self.left_in, self.right_in = sems[5:]

    def own_rows(self, part):
        return pl.ds(part.own_row, part.depth)

    def half(self, part, *where):
        lead = (part.piece,) + where + (slice(None),) * (3 - len(where))
        return self.halfway.at[lead + (pl.ds(part.offset, part.depth),)]

    def from_first(self, part, i):
        return self.first_buf.at[part.piece, i, :, :, pl.ds(part.offset, part.depth)]

    def from_next(self, part, i):
        return self.next_buf.at[part.piece, i, :, pl.ds(part.offset, part.depth)]

    def from_left(self, part, pp):
        return self.left_buf.at[part.piece, pp, pl.ds(part.offset, part.depth)]

    def from_right(self, part, pp):
        return self.right_buf.at[part.piece, pp, pl.ds(part.offset, part.depth)]

    def add(self, ref, other):
        ref[...] = ref[...] + other[...]

    def peers(self, turned):
        far, near, across, cores = self.dims
        p, q, x, c = self.at
        if turned:
            return [(lax.rem(q + step, near), device(self.dims, p, lax.rem(q + step, near), x, c)) for step in range(1, near)]
        return [(lax.rem(x + step, across), device(self.dims, p, q, lax.rem(x + step, across), c)) for step in range(1, across)]

    def core_stage(self, part):
        p, q, x, c = self.at
        send(self.own.at[:, :, :, 1 - c, self.own_rows(part)], self.half(part), self.core_sems.at[0, part.index], self.core_sems.at[1, part.index], device(self.dims, p, q, x, 1 - c))

    def across_stage(self, part):
        p, q, x, c = self.at
        arrived(self.half(part), self.core_sems.at[1, part.index])
        self.add(self.half(part), self.own.at[:, :, :, c, self.own_rows(part)])
        for i, (other, target) in enumerate(self.peers(part.turned)):
            src = self.half(part, slice(None), other) if part.turned else self.half(part, slice(None), slice(None), other)
            send(src, self.from_first(part, i), self.first_out.at[part.index, i], self.first_in.at[part.index, i], target)

    def near_stage(self, part):
        p, q, x, c = self.at
        mine = self.half(part, slice(None), q) if part.turned else self.half(part, slice(None), slice(None), x)
        for i, _ in enumerate(self.peers(part.turned)):
            arrived(self.from_first(part, i), self.first_in.at[part.index, i])
            self.add(mine, self.from_first(part, i))
        for i, (other, target) in enumerate(self.peers(not part.turned)):
            src = self.half(part, slice(None), q, other) if part.turned else self.half(part, slice(None), other, x)
            send(src, self.from_next(part, i), self.next_out.at[part.index, i], self.next_in.at[part.index, i], target)

    def line_stage(self, part):
        far, near, across, cores = self.dims
        p, q, x, c = self.at
        for i, _ in enumerate(self.peers(not part.turned)):
            arrived(self.from_next(part, i), self.next_in.at[part.index, i])
            self.add(self.half(part, slice(None), q, x), self.from_next(part, i))
        for distance in range(far - 1, 0, -1):
            pp = p + distance

            @pl.when(pp < far)
            def _(pp=pp):
                @pl.when(p > 0)
                def _():
                    arrived(self.from_left(part, pp), self.left_in.at[part.index, pp])
                    self.add(self.half(part, pp, q, x), self.from_left(part, pp))

                send(self.half(part, pp, q, x), self.from_left(part, pp), self.right_out.at[part.index, pp], self.left_in.at[part.index, pp], device(self.dims, p + 1, q, x, c))

            pm = p - distance

            @pl.when(pm >= 0)
            def _(pm=pm):
                @pl.when(p < far - 1)
                def _():
                    arrived(self.from_right(part, pm), self.right_in.at[part.index, pm])
                    self.add(self.half(part, pm, q, x), self.from_right(part, pm))

                send(self.half(part, pm, q, x), self.from_right(part, pm), self.left_out.at[part.index, pm], self.right_in.at[part.index, pm], device(self.dims, p - 1, q, x, c))

    def last_stage(self, part):
        far, near, across, cores = self.dims
        p, q, x, c = self.at
        into = self.out.at[pl.ds(part.out_row, part.depth)]
        into[...] = self.half(part, p, q, x)[...]

        @pl.when(p > 0)
        def _():
            arrived(self.from_left(part, p), self.left_in.at[part.index, p])
            self.add(into, self.from_left(part, p))

        @pl.when(p < far - 1)
        def _():
            arrived(self.from_right(part, p), self.right_in.at[part.index, p])
            self.add(into, self.from_right(part, p))

    def end(self, part):
        far, near, across, cores = self.dims
        p, q, x, c = self.at
        left_source(self.half(part), self.core_sems.at[0, part.index])
        for i, _ in enumerate(self.peers(part.turned)):
            left_source(self.from_first(part, i), self.first_out.at[part.index, i])
        for i, _ in enumerate(self.peers(not part.turned)):
            left_source(self.from_next(part, i), self.next_out.at[part.index, i])
        for pp in range(far):
            @pl.when(pp > p)
            def _(pp=pp):
                left_source(self.from_left(part, pp), self.right_out.at[part.index, pp])

            @pl.when(pp < p)
            def _(pp=pp):
                left_source(self.from_right(part, pp), self.left_out.at[part.index, pp])


def reduce_scratch(dims, pieces, parts, depth, width):
    far, near, across, cores = dims
    dma = pltpu.SemaphoreType.DMA
    bufs = [
        pltpu.VMEM((pieces, far, near, across, depth, width), f32),
        pltpu.VMEM((pieces, max(across - 1, 1), far, near, depth, width), f32),
        pltpu.VMEM((pieces, max(near - 1, 1), far, depth, width), f32),
        pltpu.VMEM((pieces, far, depth, width), f32),
        pltpu.VMEM((pieces, far, depth, width), f32),
    ]
    sems = [
        dma((2, parts)),
        dma((parts, max(across - 1, 1))),
        dma((parts, max(across - 1, 1))),
        dma((parts, max(near - 1, 1))),
        dma((parts, max(near - 1, 1))),
    ] + [dma((parts, far))] * 4
    return bufs, sems


def forward_kernel(dims, chunks, adj, sent, out, pair, pool, *sems):
    at = place(dims)
    entry_barrier(dims, at)
    forward_pass(dims, at, chunks, adj, sent, out, pair, pool, sems, Hooks())


def backward_kernel(dims, chunks, adj, sent, out, pair, pool, *sems):
    at = place(dims)
    entry_barrier(dims, at)
    backward_pass(dims, at, chunks, adj, sent, out, pair, pool, sems, Hooks())


def aggregate(dims, name_id, adj, sent, backward=False):
    far, near, across, cores = dims
    nodes, width = sent.shape
    chunks = width // LANES
    kernel = backward_kernel if backward else forward_kernel
    blocks = backward_blocks if backward else forward_blocks
    sems = backward_sems if backward else forward_sems
    depth = (across * cores if backward else far * near) * nodes
    return pl.pallas_call(
        functools.partial(kernel, dims, chunks),
        out_shape=jax.ShapeDtypeStruct((nodes, width), f32),
        in_specs=[pl.BlockSpec(memory_space=pltpu.VMEM)] * 2,
        out_specs=pl.BlockSpec(memory_space=pltpu.VMEM),
        scratch_shapes=[
            pltpu.VMEM((depth, 2 * LANES), bf16),
            pltpu.VMEM((blocks_of(blocks(dims, chunks)), nodes, LANES), f32),
        ]
        + sems(dims, chunks),
        compiler_params=pltpu.CompilerParams(
            collective_id=name_id, has_side_effects=True, vmem_limit_bytes=60 * 2**20
        ),
    )(adj, sent)


def contract(left, right, over):
    first, second = halves(left), halves(right)

    def go(a, b):
        return lax.dot_general(a, b, (over, ((), ())), preferred_element_type=f32)

    return go(first[0], second[0]) + (go(first[0], second[1]) + go(first[1], second[0]))


def plain(left, right):
    return contract(left, right, ((1,), (0,)))


def left_flip(left, right):
    return contract(left, right, ((0,), (0,)))


def right_flip(left, right):
    return contract(left, right, ((1,), (1,)))


def rows_of(every, half, start, size):
    far = every.shape[0]
    value = every[half * (far // 2) : (half + 1) * (far // 2), :, :, :, start : start + size, :]
    return value.reshape(-1, value.shape[-1])


def put_rows(every, half, start, size, value):
    far = every.shape[0]
    shape = (far // 2,) + every.shape[1:4] + (size, value.shape[-1])
    every[half * (far // 2) : (half + 1) * (far // 2), :, :, :, start : start + size, :] = value.reshape(shape)


def activation(pre_act):
    sig = jax.nn.sigmoid(pre_act)
    act = pre_act * sig
    return sig, act, lax.rsqrt(jnp.mean(act * act, -1, keepdims=True) + norm_eps)


def column_of(row):
    size = row.shape[1]
    same = lax.broadcasted_iota(jnp.int32, (size, size), 0) == lax.broadcasted_iota(jnp.int32, (size, size), 1)
    return jnp.sum(jnp.where(same, jnp.broadcast_to(row, (size, size)), 0.0), 1, keepdims=True)


def row_of(column):
    size = column.shape[0]
    same = lax.broadcasted_iota(jnp.int32, (size, size), 0) == lax.broadcasted_iota(jnp.int32, (size, size), 1)
    return jnp.sum(jnp.where(same, jnp.broadcast_to(column, (size, size)), 0.0), 0, keepdims=True)


def blend(old, mean_square):
    return 0.5 * old + 0.5 * (mean_square + stat_eps)


def row_statistic(grad, old, count):
    square = grad * grad
    return square, blend(old, jnp.sum(square, 1, keepdims=True) / count)


def train_kernel(dims, in_width, classes, adj_hbm, feats, info, w_in_t, w_side, w_proj, w_out, col_in, row_side, row_proj, row_out, red, stat, refs):
    far, near, across, cores = dims
    at = place(dims)
    nodes, wide_in = feats.shape
    layers, block, width = w_side.shape
    every = [refs["every%d" % layer] for layer in range(layers)]
    adj, stage, stage_sems = refs["adj"], refs["stage"], refs["stage_sems"]
    pair, pool, sent = refs["pair"], refs["pool"], refs["sent"]
    raw, inverse, mix, direct, back = refs["raw"], refs["inverse"], refs["mix"], refs["direct"], refs["back"]
    agg, hid, pre, outer, ready = refs["agg"], refs["hid"], refs["pre"], refs["outer"], refs["ready"]
    in_chunks, chunks = wide_in // LANES, width // LANES
    head = 2 * block
    tail = wide_in - width + LANES

    strip = stage.shape[1]

    def strip_copy(i):
        return pltpu.make_async_copy(adj_hbm.at[pl.ds(i * strip, strip)], stage.at[i % 2], stage_sems.at[i % 2])

    strips = adj.shape[0] // strip
    strip_copy(0).start()
    strip_copy(1).start()
    for layer in range(layers):
        mine = every[layer].at[at]
        mine[:block] = w_side[layer]
        mine[block : 2 * block] = w_proj[layer]
    mine = every[0].at[at]
    mine[head : head + block // 2] = w_in_t[:, :width]
    mine[head + block // 2 : head + block, : wide_in - width] = w_in_t[:, width:]
    mine[head + block // 2 : head + block, wide_in - width : tail] = jnp.zeros((block // 2, LANES), f32)
    mine[head + block // 2 : head + block, wide_in - width : wide_in - width + classes] = w_out[...]
    marked = jnp.sum(info[:, LANES + 2 : LANES + 3], 0, keepdims=True)
    mine[head + block // 2 : head + block, tail:] = jnp.broadcast_to(marked, (block // 2, width - tail))
    entry_barrier(dims, at)
    target = info[:, :LANES]
    alpha = info[:, LANES : LANES + 1]
    weight = info[:, LANES + 1 : LANES + 2]
    lane = lax.broadcasted_iota(jnp.int32, (nodes, wide_in), 1)
    sent[...] = jnp.where(lane == in_width, 1.0, feats[...] * alpha)

    def load_adjacency():
        for i in range(strips):
            strip_copy(i).wait()
            adj[i * strip : (i + 1) * strip, :] = stage[i % 2].astype(f32).astype(bf16)
            if i + 2 < strips:
                strip_copy(i + 2).start()

    spreads = [SpreadAll(dims, at, every[l], *refs["spread%d" % l]) for l in range(layers)]

    def mixing(layer):
        for half in range(2):
            side = rows_of(every[layer], half, 0, block)
            proj = rows_of(every[layer], half, block, block)
            mix[layer % 2, half] = plain(side, proj)

    def input_weights():
        def both(start):
            return jnp.concatenate([rows_of(every[0], half, start, block // 2) for half in range(2)], 0)

        first, second = both(head), both(head + block // 2)
        return jnp.concatenate([first, second[:, : wide_in - width]], 1)

    def ahead(layer):
        spreads[layer].end()
        mixing(layer)
        if layer == 0:
            hid[0] = right_flip(feats[...], input_weights())
        direct[...] = plain(hid[layer], mix[layer % 2, 0])

    rounds = iter(range(ready.shape[0]))
    for layer in range(layers):
        acts = {}
        if layer == 0:
            for step in range(1, far):
                acts["step%d" % step] = [functools.partial(spreads[0].step, step)]
            acts["begin"] = [spreads[0].begin]
            acts["sent"] = [load_adjacency]
            acts["drain"] = [spreads[0].drain]
            acts["shadow"] = [functools.partial(ahead, 0)]
        else:
            acts["sent"] = [functools.partial(spreads[layer].step, step) for step in range(3, far)]
            acts["step%d" % (far - 1)] = [spreads[layer].drain, functools.partial(ahead, layer)]
        if layer + 1 < layers:
            after = spreads[layer + 1]
            acts["drain"] = acts.get("drain", []) + [after.begin]
            acts["product"] = [functools.partial(after.step, 1)]
            acts["last"] = [functools.partial(after.step, 2)]
        if layer == 0:
            forward_pass(dims, at, in_chunks, adj, sent, raw, pair, pool, refs["forward"], Hooks(**acts))
            turn = ready.at[next(rounds)]
            announce(dims, at, turn)
            inverse[...] = jnp.broadcast_to(1.0 / (1.0 + raw[:, in_width : in_width + 1]), inverse.shape)
            raw[...] = jnp.where(lane < in_width, raw[...] * inverse[:, 0:1], 0.0)
            agg[0] = right_flip(raw[...], input_weights())
        else:
            forward_pass(dims, at, chunks, adj, sent, agg.at[layer], pair, pool, refs["forward"], Hooks(**acts))
            turn = ready.at[next(rounds)]
            announce(dims, at, turn)
            agg[layer] = agg[layer] * inverse[:, 0:1]
        pre_act = direct[...] + plain(agg[layer], mix[layer % 2, 1])
        pre[layer] = pre_act
        _, act, scale = activation(pre_act)
        after = act * scale
        hid[layer + 1] = after
        if layer + 1 < layers:
            sent[:, :width] = after * alpha
        await_all(dims, at, turn)

    def output_weights():
        at_lane = wide_in - width
        return jnp.concatenate(
            [rows_of(every[0], half, head + block // 2, block // 2)[:, at_lane : at_lane + LANES] for half in range(2)], 0
        )

    labelled = jnp.sum(every[0][:, :, :, :, head + block // 2 : head + block // 2 + 8, tail : tail + LANES].reshape(-1, 8, LANES), 0)[0:1, 0:1]
    refs["marks"][...] = jnp.broadcast_to(labelled, refs["marks"].shape)
    head_weights = output_weights()
    logits = plain(hid[layers], head_weights)
    column = lax.broadcasted_iota(jnp.int32, logits.shape, 1)
    soft = jnp.maximum(logits, 0.0) + jnp.log(1.0 + jnp.exp(-jnp.abs(logits)))
    each = jnp.where(column < classes, soft - target * logits, 0.0)
    loss = jnp.sum(weight * jnp.sum(each, -1, keepdims=True), 0, keepdims=True)
    d_logits = jnp.where(column < classes, (weight / labelled) * (jax.nn.sigmoid(logits) - target), 0.0)
    g_out = left_flip(hid[layers], d_logits)
    d_out = right_flip(d_logits, head_weights)
    start = head + block // 2
    half_rows = width // 2
    for half in range(2):
        piece = jnp.concatenate(
            [
                jnp.zeros((half_rows, wide_in - width), f32),
                g_out[half * half_rows : (half + 1) * half_rows],
                jnp.broadcast_to(loss, (half_rows, width - tail)),
            ],
            1,
        )
        put_rows(every[0], half, start, block // 2, piece)

    reduces = [ReduceAll(dims, at, every[l], red, refs["reduce_bufs"], refs["reduce_sems"]) for l in range(layers)]

    def slope(layer, d_out):
        pre_act = pre[layer]
        sig, act, scale = activation(pre_act)
        normed = act * scale
        d_act = scale * (d_out - normed * jnp.mean(d_out * normed, -1, keepdims=True))
        return d_act * sig * (1.0 + pre_act * (1.0 - sig))

    def outers(layer, d_pre):
        outer[0] = left_flip(hid[layer], d_pre)
        outer[1] = left_flip(agg[layer], d_pre)

    def weight_grads(layer, half):
        side = rows_of(every[layer], half, 0, block)
        proj = rows_of(every[layer], half, block, block)
        g_side = right_flip(outer[half], proj)
        g_proj = left_flip(side, outer[half])
        put_rows(every[layer], half, 0, block, g_side)
        put_rows(every[layer], half, block, block, g_proj)

    base = [0, 3 * block, 5 * block]
    sums = refs["sums"]
    sums[...] = jnp.zeros_like(sums)
    spot = lax.broadcasted_iota(jnp.int32, (1, wide_in), 1)
    slot = 2 * layers

    def note_total(index, new_row):
        total = jnp.sum(new_row, 0, keepdims=True)
        sums[slot + 1 : slot + 2] = sums[slot + 1 : slot + 2] + jnp.where(spot == LANES + index, total, 0.0)

    def note_layer(layer):
        for kind, old in enumerate((row_side, row_proj)):
            start = base[layer] + kind * block
            square, new_row = row_statistic(red[start : start + block], column_of(old[layer : layer + 1]), width)
            index = kind * layers + layer
            sums[index : index + 1, :width] = jnp.sum(square, 0, keepdims=True)
            sums[slot + 2 + index : slot + 3 + index, :width] = jnp.sum(square / new_row, 0, keepdims=True)
            note_total(index, new_row)

    def note_head():
        first, second = red[head : head + block // 2], red[head + block // 2 : head + block]
        square = jnp.concatenate([first * first, second[:, : wide_in - width] * second[:, : wide_in - width]], 1)
        new_col = blend(column_of(col_in[...]), jnp.sum(square, 1, keepdims=True) / in_width)
        sums[slot : slot + 1] = jnp.sum(square, 0, keepdims=True)
        sums[2 * slot + 2 : 2 * slot + 3] = jnp.sum(square / new_col, 0, keepdims=True)
        square, new_row = row_statistic(second[:, wide_in - width : tail], column_of(row_out[...]), classes)
        sums[slot + 1 : slot + 2, :LANES] = jnp.sum(square, 0, keepdims=True)
        sums[2 * slot + 3 : 2 * slot + 4, :LANES] = jnp.sum(square / new_row, 0, keepdims=True)
        note_total(slot, new_row)

    def sum_everywhere(stat):
        far, near, across, cores = dims
        p, q, x, c = at
        came_in, out_sems, in_sems = refs["sum_in"], refs["sum_out"], refs["sum_came"]
        groups = [
            [device(dims, p, q, x, 1 - c)],
            [device(dims, p, q, lax.rem(x + step, across), c) for step in range(1, across)],
            [device(dims, p, lax.rem(q + step, near), x, c) for step in range(1, near)],
            [device(dims, *other) for other in line_peers(dims, at)],
        ]
        base_slot = 0
        for turn, group in enumerate(groups):
            for i, target in enumerate(group):
                at_slot = base_slot + i
                send(sums.at[pl.ds(turn * stat.shape[0], stat.shape[0])], came_in.at[at_slot], out_sems.at[at_slot], in_sems.at[at_slot], target)
            total = sums[turn * stat.shape[0] : (turn + 1) * stat.shape[0]]
            for i in range(len(group)):
                at_slot = base_slot + i
                arrived(came_in.at[at_slot], in_sems.at[at_slot])
                total = total + came_in[at_slot]
            base_slot += len(group)
            if turn + 1 < len(groups):
                sums[(turn + 1) * stat.shape[0] : (turn + 2) * stat.shape[0]] = total
            else:
                stat[...] = total
                stat[2 * slot + 4 : 2 * slot + 5, :LANES] = jnp.broadcast_to(refs["marks"][0:1, 0:1], (1, LANES))
        for at_slot in range(base_slot):
            left_source(came_in.at[at_slot], out_sems.at[at_slot])


    def finish_reduce(layer, parts):
        for part in parts:
            reduces[layer].last_stage(part)
        for part in parts:
            reduces[layer].end(part)
        note_layer(layer)

    d_pre_ref = refs["d_pre"]
    carried, freed = [], []
    for layer in range(layers - 1, 0, -1):
        d_pre_ref[...] = slope(layer, d_out)
        sent[:, :width] = d_pre_ref[...] * inverse[:, 0:1]
        first = 2 * ((layers - 1 - layer) % 2)
        parts = [
            Part(first + kind, first + kind, 0, block, kind * block, base[layer] + kind * block, False) for kind in range(2)
        ]

        def begin_grads(layer=layer):
            outers(layer, d_pre_ref[...])
            weight_grads(layer, 0)

        def more_grads(layer=layer, parts=parts):
            weight_grads(layer, 1)
            for part in parts:
                reduces[layer].core_stage(part)

        def direct_part(layer=layer):
            direct[...] = right_flip(d_pre_ref[...], mix[layer % 2, 0])

        def stage(name, layer=layer, parts=parts):
            for part in parts:
                getattr(reduces[layer], name)(part)

        acts = {
            "sent": carried[:1] + [begin_grads],
            "chunk0": carried[1:],
            "chunk1": [more_grads],
            "chunk2": [direct_part, functools.partial(stage, "across_stage")],
            "early": [functools.partial(mixing, 0)] if layer == 1 else [],
            "line": [functools.partial(stage, "near_stage")],
        }
        backward_pass(dims, at, chunks, adj, sent, back, pair, pool, refs["backward"], Hooks(**acts))
        if layer > 1:
            turn = ready.at[next(rounds)]
            announce(dims, at, turn)
        d_out = direct[...] + right_flip(back[...] * alpha, mix[layer % 2, 1])
        if layer > 1:
            await_all(dims, at, turn)

        def close(layer=layer, parts=parts):
            finish_reduce(layer, parts)
            if layer == layers - 1 or layer == 1:
                freed.append(ready.at[next(rounds)])
                announce(dims, at, freed[-1])

        carried = [functools.partial(stage, "line_stage"), close]

    d_pre = slope(0, d_out)
    d_pre_ref[...] = d_pre
    carried[0]()
    d_self = right_flip(d_pre, mix[0, 0])
    d_neigh = right_flip(d_pre, mix[0, 1])
    g_in = left_flip(d_self, feats[...]) + left_flip(d_neigh, raw[...])
    for half in range(2):
        top = slice(half * half_rows, (half + 1) * half_rows)
        put_rows(every[0], half, head, block // 2, g_in[top, :width])
        where = (slice(half * (far // 2), (half + 1) * (far // 2)),) + (slice(None),) * 3
        value = g_in[top, width:]
        every[0][where + (slice(head + block // 2, head + block), slice(0, wide_in - width))] = value.reshape(
            (far // 2, near, across, cores, block // 2, wide_in - width)
        )
    carried[1]()
    for turn in freed:
        await_all(dims, at, turn)
    final = reduces[0]
    depth = block // 2
    order = [
        Part(2 * piece + turned, piece, turned * depth, depth, piece * block + turned * depth, piece * block + turned * depth, turned == 1 and near == across)
        for piece in (2, 0, 1)
        for turned in range(2)
    ]
    for part in order[:2]:
        final.core_stage(part)
    outers(0, d_pre)
    for part in order[:2]:
        final.across_stage(part)
    weight_grads(0, 0)
    for part in order[:2]:
        final.near_stage(part)
    weight_grads(0, 1)
    for part in order[2:]:
        final.core_stage(part)
    for part in order[:2]:
        final.line_stage(part)
    for part in order[2:]:
        final.across_stage(part)
    for part in order[2:]:
        final.near_stage(part)
    for part in order[2:]:
        final.line_stage(part)
    finish_reduce(0, order)
    note_head()
    sum_everywhere(stat)


def update_kernel(in_width, classes, red, stat, w_in_t, w_side, w_proj, w_out, row_in, col_in, row_side, col_side, row_proj, col_proj, row_out, col_out, loss, count, g_in, g_side, g_proj, g_out, n_in, n_side, n_proj, n_out, s_row_in, s_col_in, s_row_side, s_col_side, s_row_proj, s_col_proj, s_row_out, s_col_out):
    layers, block, width = w_side.shape
    head = 2 * block
    wide_in = w_in_t.shape[1]
    tail = wide_in - width + LANES
    slot = 2 * layers
    base = [0, 3 * block, 5 * block]

    def step_of(weight, grad, new_row, new_col, mean, over, size):
        update = grad * lax.rsqrt(new_row * new_col / mean)
        factor = 1.0 / jnp.maximum(1.0, jnp.sqrt(mean * over / size) / clip_level)
        return weight - step_rate * (update * factor)

    def total_of(index):
        return stat[slot + 1 : slot + 2, LANES + index : LANES + index + 1]

    kinds = (
        (w_side, row_side, col_side, g_side, n_side, s_row_side, s_col_side),
        (w_proj, row_proj, col_proj, g_proj, n_proj, s_row_proj, s_col_proj),
    )
    for layer in range(layers):
        for kind, (weight, row, col, g, n, s_row, s_col) in enumerate(kinds):
            start = base[layer] + kind * block
            index = kind * layers + layer
            grad = red[start : start + block]
            _, new_row = row_statistic(grad, column_of(row[layer : layer + 1]), width)
            new_col = blend(col[layer : layer + 1], stat[index : index + 1, :width] / (2 * width))
            over = jnp.sum(stat[slot + 2 + index : slot + 3 + index, :width] / new_col, 1, keepdims=True)
            g[layer] = grad
            n[layer] = step_of(weight[layer], grad, new_row, new_col, total_of(index) / (2 * width), over, 2 * width * width)
            s_row[layer : layer + 1] = row_of(new_row)
            s_col[layer : layer + 1] = new_col
    first, second = red[head : head + block // 2], red[head + block // 2 : head + block]
    grad = jnp.concatenate([first, second[:, : wide_in - width]], 1)[:, :in_width]
    new_col = blend(column_of(col_in[...]), jnp.sum(grad * grad, 1, keepdims=True) / in_width)
    new_row = blend(row_in[...], stat[slot : slot + 1, :in_width] / width)
    mean = jnp.sum(new_row, 1, keepdims=True) / in_width
    over = jnp.sum(stat[2 * slot + 2 : 2 * slot + 3, :in_width] / new_row, 1, keepdims=True)
    g_in[...] = grad
    n_in[...] = step_of(w_in_t[:, :in_width], grad, new_col, new_row, mean, over, in_width * width)
    s_row_in[...] = new_row
    s_col_in[...] = row_of(new_col)
    grad = second[:, wide_in - width : wide_in - width + classes]
    _, new_row = row_statistic(grad, column_of(row_out[...]), classes)
    new_col = blend(col_out[...], stat[slot + 1 : slot + 2, :classes] / width)
    over = jnp.sum(stat[2 * slot + 3 : 2 * slot + 4, :classes] / new_col, 1, keepdims=True)
    g_out[...] = grad
    n_out[...] = step_of(w_out[...], grad, new_row, new_col, total_of(slot) / width, over, width * classes)
    s_row_out[...] = row_of(new_row)
    s_col_out[...] = new_col
    loss[...] = second[0:1, tail : tail + 1]
    count[...] = stat[2 * slot + 4 : 2 * slot + 5, 0:1]


def train_on_device(dims, name_id, in_width, classes, adjacency, feats, info, w_in_t, w_side, w_proj, w_out, col_in, row_side, row_proj, row_out):
    far, near, across, cores = dims
    nodes, wide_in = feats.shape
    layers, block, width = w_side.shape
    in_chunks, chunks = wide_in // LANES, width // LANES
    dma = pltpu.SemaphoreType.DMA
    pool = max(blocks_of(forward_blocks(dims, in_chunks)), blocks_of(backward_blocks(dims, chunks)))
    bufs, sems = reduce_scratch(dims, 4, 6, block, width)
    strip = 128
    stat_rows = 24
    partners = 1 + (across - 1) + (near - 1) + (far - 1)
    vmem = pl.BlockSpec(memory_space=pltpu.VMEM)
    refs = {
        "adj": pltpu.VMEM(adjacency.shape, bf16),
        "stage": pltpu.VMEM((2, strip, adjacency.shape[1]), jnp.int32),
        "stage_sems": dma((2,)),
        "pair": pltpu.VMEM((max(far * near, across * cores) * nodes, 2 * LANES), bf16),
        "pool": pltpu.VMEM((pool, nodes, LANES), f32),
        "sent": pltpu.VMEM((nodes, wide_in), f32),
        "raw": pltpu.VMEM((nodes, wide_in), f32),
        "inverse": pltpu.VMEM((nodes, LANES), f32),
        "mix": pltpu.VMEM((2, 2, width, width), f32),
        "direct": pltpu.VMEM((nodes, width), f32),
        "back": pltpu.VMEM((nodes, width), f32),
        "d_pre": pltpu.VMEM((nodes, width), f32),
        "agg": pltpu.VMEM((layers, nodes, width), f32),
        "hid": pltpu.VMEM((layers + 1, nodes, width), f32),
        "pre": pltpu.VMEM((layers, nodes, width), f32),
        "outer": pltpu.VMEM((2, width, width), f32),
        "ready": pltpu.SemaphoreType.REGULAR((3 * layers - 3,)),
        "forward": forward_sems(dims, in_chunks),
        "backward": backward_sems(dims, chunks),
        "sums": pltpu.VMEM((4 * stat_rows, wide_in), f32),
        "sum_in": pltpu.VMEM((partners, stat_rows, wide_in), f32),
        "sum_out": dma((partners,)),
        "sum_came": dma((partners,)),
        "marks": pltpu.VMEM((8, LANES), f32),
        "reduce_bufs": bufs,
        "reduce_sems": sems,
    }
    for layer in range(layers):
        refs["every%d" % layer] = pltpu.VMEM(dims + ((3 if layer == 0 else 2) * block, width), f32)
        refs["spread%d" % layer] = spread_sems(dims)
    return pl.pallas_call(
        functools.partial(train_kernel, dims, in_width, classes),
        out_shape=(
            jax.ShapeDtypeStruct((7 * block, width), f32),
            jax.ShapeDtypeStruct((stat_rows, wide_in), f32),
        ),
        in_specs=[pl.BlockSpec(memory_space=pl.ANY)] + [vmem] * 10,
        out_specs=(vmem, vmem),
        scratch_shapes=[refs],
        compiler_params=pltpu.CompilerParams(
            collective_id=name_id, has_side_effects=True, vmem_limit_bytes=63 * 2**20
        ),
    )(adjacency, feats, info, w_in_t, w_side, w_proj, w_out, col_in, row_side, row_proj, row_out)


def update_on_device(in_width, classes, *arrays):
    w_side, w_out = arrays[3], arrays[5]
    layers, block, width = w_side.shape
    shapes = [
        (1, 1),
        (1, 1),
        (block // 2, in_width),
        w_side.shape,
        w_side.shape,
        w_out.shape,
        (block // 2, in_width),
        w_side.shape,
        w_side.shape,
        w_out.shape,
        (1, in_width),
        (1, block // 2),
        (layers, block),
        (layers, width),
        (layers, block),
        (layers, width),
        (1, block // 2),
        (1, classes),
    ]
    vmem = pl.BlockSpec(memory_space=pltpu.VMEM)
    return pl.pallas_call(
        functools.partial(update_kernel, in_width, classes),
        out_shape=[jax.ShapeDtypeStruct(shape, f32) for shape in shapes],
        in_specs=[vmem] * len(arrays),
        out_specs=[vmem] * len(shapes),
    )(*arrays)


def dot(left, right, over=((1,), (0,))):
    return lax.dot_general(
        left, right, (over, ((), ())), precision=lax.Precision.HIGH, preferred_element_type=f32
    )


def left_t(left, right):
    return dot(left, right, ((0,), (0,)))


def right_t(left, right):
    return dot(left, right, ((1,), (1,)))


def pad_lanes(value, lanes):
    return jnp.pad(value, ((0, 0), (0, lanes - value.shape[1])))


def fits_on_chip(adjacency):
    return 2 * adjacency.shape[0] * adjacency.shape[1] <= 4 * 2**20


def step_fused(
    dims,
    features,
    adjacency,
    labels,
    labelled,
    node_count,
    w_in,
    w_side,
    w_proj,
    w_out,
    row_in,
    col_in,
    row_side,
    col_side,
    row_proj,
    col_proj,
    row_out,
    col_out,
):
    nodes, in_width = features.shape
    classes = w_out.shape[1]
    wide_in = -(-(in_width + 1) // LANES) * LANES
    counts = node_count.astype(f32)
    mask = labelled.astype(f32)
    lane = lax.broadcasted_iota(jnp.int32, (nodes, LANES), 1)
    facts = jnp.where(
        lane == 0,
        (2.0 / (1.0 + counts))[:, None],
        jnp.where(lane == 1, (mask * lax.rsqrt(counts))[:, None], jnp.where(lane == 2, mask[:, None], 0.0)),
    )
    info = jnp.concatenate([pad_lanes(labels.astype(f32), LANES), facts], 1)
    w_in_t = pad_lanes(w_in.T, wide_in)
    local = (w_in_t, w_side, w_proj, w_out)
    red, stat = train_on_device(
        dims, 1, in_width, classes, adjacency, pad_lanes(features, wide_in), info, *local,
        col_in[None], row_side, row_proj, row_out[None],
    )
    done = update_on_device(
        in_width, classes, red, stat, *local,
        row_in[None], col_in[None], row_side, col_side, row_proj, col_proj, row_out[None], col_out[None],
    )
    (loss, count, g_in, g_side, g_proj, g_out, n_in, n_side, n_proj, n_out,
     s_row_in, s_col_in, s_row_side, s_col_side, s_row_proj, s_col_proj, s_row_out, s_col_out) = done
    return (
        loss[0, 0],
        count[0, 0],
        g_in.T,
        g_side,
        g_proj,
        g_out,
        n_in.T,
        n_side,
        n_proj,
        n_out,
        s_row_in[0],
        s_col_in[0],
        s_row_side,
        s_col_side,
        s_row_proj,
        s_col_proj,
        s_row_out[0],
        s_col_out[0],
    )


def step_apart(
    dims,
    features,
    adjacency,
    labels,
    labelled,
    node_count,
    w_in,
    w_side,
    w_proj,
    w_out,
    row_in,
    col_in,
    row_side,
    col_side,
    row_proj,
    col_proj,
    row_out,
    col_out,
):
    layers = w_side.shape[0]
    width = w_side.shape[2]
    in_width = features.shape[1]
    classes = w_out.shape[1]
    nodes = features.shape[0]
    both = ("wide", "narrow")
    adj = adjacency.astype(bf16)
    counts = node_count.astype(f32)
    alpha = 2.0 / (1.0 + counts)
    lam = lax.rsqrt(counts)
    target = labels.astype(f32)
    weight_mask = labelled.astype(f32)

    spare = -(in_width + 1) % LANES
    sent = jnp.concatenate(
        [alpha[:, None] * features, jnp.ones((nodes, 1), f32), jnp.zeros((nodes, spare), f32)], 1
    )
    summed = aggregate(dims, 1, adj, sent)
    inverse = 1.0 / (1.0 + summed[:, in_width : in_width + 1])
    agg_features = summed[:, :in_width] * inverse

    full_in, full_side, full_proj, full_out = (
        lax.all_gather(w_in, both, axis=1, tiled=True),
        lax.all_gather(w_side, both, axis=1, tiled=True),
        lax.all_gather(w_proj, both, axis=1, tiled=True),
        lax.all_gather(w_out, both, axis=0, tiled=True),
    )
    mix_self = [dot(full_side[l, :width], full_proj[l, :width]) for l in range(layers)]
    mix_neigh = [dot(full_side[l, width:], full_proj[l, width:]) for l in range(layers)]

    kept = []
    hidden = dot(features, full_in)
    agg = dot(agg_features, full_in)
    for layer in range(layers):
        if layer > 0:
            agg = aggregate(dims, 1 + layer, adj, alpha[:, None] * hidden) * inverse
        pre_act = dot(hidden, mix_self[layer]) + dot(agg, mix_neigh[layer])
        kept.append((hidden, agg, pre_act))
        act = jax.nn.silu(pre_act)
        hidden = act * lax.rsqrt(jnp.mean(act * act, -1, keepdims=True) + norm_eps)

    logits = dot(hidden, full_out)
    per = jnp.sum(jax.nn.softplus(logits) - target * logits, -1)
    loss_sum, label_count = lax.psum(
        (jnp.sum(weight_mask * lam * per), jnp.sum(weight_mask)), both
    )
    d_logits = (weight_mask * lam / label_count)[:, None] * (jax.nn.sigmoid(logits) - target)
    g_out = left_t(hidden, d_logits)
    d_out = right_t(d_logits, full_out)
    side_grads = [None] * layers
    proj_grads = [None] * layers
    for layer in reversed(range(layers)):
        hidden, agg, pre_act = kept[layer]
        sig = jax.nn.sigmoid(pre_act)
        act = pre_act * sig
        scale = lax.rsqrt(jnp.mean(act * act, -1, keepdims=True) + norm_eps)
        normed = act * scale
        d_act = scale * (d_out - normed * jnp.mean(d_out * normed, -1, keepdims=True))
        d_pre = d_act * sig * (1.0 + pre_act * (1.0 - sig))
        outer_self = left_t(hidden, d_pre)
        outer_neigh = left_t(agg, d_pre)
        side, proj = full_side[layer], full_proj[layer]
        side_grads[layer] = jnp.concatenate(
            [right_t(outer_self, proj[:width]), right_t(outer_neigh, proj[width:])], 0
        )
        proj_grads[layer] = jnp.concatenate(
            [left_t(side[:width], outer_self), left_t(side[width:], outer_neigh)], 0
        )
        d_self = right_t(d_pre, mix_self[layer])
        if layer > 0:
            back = aggregate(dims, 3 + layer, adj, d_pre * inverse, backward=True)
            d_out = d_self + right_t(alpha[:, None] * back, mix_neigh[layer])
        else:
            g_in = left_t(features, d_self) + left_t(agg_features, right_t(d_pre, mix_neigh[layer]))
    red_in, red_side, red_proj, red_out = (
        lax.psum_scatter(g_in, both, scatter_dimension=1, tiled=True),
        lax.psum_scatter(jnp.stack(side_grads), both, scatter_dimension=1, tiled=True),
        lax.psum_scatter(jnp.stack(proj_grads), both, scatter_dimension=1, tiled=True),
        lax.psum_scatter(g_out, both, scatter_dimension=0, tiled=True),
    )
    sq_in = red_in * red_in
    sq_side = red_side * red_side
    sq_proj = red_proj * red_proj
    sq_out = red_out * red_out
    new_col_in = 0.5 * col_in + 0.5 * (jnp.mean(sq_in, 0) + stat_eps)
    new_row_side = 0.5 * row_side + 0.5 * (jnp.mean(sq_side, 2) + stat_eps)
    new_row_proj = 0.5 * row_proj + 0.5 * (jnp.mean(sq_proj, 2) + stat_eps)
    new_row_out = 0.5 * row_out + 0.5 * (jnp.mean(sq_out, 1) + stat_eps)
    (
        sum_row_in,
        sum_col_side,
        sum_col_proj,
        sum_col_out,
        total_side,
        total_proj,
        total_out,
        over_in,
        over_side,
        over_proj,
        over_out,
    ) = lax.psum(
        (
            jnp.sum(sq_in, 1),
            jnp.sum(sq_side, 1),
            jnp.sum(sq_proj, 1),
            jnp.sum(sq_out, 0),
            jnp.sum(new_row_side, 1),
            jnp.sum(new_row_proj, 1),
            jnp.sum(new_row_out),
            jnp.sum(sq_in / new_col_in[None, :], 1),
            jnp.sum(sq_side / new_row_side[:, :, None], 1),
            jnp.sum(sq_proj / new_row_proj[:, :, None], 1),
            jnp.sum(sq_out / new_row_out[:, None], 0),
        ),
        both,
    )
    new_row_in = 0.5 * row_in + 0.5 * (sum_row_in / width + stat_eps)
    new_col_side = 0.5 * col_side + 0.5 * (sum_col_side / (2 * width) + stat_eps)
    new_col_proj = 0.5 * col_proj + 0.5 * (sum_col_proj / (2 * width) + stat_eps)
    new_col_out = 0.5 * col_out + 0.5 * (sum_col_out / width + stat_eps)
    mean_in = jnp.mean(new_row_in)
    mean_side = total_side / (2 * width)
    mean_proj = total_proj / (2 * width)
    mean_out = total_out / width
    up_in = red_in * lax.rsqrt(new_row_in[:, None] * new_col_in[None, :] / mean_in)
    up_side = red_side * lax.rsqrt(
        new_row_side[:, :, None] * new_col_side[:, None, :] / mean_side[:, None, None]
    )
    up_proj = red_proj * lax.rsqrt(
        new_row_proj[:, :, None] * new_col_proj[:, None, :] / mean_proj[:, None, None]
    )
    up_out = red_out * lax.rsqrt(new_row_out[:, None] * new_col_out[None, :] / mean_out)
    ms_in = mean_in * jnp.sum(over_in / new_row_in) / (in_width * width)
    ms_side = mean_side * jnp.sum(over_side / new_col_side, 1) / (2 * width * width)
    ms_proj = mean_proj * jnp.sum(over_proj / new_col_proj, 1) / (2 * width * width)
    ms_out = mean_out * jnp.sum(over_out / new_col_out) / (width * classes)
    fac_in = 1.0 / jnp.maximum(1.0, jnp.sqrt(ms_in) / clip_level)
    fac_side = 1.0 / jnp.maximum(1.0, jnp.sqrt(ms_side) / clip_level)
    fac_proj = 1.0 / jnp.maximum(1.0, jnp.sqrt(ms_proj) / clip_level)
    fac_out = 1.0 / jnp.maximum(1.0, jnp.sqrt(ms_out) / clip_level)
    new_in = w_in - step_rate * (up_in * fac_in)
    new_side = w_side - step_rate * (up_side * fac_side[:, None, None])
    new_proj = w_proj - step_rate * (up_proj * fac_proj[:, None, None])
    new_out = w_out - step_rate * (up_out * fac_out)
    return (
        loss_sum,
        label_count,
        red_in,
        red_side,
        red_proj,
        red_out,
        new_in,
        new_side,
        new_proj,
        new_out,
        new_row_in,
        new_col_in,
        new_row_side,
        new_col_side,
        new_row_proj,
        new_col_proj,
        new_row_out,
        new_col_out,
    )


def step_on_device(dims, features, adjacency, *others):
    step = step_fused if dims[0] == 4 and fits_on_chip(adjacency) else step_apart
    return step(dims, features, adjacency, *others)


def solution(mesh):
    in_specs = (
        P(("wide", "narrow"), None),
        P("wide", "narrow"),
        P(("wide", "narrow"), None),
        P(("wide", "narrow")),
        P(("wide", "narrow")),
        P(None, ("wide", "narrow")),
        P(None, ("wide", "narrow"), None),
        P(None, ("wide", "narrow"), None),
        P(("wide", "narrow"), None),
        P(),
        P(("wide", "narrow")),
        P(None, ("wide", "narrow")),
        P(),
        P(None, ("wide", "narrow")),
        P(),
        P(("wide", "narrow")),
        P(),
    )
    out_specs = (
        P(),
        P(),
        P(None, ("wide", "narrow")),
        P(None, ("wide", "narrow"), None),
        P(None, ("wide", "narrow"), None),
        P(("wide", "narrow"), None),
        P(None, ("wide", "narrow")),
        P(None, ("wide", "narrow"), None),
        P(None, ("wide", "narrow"), None),
        P(("wide", "narrow"), None),
        P(),
        P(("wide", "narrow")),
        P(None, ("wide", "narrow")),
        P(),
        P(None, ("wide", "narrow")),
        P(),
        P(("wide", "narrow")),
        P(),
    )
    shards = functools.partial(step_on_device, grid_of(mesh))
    return jax.shard_map(shards, mesh=mesh, in_specs=in_specs, out_specs=out_specs, check_vma=False)
```

```python
import functools
import jax
import jax.numpy as jnp
from jax import lax
from jax.experimental import pallas as pl
from jax.experimental.pallas import tpu as pltpu
from jax.sharding import PartitionSpec as P

MESH = pl.DeviceIdType.MESH
LANES = 128
CORES = 2
f32 = jnp.float32
bf16 = jnp.bfloat16


norm_eps = 1e-06
stat_eps = 1e-30
clip_level = 0.5
step_rate = 0.04


def grid_of(mesh):
    wide, narrow = mesh.shape["wide"], mesh.shape["narrow"]
    far = 4 if wide % 4 == 0 else wide
    return far, wide // far, narrow // CORES, CORES


def place(dims):
    far, near, across, cores = dims
    wide, narrow = lax.axis_index("wide"), lax.axis_index("narrow")
    return wide // near, lax.rem(wide, near), narrow // cores, lax.rem(narrow, cores)


def device(dims, far_at, near_at, across_at, core_at):
    return (far_at * dims[1] + near_at, across_at * dims[3] + core_at)


def send(src, dst, send_sem, recv_sem, target):
    pltpu.make_async_remote_copy(
        src_ref=src,
        dst_ref=dst,
        send_sem=send_sem,
        recv_sem=recv_sem,
        device_id=target,
        device_id_type=MESH,
    ).start()


def arrived(dst, recv_sem):
    pltpu.make_async_copy(dst, dst, recv_sem).wait()


def left_source(src, send_sem):
    pltpu.make_async_copy(src, src, send_sem).wait()


def halves(value):
    high = value.astype(bf16)
    return high, (value - high.astype(f32)).astype(bf16)


def neighbours(dims, at):
    far, near, across, cores = dims
    p, q, x, c = at
    always = [(p, lax.rem(q + step, near), x, c) for step in range(1, near)]
    always += [(p, q, lax.rem(x + step, across), c) for step in range(1, across)]
    always += [(p, q, x, 1 - c)]
    return always


def line_peers(dims, at):
    far = dims[0]
    p, q, x, c = at
    return [(lax.rem(p + step, far), q, x, c) for step in range(1, far)]


def entry_barrier(dims, at):
    barrier = pltpu.get_barrier_semaphore()
    everyone = neighbours(dims, at) + line_peers(dims, at)
    for other in everyone:
        pl.semaphore_signal(barrier, inc=1, device_id=device(dims, *other), device_id_type=MESH)
    pl.semaphore_wait(barrier, len(everyone))


def chunk(ref, k):
    return ref.at[:, pl.ds(k * LANES, LANES)]


class SpreadAll:
    def __init__(self, dims, at, every, right_out, left_out, near_out, across_out, core_out, came):
        self.dims, self.at, self.every = dims, at, every
        self.right_out, self.left_out, self.near_out = right_out, left_out, near_out
        self.across_out, self.core_out, self.came = across_out, core_out, came

    def away(self, distance):
        far, p = self.dims[0], self.at[0]
        if distance == 0:
            return [(p, None)]
        return [(p - distance, p >= distance), (p + distance, p + distance < far)]

    def when(self, flag, act):
        if flag is None:
            act()
        else:
            pl.when(flag)(act)

    def on_line(self, pp, src):
        far, near, across, cores = self.dims
        p, q, x, c = self.at
        dst = self.every.at[pp, q, x, c]
        sem = self.came.at[pp, q, x, c]

        @pl.when(jnp.logical_and(p < far - 1, pp <= p))
        def _():
            send(src, dst, self.right_out.at[pp], sem, device(self.dims, p + 1, q, x, c))

        @pl.when(jnp.logical_and(p > 0, pp >= p))
        def _():
            send(src, dst, self.left_out.at[pp], sem, device(self.dims, p - 1, q, x, c))

        for step in range(1, near):
            send(src, dst, self.near_out.at[pp, step - 1], sem, device(self.dims, p, lax.rem(q + step, near), x, c))

    def on_plane(self, pp, qq, src):
        far, near, across, cores = self.dims
        p, q, x, c = self.at
        dst, sem = self.every.at[pp, qq, x, c], self.came.at[pp, qq, x, c]
        for step in range(1, across):
            send(src, dst, self.across_out.at[pp, qq, step - 1], sem, device(self.dims, p, q, lax.rem(x + step, across), c))
        self.to_core(pp, qq, x, src)

    def to_core(self, pp, qq, xx, src):
        p, q, x, c = self.at
        send(src, self.every.at[pp, qq, xx, c], self.core_out.at[pp, qq, xx], self.came.at[pp, qq, xx, c], device(self.dims, p, q, x, 1 - c))

    def wait(self, *where):
        arrived(self.every.at[where], self.came.at[where])

    def begin(self):
        p, q, x, c = self.at
        own = self.every.at[p, q, x, c]
        self.on_line(p, own)
        self.on_plane(p, q, own)

    def from_line(self, distance):
        p, q, x, c = self.at
        for pp, flag in self.away(distance):
            def act(pp=pp):
                self.wait(pp, q, x, c)
                self.on_line(pp, self.every.at[pp, q, x, c])
                self.on_plane(pp, q, self.every.at[pp, q, x, c])
            self.when(flag, act)

    def from_near(self, distance):
        far, near, across, cores = self.dims
        p, q, x, c = self.at
        for pp, flag in self.away(distance):
            def act(pp=pp):
                for step in range(1, near):
                    qq = lax.rem(q + step, near)
                    self.wait(pp, qq, x, c)
                    self.on_plane(pp, qq, self.every.at[pp, qq, x, c])
            self.when(flag, act)

    def from_across(self, distance):
        far, near, across, cores = self.dims
        p, q, x, c = self.at
        for pp, flag in self.away(distance):
            def act(pp=pp):
                for qq in range(near):
                    for step in range(1, across):
                        xx = lax.rem(x + step, across)
                        self.wait(pp, qq, xx, c)
                        self.to_core(pp, qq, xx, self.every.at[pp, qq, xx, c])
            self.when(flag, act)

    def step(self, distance):
        self.from_line(distance)
        self.from_near(distance - 1)
        if distance >= 2:
            self.from_across(distance - 2)

    def drain(self):
        far = self.dims[0]
        self.from_near(far - 1)
        if far >= 2:
            self.from_across(far - 2)

    def end(self):
        far, near, across, cores = self.dims
        p, q, x, c = self.at
        self.from_across(far - 1)
        for pp in range(far):
            for qq in range(near):
                for xx in range(across):
                    self.wait(pp, qq, xx, 1 - c)
        for pp in range(far):
            block = self.every.at[pp, q, x, c]

            @pl.when(jnp.logical_and(p < far - 1, pp <= p))
            def _(pp=pp, block=block):
                left_source(block, self.right_out.at[pp])

            @pl.when(jnp.logical_and(p > 0, pp >= p))
            def _(pp=pp, block=block):
                left_source(block, self.left_out.at[pp])

            for step in range(1, near):
                left_source(block, self.near_out.at[pp, step - 1])
            for qq in range(near):
                for step in range(1, across):
                    left_source(block, self.across_out.at[pp, qq, step - 1])
                for xx in range(across):
                    left_source(block, self.core_out.at[pp, qq, xx])


def spread_sems(dims):
    far, near, across, cores = dims
    dma = pltpu.SemaphoreType.DMA
    return [
        dma((far,)),
        dma((far,)),
        dma((far, max(near - 1, 1))),
        dma((far, near, max(across - 1, 1))),
        dma((far, near, across)),
        dma((far, near, across, cores)),
    ]


class Blocks:
    def __init__(self, pool, base, *shape):
        self.pool, self.base, self.shape = pool, base, shape

    @property
    def count(self):
        total = 1
        for size in self.shape:
            total *= size
        return total

    def flat(self, where):
        index = 0
        for size, at in zip(self.shape, where):
            index = index * size + at
        left = 1
        for size in self.shape[len(where) :]:
            left *= size
        return self.base + index * left, left

    def ref(self, *where):
        start, _ = self.flat(where)
        return self.pool.at[start]

    def run(self, *where):
        start, left = self.flat(where)
        return self.pool.at[pl.ds(start, left)]

    def add(self, where, other):
        ref = self.ref(*where)
        ref[...] = ref[...] + other[...]


def take(pool, *shapes):
    base, made = 0, []
    for shape in shapes:
        made.append(Blocks(pool, base, *shape))
        base += made[-1].count
    return made


def forward_blocks(dims, chunks):
    far, near, across, cores = dims
    return (
        (chunks, far, near),
        (chunks, cores, across),
        (chunks, across),
        (chunks, across),
    )


def backward_blocks(dims, chunks):
    far, near, across, cores = dims
    return (
        (chunks, across, cores),
        (chunks, far, near),
        (far, near),
        (chunks, far),
        (near,),
        (chunks,),
        (chunks, far, near),
    )


def blocks_of(shapes):
    total = 0
    for shape in shapes:
        size = 1
        for extent in shape:
            size *= extent
        total += size
    return total


def counted(dims, at):
    p, far = at[0], dims[0]
    ends = jnp.where(p > 0, 1, 0) + jnp.where(p < far - 1, 1, 0)
    return len(neighbours(dims, at)) + ends


def announce(dims, at, sem):
    far = dims[0]
    p, q, x, c = at
    for other in neighbours(dims, at):
        pl.semaphore_signal(sem, inc=1, device_id=device(dims, *other), device_id_type=MESH)

    @pl.when(p > 0)
    def _():
        pl.semaphore_signal(sem, inc=1, device_id=device(dims, p - 1, q, x, c), device_id_type=MESH)

    @pl.when(p < far - 1)
    def _():
        pl.semaphore_signal(sem, inc=1, device_id=device(dims, p + 1, q, x, c), device_id_type=MESH)


def await_all(dims, at, sem):
    pl.semaphore_wait(sem, counted(dims, at))


class Hooks:
    def __init__(self, **acts):
        self.acts = acts

    def run(self, name):
        for act in self.acts.get(name, ()):
            act()


def forward_pass(dims, at, chunks, adj, sent, out, pair, pool, sems, hooks):
    to_right, to_left, to_near, came, core_sems, across_out, across_in = sems
    gathered, part, from_core, from_across = take(pool, *forward_blocks(dims, chunks))
    far, near, across, cores = dims
    p, q, x, c = at
    nodes = sent.shape[0]
    early = chunks - 1
    right, left = device(dims, p + 1, q, x, c), device(dims, p - 1, q, x, c)
    others = [lax.rem(q + step, near) for step in range(1, near)]

    def go_right(k, pp, qq, src):
        @pl.when(p < far - 1)
        def _():
            send(src, gathered.ref(k, pp, qq), to_right.at[k, pp, qq], came.at[k, pp, qq], right)

    def go_left(k, pp, qq, src):
        @pl.when(p > 0)
        def _():
            send(src, gathered.ref(k, pp, qq), to_left.at[k, pp, qq], came.at[k, pp, qq], left)

    def go_near(k, pp, src):
        for step, qq in enumerate(others):
            send(src, gathered.ref(k, pp, q), to_near.at[k, pp, step], came.at[k, pp, q], device(dims, p, qq, x, c))

    hooks.run("begin")
    for k in [early] + list(range(chunks - 1)):
        src = chunk(sent, k)
        go_near(k, p, src)
        go_right(k, p, q, src)
        go_left(k, p, q, src)
    for k in range(chunks):
        gathered.ref(k, p, q)[...] = sent[:, k * LANES : (k + 1) * LANES]
    hooks.run("sent")
    for qq in others:
        arrived(gathered.ref(early, p, qq), came.at[early, p, qq])
        go_right(early, p, qq, gathered.ref(early, p, qq))
        go_left(early, p, qq, gathered.ref(early, p, qq))
    group = near * nodes

    def accumulate(k, pp, fresh):
        high, low = halves(gathered.run(k, pp)[...].reshape(group, LANES))
        pair[:group, :LANES] = high
        pair[:group, LANES:] = low
        columns = pl.ds(pl.multiple_of(pp * group, group), group)

        def product(index, carry):
            cc = lax.rem(index // across + 1 + c, cores)
            xx = lax.rem(index, across)
            rows = pl.multiple_of((xx * cores + cc) * nodes, nodes)
            both = jnp.dot(adj[pl.ds(rows, nodes), columns], pair[:group, :], preferred_element_type=f32)
            both = both[:, :LANES] + both[:, LANES:]
            into = part.ref(k, cc, xx)
            into[...] = both if fresh else into[...] + both
            return carry

        lax.fori_loop(0, cores * across, product, 0)

    def from_near(k, pp):
        if isinstance(k, int) and k == early:
            return

        def act():
            for qq in others:
                arrived(gathered.ref(k, pp, qq), came.at[k, pp, qq])

        if isinstance(k, int):
            act()
        else:
            pl.when(k != early)(act)

    def sides(distance):
        if distance == 0:
            return [(p, p >= 0)]
        return [(p - distance, p >= distance), (p + distance, p + distance < far)]

    def from_line(step, k):
        for pp, flag in sides(step):

            @pl.when(flag)
            def _(pp=pp):
                for qq in [q] + (others if k == early else []):
                    block = gathered.ref(k, pp, qq)
                    arrived(block, came.at[k, pp, qq])

                    @pl.when(pp < p)
                    def _():
                        go_right(k, pp, qq, block)

                    @pl.when(pp > p)
                    def _():
                        go_left(k, pp, qq, block)

                if k != early:
                    go_near(k, pp, gathered.ref(k, pp, q))

    def take_in(k, distance):
        for pp, flag in sides(distance):

            @pl.when(flag)
            def _(pp=pp):
                from_near(k, pp)
                accumulate(k, pp, distance == 0)

    def every_chunk(distance):
        def act(k, carry):
            take_in(k, distance)
            return carry

        lax.fori_loop(0, chunks, act, 0)

    def reduce_across(k):
        arrived(from_core.run(k), core_sems.at[1, k])
        for step in range(1, across):
            xx = lax.rem(x + step, across)
            part.add((k, c, xx), from_core.ref(k, xx))
            send(part.ref(k, c, xx), from_across.ref(k, x), across_out.at[k, xx], across_in.at[k, x], device(dims, p, q, xx, c))

    def finish(k):
        total = part.ref(k, c, x)[...] + from_core.ref(k, x)[...]
        for step in range(1, across):
            xx = lax.rem(x + step, across)
            arrived(from_across.ref(k, xx), across_in.at[k, xx])
            total = total + from_across.ref(k, xx)[...]
        out[:, k * LANES : (k + 1) * LANES] = total

    def complete(k):
        take_in(k, last)
        send(part.run(k, 1 - c), from_core.run(k), core_sems.at[0, k], core_sems.at[1, k], device(dims, p, q, x, 1 - c))

    last = far - 1
    for step in range(1, last):
        hooks.run("step%d" % step)
        for k in range(chunks):
            from_line(step, k)
        every_chunk(step - 1)
    hooks.run("step%d" % last)
    for k in range(early):
        if k >= 2:
            reduce_across(k - 2)
        from_line(last, k)
        take_in(k, last - 1)
        if k >= 1:
            complete(k - 1)
    if early >= 2:
        reduce_across(early - 2)
    take_in(early, last - 1)
    hooks.run("drain")
    if early >= 1:
        complete(early - 1)
    for k in range(early - 2):
        finish(k)
    if early >= 1:
        reduce_across(early - 1)
    from_line(last, early)
    complete(early)
    if early >= 2:
        finish(early - 2)
    hooks.run("product")
    reduce_across(early)
    if early >= 1:
        finish(early - 1)
    hooks.run("shadow")
    finish(chunks - 1)
    hooks.run("last")

    for k in range(chunks):
        left_source(part.run(k, 1 - c), core_sems.at[0, k])
        for step in range(1, across):
            xx = lax.rem(x + step, across)
            left_source(part.ref(k, c, xx), across_out.at[k, xx])
        for pp in range(far):
            for qq in [q] + (others if k == early else []):
                block = gathered.ref(k, pp, qq)

                @pl.when(jnp.logical_and(p < far - 1, pp <= p))
                def _(k=k, pp=pp, qq=qq, block=block):
                    left_source(block, to_right.at[k, pp, qq])

                @pl.when(jnp.logical_and(p > 0, pp >= p))
                def _(k=k, pp=pp, qq=qq, block=block):
                    left_source(block, to_left.at[k, pp, qq])

            def near_sent(k=k, pp=pp):
                for step in range(near - 1):
                    left_source(gathered.ref(k, pp, q), to_near.at[k, pp, step])

            if k == early:
                pl.when(pp == p)(near_sent)
            else:
                near_sent()


def forward_sems(dims, chunks):
    far, near, across, cores = dims
    dma = pltpu.SemaphoreType.DMA
    return [dma((chunks, far, near))] * 4 + [dma((2, chunks)), dma((chunks, across)), dma((chunks, across))]


def backward_pass(dims, at, chunks, adj, sent, out, pair, pool, sems, hooks):
    row_out, row_in, near_out, near_in, right_out, left_out, left_in, right_in = sems
    rows, part, line_early, line_rest, right_early, right_rest, from_near = take(
        pool, *backward_blocks(dims, chunks)
    )
    far, near, across, cores = dims
    p, q, x, c = at
    nodes = sent.shape[0]
    total_rows = across * cores * nodes
    early = 0
    right, left = device(dims, p + 1, q, x, c), device(dims, p - 1, q, x, c)
    others = [lax.rem(q + step, near) for step in range(1, near)]
    crossing = [lax.rem(x + step, across) for step in range(1, across)]

    at_end = jnp.logical_or(p == 0, p == far - 1)

    def on_line(k, pp, qq):
        return line_early.ref(pp, qq) if k == early else line_rest.ref(k, pp)

    def from_right_own(k, qq):
        return right_early.ref(qq) if k == early else right_rest.ref(k)

    for k in range(chunks):
        src = chunk(sent, k)
        for xx in crossing:
            send(src, rows.ref(k, x, c), row_out.at[k, xx], row_in.at[k, x, c], device(dims, p, q, xx, c))
        send(src, rows.ref(k, x, c), row_out.at[k, across + x], row_in.at[k, x, c], device(dims, p, q, x, 1 - c))
    for k in range(chunks):
        rows.ref(k, x, c)[...] = sent[:, k * LANES : (k + 1) * LANES]
    hooks.run("sent")

    def dest(i):
        rights = far - 1 - p
        low = jnp.where(i < rights, far - 1 - i, jnp.where(i < far - 1, i - rights, p))
        high = jnp.where(i < p, i, jnp.where(i < far - 1, far - 1 - (i - p), p))
        return jnp.where(p < far // 2, low, high)

    def along(k, pp, qq):
        @pl.when(pp > p)
        def _():
            @pl.when(p > 0)
            def _():
                arrived(on_line(k, pp, qq), left_in.at[k, pp, qq])
                part.add((k, pp, qq), on_line(k, pp, qq))

            send(part.ref(k, pp, qq), on_line(k, pp, qq), right_out.at[k, pp, qq], left_in.at[k, pp, qq], right)

        @pl.when(pp < p)
        def _():
            @pl.when(p < far - 1)
            def _():
                arrived(on_line(k, pp, qq), right_in.at[k, pp, qq])
                part.add((k, pp, qq), on_line(k, pp, qq))

            @pl.when(pp < p - 1)
            def _():
                send(part.ref(k, pp, qq), on_line(k, pp, qq), left_out.at[k, pp, qq], right_in.at[k, pp, qq], left)

            @pl.when(pp == p - 1)
            def _():
                send(part.ref(k, pp, qq), from_right_own(k, qq), left_out.at[k, pp, qq], right_in.at[k, pp, qq], left)

    def settle(k, qq):
        @pl.when(p > 0)
        def _():
            arrived(on_line(k, p, qq), left_in.at[k, p, qq])
            part.add((k, p, qq), on_line(k, p, qq))

        @pl.when(p < far - 1)
        def _():
            arrived(from_right_own(k, qq), right_in.at[k, p, qq])
            part.add((k, p, qq), from_right_own(k, qq))

    def line(k):
        def step(i, carry):
            pp = dest(i)
            if k == early:
                @pl.when(jnp.logical_not(at_end))
                def _():
                    for qq in others + [q]:
                        along(k, pp, qq)
            else:
                for qq in others:
                    arrived(from_near.ref(k, pp, qq), near_in.at[k, pp, qq])
                    part.add((k, pp, q), from_near.ref(k, pp, qq))
                along(k, pp, q)
            return carry

        lax.fori_loop(0, far, step, 0)

    def early_end():
        for step, qq in enumerate(others):
            settle(early, qq)
            send(part.ref(early, p, qq), from_near.ref(early, p, q), near_out.at[early, p, step], near_in.at[early, p, q], device(dims, p, qq, x, c))

    for k in range(chunks):
        for xx in crossing:
            arrived(rows.ref(k, xx, c), row_in.at[k, xx, c])
            send(rows.ref(k, xx, c), rows.ref(k, xx, c), row_out.at[k, across + xx], row_in.at[k, xx, c], device(dims, p, q, x, 1 - c))
        for xx in range(across):
            arrived(rows.ref(k, xx, 1 - c), row_in.at[k, xx, 1 - c])
        high, low = halves(rows.run(k)[...].reshape(total_rows, LANES))
        pair[:total_rows, :LANES] = high
        pair[:total_rows, LANES:] = low

        def product(i, carry, k=k):
            pp = dest(i // near)
            qq = lax.rem(q + 1 + lax.rem(i, near), near)
            start = pl.multiple_of((pp * near + qq) * nodes, nodes)
            both = lax.dot_general(adj[:, pl.ds(start, nodes)], pair[:total_rows, :], (((0,), (0,)), ((), ())), preferred_element_type=f32)
            part.ref(k, pp, qq)[...] = both[:, :LANES] + both[:, LANES:]
            if k == early:
                @pl.when(at_end)
                def _():
                    pl.when(pp != p)(lambda: along(k, pp, qq))
            else:
                @pl.when(qq != q)
                def _():
                    send(part.ref(k, pp, qq), from_near.ref(k, pp, q), near_out.at[k, pp, lax.rem(qq - q - 1 + near, near)], near_in.at[k, pp, q], device(dims, p, qq, x, c))

            return carry

        lax.fori_loop(0, far * near, product, 0)
        if k >= 1:
            line(k - 1)
        hooks.run("chunk%d" % k)
    early_end()
    hooks.run("early")
    line(chunks - 1)
    hooks.run("line")
    for k in range(chunks):
        settle(k, q)
        total = part.ref(k, p, q)[...]
        if k == early:
            for qq in others:
                arrived(from_near.ref(k, p, qq), near_in.at[k, p, qq])
                total = total + from_near.ref(k, p, qq)[...]
        out[:, k * LANES : (k + 1) * LANES] = total

    for k in range(chunks):
        for xx in crossing:
            left_source(rows.ref(k, x, c), row_out.at[k, xx])
        for xx in range(across):
            left_source(rows.ref(k, xx, c), row_out.at[k, across + xx])
        for pp in range(far):
            for qq in [q] + (others if k == early else []):
                @pl.when(pp > p)
                def _(k=k, pp=pp, qq=qq):
                    left_source(part.ref(k, pp, qq), right_out.at[k, pp, qq])

                @pl.when(pp < p)
                def _(k=k, pp=pp, qq=qq):
                    left_source(part.ref(k, pp, qq), left_out.at[k, pp, qq])

            def near_sent(k=k, pp=pp):
                for step in range(near - 1):
                    left_source(part.ref(k, pp, q), near_out.at[k, pp, step])

            if k == early:
                pl.when(pp == p)(near_sent)
            else:
                near_sent()


def backward_sems(dims, chunks):
    far, near, across, cores = dims
    dma = pltpu.SemaphoreType.DMA
    return [dma((chunks, 2 * across)), dma((chunks, across, cores))] + [dma((chunks, far, near))] * 6


class Part:
    def __init__(self, index, piece, offset, depth, own_row, out_row, turned):
        self.index, self.piece, self.offset, self.depth = index, piece, offset, depth
        self.own_row, self.out_row, self.turned = own_row, out_row, turned


class ReduceAll:
    def __init__(self, dims, at, own, out, bufs, sems):
        self.dims, self.at, self.own, self.out = dims, at, own, out
        self.halfway, self.first_buf, self.next_buf, self.left_buf, self.right_buf = bufs
        self.core_sems, self.first_out, self.first_in, self.next_out, self.next_in = sems[:5]
        self.right_out, self.left_out, self.left_in, self.right_in = sems[5:]

    def own_rows(self, part):
        return pl.ds(part.own_row, part.depth)

    def half(self, part, *where):
        lead = (part.piece,) + where + (slice(None),) * (3 - len(where))
        return self.halfway.at[lead + (pl.ds(part.offset, part.depth),)]

    def from_first(self, part, i):
        return self.first_buf.at[part.piece, i, :, :, pl.ds(part.offset, part.depth)]

    def from_next(self, part, i):
        return self.next_buf.at[part.piece, i, :, pl.ds(part.offset, part.depth)]

    def from_left(self, part, pp):
        return self.left_buf.at[part.piece, pp, pl.ds(part.offset, part.depth)]

    def from_right(self, part, pp):
        return self.right_buf.at[part.piece, pp, pl.ds(part.offset, part.depth)]

    def add(self, ref, other):
        ref[...] = ref[...] + other[...]

    def peers(self, turned):
        far, near, across, cores = self.dims
        p, q, x, c = self.at
        if turned:
            return [(lax.rem(q + step, near), device(self.dims, p, lax.rem(q + step, near), x, c)) for step in range(1, near)]
        return [(lax.rem(x + step, across), device(self.dims, p, q, lax.rem(x + step, across), c)) for step in range(1, across)]

    def core_stage(self, part):
        p, q, x, c = self.at
        send(self.own.at[:, :, :, 1 - c, self.own_rows(part)], self.half(part), self.core_sems.at[0, part.index], self.core_sems.at[1, part.index], device(self.dims, p, q, x, 1 - c))

    def across_stage(self, part):
        p, q, x, c = self.at
        arrived(self.half(part), self.core_sems.at[1, part.index])
        self.add(self.half(part), self.own.at[:, :, :, c, self.own_rows(part)])
        for i, (other, target) in enumerate(self.peers(part.turned)):
            src = self.half(part, slice(None), other) if part.turned else self.half(part, slice(None), slice(None), other)
            send(src, self.from_first(part, i), self.first_out.at[part.index, i], self.first_in.at[part.index, i], target)

    def near_stage(self, part):
        p, q, x, c = self.at
        mine = self.half(part, slice(None), q) if part.turned else self.half(part, slice(None), slice(None), x)
        for i, _ in enumerate(self.peers(part.turned)):
            arrived(self.from_first(part, i), self.first_in.at[part.index, i])
            self.add(mine, self.from_first(part, i))
        for i, (other, target) in enumerate(self.peers(not part.turned)):
            src = self.half(part, slice(None), q, other) if part.turned else self.half(part, slice(None), other, x)
            send(src, self.from_next(part, i), self.next_out.at[part.index, i], self.next_in.at[part.index, i], target)

    def line_stage(self, part):
        far, near, across, cores = self.dims
        p, q, x, c = self.at
        for i, _ in enumerate(self.peers(not part.turned)):
            arrived(self.from_next(part, i), self.next_in.at[part.index, i])
            self.add(self.half(part, slice(None), q, x), self.from_next(part, i))
        for distance in range(far - 1, 0, -1):
            pp = p + distance

            @pl.when(pp < far)
            def _(pp=pp):
                @pl.when(p > 0)
                def _():
                    arrived(self.from_left(part, pp), self.left_in.at[part.index, pp])
                    self.add(self.half(part, pp, q, x), self.from_left(part, pp))

                send(self.half(part, pp, q, x), self.from_left(part, pp), self.right_out.at[part.index, pp], self.left_in.at[part.index, pp], device(self.dims, p + 1, q, x, c))

            pm = p - distance

            @pl.when(pm >= 0)
            def _(pm=pm):
                @pl.when(p < far - 1)
                def _():
                    arrived(self.from_right(part, pm), self.right_in.at[part.index, pm])
                    self.add(self.half(part, pm, q, x), self.from_right(part, pm))

                send(self.half(part, pm, q, x), self.from_right(part, pm), self.left_out.at[part.index, pm], self.right_in.at[part.index, pm], device(self.dims, p - 1, q, x, c))

    def last_stage(self, part):
        far, near, across, cores = self.dims
        p, q, x, c = self.at
        into = self.out.at[pl.ds(part.out_row, part.depth)]
        into[...] = self.half(part, p, q, x)[...]

        @pl.when(p > 0)
        def _():
            arrived(self.from_left(part, p), self.left_in.at[part.index, p])
            self.add(into, self.from_left(part, p))

        @pl.when(p < far - 1)
        def _():
            arrived(self.from_right(part, p), self.right_in.at[part.index, p])
            self.add(into, self.from_right(part, p))

    def end(self, part):
        far, near, across, cores = self.dims
        p, q, x, c = self.at
        left_source(self.half(part), self.core_sems.at[0, part.index])
        for i, _ in enumerate(self.peers(part.turned)):
            left_source(self.from_first(part, i), self.first_out.at[part.index, i])
        for i, _ in enumerate(self.peers(not part.turned)):
            left_source(self.from_next(part, i), self.next_out.at[part.index, i])
        for pp in range(far):
            @pl.when(pp > p)
            def _(pp=pp):
                left_source(self.from_left(part, pp), self.right_out.at[part.index, pp])

            @pl.when(pp < p)
            def _(pp=pp):
                left_source(self.from_right(part, pp), self.left_out.at[part.index, pp])


def reduce_scratch(dims, pieces, parts, depth, width):
    far, near, across, cores = dims
    dma = pltpu.SemaphoreType.DMA
    bufs = [
        pltpu.VMEM((pieces, far, near, across, depth, width), f32),
        pltpu.VMEM((pieces, max(across - 1, 1), far, near, depth, width), f32),
        pltpu.VMEM((pieces, max(near - 1, 1), far, depth, width), f32),
        pltpu.VMEM((pieces, far, depth, width), f32),
        pltpu.VMEM((pieces, far, depth, width), f32),
    ]
    sems = [
        dma((2, parts)),
        dma((parts, max(across - 1, 1))),
        dma((parts, max(across - 1, 1))),
        dma((parts, max(near - 1, 1))),
        dma((parts, max(near - 1, 1))),
    ] + [dma((parts, far))] * 4
    return bufs, sems


def forward_kernel(dims, chunks, adj, sent, out, pair, pool, *sems):
    at = place(dims)
    entry_barrier(dims, at)
    forward_pass(dims, at, chunks, adj, sent, out, pair, pool, sems, Hooks())


def backward_kernel(dims, chunks, adj, sent, out, pair, pool, *sems):
    at = place(dims)
    entry_barrier(dims, at)
    backward_pass(dims, at, chunks, adj, sent, out, pair, pool, sems, Hooks())


def aggregate(dims, name_id, adj, sent, backward=False):
    far, near, across, cores = dims
    nodes, width = sent.shape
    chunks = width // LANES
    kernel = backward_kernel if backward else forward_kernel
    blocks = backward_blocks if backward else forward_blocks
    sems = backward_sems if backward else forward_sems
    depth = (across * cores if backward else far * near) * nodes
    return pl.pallas_call(
        functools.partial(kernel, dims, chunks),
        out_shape=jax.ShapeDtypeStruct((nodes, width), f32),
        in_specs=[pl.BlockSpec(memory_space=pltpu.VMEM)] * 2,
        out_specs=pl.BlockSpec(memory_space=pltpu.VMEM),
        scratch_shapes=[
            pltpu.VMEM((depth, 2 * LANES), bf16),
            pltpu.VMEM((blocks_of(blocks(dims, chunks)), nodes, LANES), f32),
        ]
        + sems(dims, chunks),
        compiler_params=pltpu.CompilerParams(
            collective_id=name_id, has_side_effects=True, vmem_limit_bytes=60 * 2**20
        ),
    )(adj, sent)


def contract(left, right, over):
    first, second = halves(left), halves(right)

    def go(a, b):
        return lax.dot_general(a, b, (over, ((), ())), preferred_element_type=f32)

    return go(first[0], second[0]) + (go(first[0], second[1]) + go(first[1], second[0]))


def plain(left, right):
    return contract(left, right, ((1,), (0,)))


def left_flip(left, right):
    return contract(left, right, ((0,), (0,)))


def right_flip(left, right):
    return contract(left, right, ((1,), (1,)))


def rows_of(every, half, start, size):
    far = every.shape[0]
    value = every[half * (far // 2) : (half + 1) * (far // 2), :, :, :, start : start + size, :]
    return value.reshape(-1, value.shape[-1])


def put_rows(every, half, start, size, value):
    far = every.shape[0]
    shape = (far // 2,) + every.shape[1:4] + (size, value.shape[-1])
    every[half * (far // 2) : (half + 1) * (far // 2), :, :, :, start : start + size, :] = value.reshape(shape)


def activation(pre_act):
    sig = jax.nn.sigmoid(pre_act)
    act = pre_act * sig
    return sig, act, lax.rsqrt(jnp.mean(act * act, -1, keepdims=True) + norm_eps)


def column_of(row):
    size = row.shape[1]
    same = lax.broadcasted_iota(jnp.int32, (size, size), 0) == lax.broadcasted_iota(jnp.int32, (size, size), 1)
    return jnp.sum(jnp.where(same, jnp.broadcast_to(row, (size, size)), 0.0), 1, keepdims=True)


def row_of(column):
    size = column.shape[0]
    same = lax.broadcasted_iota(jnp.int32, (size, size), 0) == lax.broadcasted_iota(jnp.int32, (size, size), 1)
    return jnp.sum(jnp.where(same, jnp.broadcast_to(column, (size, size)), 0.0), 0, keepdims=True)


def blend(old, mean_square):
    return 0.5 * old + 0.5 * (mean_square + stat_eps)


def row_statistic(grad, old, count):
    square = grad * grad
    return square, blend(old, jnp.sum(square, 1, keepdims=True) / count)


def train_kernel(dims, in_width, classes, adj_hbm, feats, info, w_in_t, w_side, w_proj, w_out, col_in, row_side, row_proj, row_out, red, stat, refs):
    far, near, across, cores = dims
    at = place(dims)
    nodes, wide_in = feats.shape
    layers, block, width = w_side.shape
    every = [refs["every%d" % layer] for layer in range(layers)]
    adj, stage, stage_sems = refs["adj"], refs["stage"], refs["stage_sems"]
    pair, pool, sent = refs["pair"], refs["pool"], refs["sent"]
    raw, inverse, mix, direct, back = refs["raw"], refs["inverse"], refs["mix"], refs["direct"], refs["back"]
    agg, hid, pre, outer, ready = refs["agg"], refs["hid"], refs["pre"], refs["outer"], refs["ready"]
    in_chunks, chunks = wide_in // LANES, width // LANES
    head = 2 * block
    tail = wide_in - width + LANES

    strip = stage.shape[1]

    def strip_copy(i):
        return pltpu.make_async_copy(adj_hbm.at[pl.ds(i * strip, strip)], stage.at[i % 2], stage_sems.at[i % 2])

    strips = adj.shape[0] // strip
    strip_copy(0).start()
    strip_copy(1).start()
    for layer in range(layers):
        mine = every[layer].at[at]
        mine[:block] = w_side[layer]
        mine[block : 2 * block] = w_proj[layer]
    mine = every[0].at[at]
    mine[head : head + block // 2] = w_in_t[:, :width]
    mine[head + block // 2 : head + block, : wide_in - width] = w_in_t[:, width:]
    mine[head + block // 2 : head + block, wide_in - width : tail] = jnp.zeros((block // 2, LANES), f32)
    mine[head + block // 2 : head + block, wide_in - width : wide_in - width + classes] = w_out[...]
    marked = jnp.sum(info[:, LANES + 2 : LANES + 3], 0, keepdims=True)
    mine[head + block // 2 : head + block, tail:] = jnp.broadcast_to(marked, (block // 2, width - tail))
    entry_barrier(dims, at)
    target = info[:, :LANES]
    alpha = info[:, LANES : LANES + 1]
    weight = info[:, LANES + 1 : LANES + 2]
    lane = lax.broadcasted_iota(jnp.int32, (nodes, wide_in), 1)
    sent[...] = jnp.where(lane == in_width, 1.0, feats[...] * alpha)

    def load_adjacency():
        for i in range(strips):
            strip_copy(i).wait()
            adj[i * strip : (i + 1) * strip, :] = stage[i % 2].astype(f32).astype(bf16)
            if i + 2 < strips:
                strip_copy(i + 2).start()

    spreads = [SpreadAll(dims, at, every[l], *refs["spread%d" % l]) for l in range(layers)]

    def mixing(layer):
        for half in range(2):
            side = rows_of(every[layer], half, 0, block)
            proj = rows_of(every[layer], half, block, block)
            mix[layer % 2, half] = plain(side, proj)

    def input_weights():
        def both(start):
            return jnp.concatenate([rows_of(every[0], half, start, block // 2) for half in range(2)], 0)

        first, second = both(head), both(head + block // 2)
        return jnp.concatenate([first, second[:, : wide_in - width]], 1)

    def ahead(layer):
        spreads[layer].end()
        mixing(layer)
        if layer == 0:
            hid[0] = right_flip(feats[...], input_weights())
        direct[...] = plain(hid[layer], mix[layer % 2, 0])

    rounds = iter(range(ready.shape[0]))
    for layer in range(layers):
        acts = {}
        now = spreads[layer]
        if layer == 0:
            acts = {"begin": [now.begin], "sent": [load_adjacency], "step1": [functools.partial(now.step, 1)], "step2": [functools.partial(now.step, 2)], "step3": [functools.partial(now.step, 3)], "drain": [now.drain], "shadow": [functools.partial(ahead, 0)]}
        else:
            acts = {"sent": [functools.partial(now.step, 2)], "step2": [functools.partial(now.step, 3)], "step3": [now.drain, functools.partial(ahead, layer)]}
        if layer + 1 < layers:
            after = spreads[layer + 1]
            for name, act in [("drain", after.begin), ("last", functools.partial(after.step, 1))]:
                acts[name] = acts.get(name, []) + [act]
        if layer == 0:
            forward_pass(dims, at, in_chunks, adj, sent, raw, pair, pool, refs["forward"], Hooks(**acts))
            turn = ready.at[next(rounds)]
            announce(dims, at, turn)
            inverse[...] = jnp.broadcast_to(1.0 / (1.0 + raw[:, in_width : in_width + 1]), inverse.shape)
            raw[...] = jnp.where(lane < in_width, raw[...] * inverse[:, 0:1], 0.0)
            agg[0] = right_flip(raw[...], input_weights())
        else:
            forward_pass(dims, at, chunks, adj, sent, agg.at[layer], pair, pool, refs["forward"], Hooks(**acts))
            turn = ready.at[next(rounds)]
            announce(dims, at, turn)
            agg[layer] = agg[layer] * inverse[:, 0:1]
        pre_act = direct[...] + plain(agg[layer], mix[layer % 2, 1])
        pre[layer] = pre_act
        _, act, scale = activation(pre_act)
        after = act * scale
        hid[layer + 1] = after
        if layer + 1 < layers:
            sent[:, :width] = after * alpha
        await_all(dims, at, turn)

    def output_weights():
        at_lane = wide_in - width
        return jnp.concatenate(
            [rows_of(every[0], half, head + block // 2, block // 2)[:, at_lane : at_lane + LANES] for half in range(2)], 0
        )

    labelled = jnp.sum(every[0][:, :, :, :, head + block // 2 : head + block // 2 + 8, tail : tail + LANES].reshape(-1, 8, LANES), 0)[0:1, 0:1]
    refs["marks"][...] = jnp.broadcast_to(labelled, refs["marks"].shape)
    head_weights = output_weights()
    logits = plain(hid[layers], head_weights)
    column = lax.broadcasted_iota(jnp.int32, logits.shape, 1)
    soft = jnp.maximum(logits, 0.0) + jnp.log(1.0 + jnp.exp(-jnp.abs(logits)))
    each = jnp.where(column < classes, soft - target * logits, 0.0)
    loss = jnp.sum(weight * jnp.sum(each, -1, keepdims=True), 0, keepdims=True)
    d_logits = jnp.where(column < classes, (weight / labelled) * (jax.nn.sigmoid(logits) - target), 0.0)
    g_out = left_flip(hid[layers], d_logits)
    d_out = right_flip(d_logits, head_weights)
    start = head + block // 2
    half_rows = width // 2
    for half in range(2):
        piece = jnp.concatenate(
            [
                jnp.zeros((half_rows, wide_in - width), f32),
                g_out[half * half_rows : (half + 1) * half_rows],
                jnp.broadcast_to(loss, (half_rows, width - tail)),
            ],
            1,
        )
        put_rows(every[0], half, start, block // 2, piece)

    reduces = [ReduceAll(dims, at, every[l], red, refs["reduce_bufs"], refs["reduce_sems"]) for l in range(layers)]

    def slope(layer, d_out):
        pre_act = pre[layer]
        sig, act, scale = activation(pre_act)
        normed = act * scale
        d_act = scale * (d_out - normed * jnp.mean(d_out * normed, -1, keepdims=True))
        return d_act * sig * (1.0 + pre_act * (1.0 - sig))

    def outers(layer, d_pre):
        outer[0] = left_flip(hid[layer], d_pre)
        outer[1] = left_flip(agg[layer], d_pre)

    def weight_grads(layer, half):
        side = rows_of(every[layer], half, 0, block)
        proj = rows_of(every[layer], half, block, block)
        g_side = right_flip(outer[half], proj)
        g_proj = left_flip(side, outer[half])
        put_rows(every[layer], half, 0, block, g_side)
        put_rows(every[layer], half, block, block, g_proj)

    base = [0, 3 * block, 5 * block]
    sums = refs["sums"]
    sums[...] = jnp.zeros_like(sums)
    spot = lax.broadcasted_iota(jnp.int32, (1, wide_in), 1)
    slot = 2 * layers

    def note_total(index, new_row):
        total = jnp.sum(new_row, 0, keepdims=True)
        sums[slot + 1 : slot + 2] = sums[slot + 1 : slot + 2] + jnp.where(spot == LANES + index, total, 0.0)

    def note_layer(layer):
        for kind, old in enumerate((row_side, row_proj)):
            start = base[layer] + kind * block
            square, new_row = row_statistic(red[start : start + block], column_of(old[layer : layer + 1]), width)
            index = kind * layers + layer
            sums[index : index + 1, :width] = jnp.sum(square, 0, keepdims=True)
            sums[slot + 2 + index : slot + 3 + index, :width] = jnp.sum(square / new_row, 0, keepdims=True)
            note_total(index, new_row)

    def note_head():
        first, second = red[head : head + block // 2], red[head + block // 2 : head + block]
        square = jnp.concatenate([first * first, second[:, : wide_in - width] * second[:, : wide_in - width]], 1)
        new_col = blend(column_of(col_in[...]), jnp.sum(square, 1, keepdims=True) / in_width)
        sums[slot : slot + 1] = jnp.sum(square, 0, keepdims=True)
        sums[2 * slot + 2 : 2 * slot + 3] = jnp.sum(square / new_col, 0, keepdims=True)
        square, new_row = row_statistic(second[:, wide_in - width : tail], column_of(row_out[...]), classes)
        sums[slot + 1 : slot + 2, :LANES] = jnp.sum(square, 0, keepdims=True)
        sums[2 * slot + 3 : 2 * slot + 4, :LANES] = jnp.sum(square / new_row, 0, keepdims=True)
        note_total(slot, new_row)

    def sum_everywhere(stat):
        far, near, across, cores = dims
        p, q, x, c = at
        came_in, out_sems, in_sems = refs["sum_in"], refs["sum_out"], refs["sum_came"]
        groups = [
            [device(dims, p, q, x, 1 - c)],
            [device(dims, p, q, lax.rem(x + step, across), c) for step in range(1, across)],
            [device(dims, p, lax.rem(q + step, near), x, c) for step in range(1, near)],
            [device(dims, *other) for other in line_peers(dims, at)],
        ]
        base_slot = 0
        for turn, group in enumerate(groups):
            for i, target in enumerate(group):
                at_slot = base_slot + i
                send(sums.at[pl.ds(turn * stat.shape[0], stat.shape[0])], came_in.at[at_slot], out_sems.at[at_slot], in_sems.at[at_slot], target)
            total = sums[turn * stat.shape[0] : (turn + 1) * stat.shape[0]]
            for i in range(len(group)):
                at_slot = base_slot + i
                arrived(came_in.at[at_slot], in_sems.at[at_slot])
                total = total + came_in[at_slot]
            base_slot += len(group)
            if turn + 1 < len(groups):
                sums[(turn + 1) * stat.shape[0] : (turn + 2) * stat.shape[0]] = total
            else:
                stat[...] = total
                stat[2 * slot + 4 : 2 * slot + 5, :LANES] = jnp.broadcast_to(refs["marks"][0:1, 0:1], (1, LANES))
        for at_slot in range(base_slot):
            left_source(came_in.at[at_slot], out_sems.at[at_slot])


    def finish_reduce(layer, parts):
        for part in parts:
            reduces[layer].last_stage(part)
        for part in parts:
            reduces[layer].end(part)
        note_layer(layer)

    d_pre_ref = refs["d_pre"]
    carried, freed = [], []
    for layer in range(layers - 1, 0, -1):
        d_pre_ref[...] = slope(layer, d_out)
        sent[:, :width] = d_pre_ref[...] * inverse[:, 0:1]
        first = 2 * ((layers - 1 - layer) % 2)
        parts = [
            Part(first + kind, first + kind, 0, block, kind * block, base[layer] + kind * block, False) for kind in range(2)
        ]

        def begin_grads(layer=layer):
            outers(layer, d_pre_ref[...])
            weight_grads(layer, 0)

        def more_grads(layer=layer, parts=parts):
            weight_grads(layer, 1)
            for part in parts:
                reduces[layer].core_stage(part)

        def direct_part(layer=layer):
            direct[...] = right_flip(d_pre_ref[...], mix[layer % 2, 0])

        def stage(name, layer=layer, parts=parts):
            for part in parts:
                getattr(reduces[layer], name)(part)

        acts = {
            "sent": carried[:1] + [begin_grads],
            "chunk0": carried[1:],
            "chunk1": [more_grads],
            "chunk2": [direct_part, functools.partial(stage, "across_stage")],
            "early": [functools.partial(mixing, 0)] if layer == 1 else [],
            "line": [functools.partial(stage, "near_stage")],
        }
        backward_pass(dims, at, chunks, adj, sent, back, pair, pool, refs["backward"], Hooks(**acts))
        if layer > 1:
            turn = ready.at[next(rounds)]
            announce(dims, at, turn)
        d_out = direct[...] + right_flip(back[...] * alpha, mix[layer % 2, 1])
        if layer > 1:
            await_all(dims, at, turn)

        def close(layer=layer, parts=parts):
            finish_reduce(layer, parts)
            if layer == layers - 1 or layer == 1:
                freed.append(ready.at[next(rounds)])
                announce(dims, at, freed[-1])

        carried = [functools.partial(stage, "line_stage"), close]

    d_pre = slope(0, d_out)
    d_pre_ref[...] = d_pre
    carried[0]()
    d_self = right_flip(d_pre, mix[0, 0])
    d_neigh = right_flip(d_pre, mix[0, 1])
    g_in = left_flip(d_self, feats[...]) + left_flip(d_neigh, raw[...])
    for half in range(2):
        top = slice(half * half_rows, (half + 1) * half_rows)
        put_rows(every[0], half, head, block // 2, g_in[top, :width])
        where = (slice(half * (far // 2), (half + 1) * (far // 2)),) + (slice(None),) * 3
        value = g_in[top, width:]
        every[0][where + (slice(head + block // 2, head + block), slice(0, wide_in - width))] = value.reshape(
            (far // 2, near, across, cores, block // 2, wide_in - width)
        )
    carried[1]()
    for turn in freed:
        await_all(dims, at, turn)
    final = reduces[0]
    depth = block // 2
    order = [
        Part(2 * piece + turned, piece, turned * depth, depth, piece * block + turned * depth, piece * block + turned * depth, turned == 1 and near == across)
        for piece in (2, 0, 1)
        for turned in range(2)
    ]
    for part in order[:2]:
        final.core_stage(part)
    outers(0, d_pre)
    for part in order[:2]:
        final.across_stage(part)
    weight_grads(0, 0)
    for part in order[:2]:
        final.near_stage(part)
    weight_grads(0, 1)
    for part in order[2:]:
        final.core_stage(part)
    for part in order[:2]:
        final.line_stage(part)
    for part in order[2:]:
        final.across_stage(part)
    for part in order[2:]:
        final.near_stage(part)
    for part in order[2:]:
        final.line_stage(part)
    finish_reduce(0, order)
    note_head()
    sum_everywhere(stat)


def update_kernel(in_width, classes, red, stat, w_in_t, w_side, w_proj, w_out, row_in, col_in, row_side, col_side, row_proj, col_proj, row_out, col_out, loss, count, g_in, g_side, g_proj, g_out, n_in, n_side, n_proj, n_out, s_row_in, s_col_in, s_row_side, s_col_side, s_row_proj, s_col_proj, s_row_out, s_col_out):
    layers, block, width = w_side.shape
    head = 2 * block
    wide_in = w_in_t.shape[1]
    tail = wide_in - width + LANES
    slot = 2 * layers
    base = [0, 3 * block, 5 * block]

    def step_of(weight, grad, new_row, new_col, mean, over, size):
        update = grad * lax.rsqrt(new_row * new_col / mean)
        factor = 1.0 / jnp.maximum(1.0, jnp.sqrt(mean * over / size) / clip_level)
        return weight - step_rate * (update * factor)

    def total_of(index):
        return stat[slot + 1 : slot + 2, LANES + index : LANES + index + 1]

    kinds = (
        (w_side, row_side, col_side, g_side, n_side, s_row_side, s_col_side),
        (w_proj, row_proj, col_proj, g_proj, n_proj, s_row_proj, s_col_proj),
    )
    for layer in range(layers):
        for kind, (weight, row, col, g, n, s_row, s_col) in enumerate(kinds):
            start = base[layer] + kind * block
            index = kind * layers + layer
            grad = red[start : start + block]
            _, new_row = row_statistic(grad, column_of(row[layer : layer + 1]), width)
            new_col = blend(col[layer : layer + 1], stat[index : index + 1, :width] / (2 * width))
            over = jnp.sum(stat[slot + 2 + index : slot + 3 + index, :width] / new_col, 1, keepdims=True)
            g[layer] = grad
            n[layer] = step_of(weight[layer], grad, new_row, new_col, total_of(index) / (2 * width), over, 2 * width * width)
            s_row[layer : layer + 1] = row_of(new_row)
            s_col[layer : layer + 1] = new_col
    first, second = red[head : head + block // 2], red[head + block // 2 : head + block]
    grad = jnp.concatenate([first, second[:, : wide_in - width]], 1)[:, :in_width]
    new_col = blend(column_of(col_in[...]), jnp.sum(grad * grad, 1, keepdims=True) / in_width)
    new_row = blend(row_in[...], stat[slot : slot + 1, :in_width] / width)
    mean = jnp.sum(new_row, 1, keepdims=True) / in_width
    over = jnp.sum(stat[2 * slot + 2 : 2 * slot + 3, :in_width] / new_row, 1, keepdims=True)
    g_in[...] = grad
    n_in[...] = step_of(w_in_t[:, :in_width], grad, new_col, new_row, mean, over, in_width * width)
    s_row_in[...] = new_row
    s_col_in[...] = row_of(new_col)
    grad = second[:, wide_in - width : wide_in - width + classes]
    _, new_row = row_statistic(grad, column_of(row_out[...]), classes)
    new_col = blend(col_out[...], stat[slot + 1 : slot + 2, :classes] / width)
    over = jnp.sum(stat[2 * slot + 3 : 2 * slot + 4, :classes] / new_col, 1, keepdims=True)
    g_out[...] = grad
    n_out[...] = step_of(w_out[...], grad, new_row, new_col, total_of(slot) / width, over, width * classes)
    s_row_out[...] = row_of(new_row)
    s_col_out[...] = new_col
    loss[...] = second[0:1, tail : tail + 1]
    count[...] = stat[2 * slot + 4 : 2 * slot + 5, 0:1]


def train_on_device(dims, name_id, in_width, classes, adjacency, feats, info, w_in_t, w_side, w_proj, w_out, col_in, row_side, row_proj, row_out):
    far, near, across, cores = dims
    nodes, wide_in = feats.shape
    layers, block, width = w_side.shape
    in_chunks, chunks = wide_in // LANES, width // LANES
    dma = pltpu.SemaphoreType.DMA
    pool = max(blocks_of(forward_blocks(dims, in_chunks)), blocks_of(backward_blocks(dims, chunks)))
    bufs, sems = reduce_scratch(dims, 4, 6, block, width)
    strip = 128
    stat_rows = 24
    partners = 1 + (across - 1) + (near - 1) + (far - 1)
    vmem = pl.BlockSpec(memory_space=pltpu.VMEM)
    refs = {
        "adj": pltpu.VMEM(adjacency.shape, bf16),
        "stage": pltpu.VMEM((2, strip, adjacency.shape[1]), jnp.int32),
        "stage_sems": dma((2,)),
        "pair": pltpu.VMEM((max(far * near, across * cores) * nodes, 2 * LANES), bf16),
        "pool": pltpu.VMEM((pool, nodes, LANES), f32),
        "sent": pltpu.VMEM((nodes, wide_in), f32),
        "raw": pltpu.VMEM((nodes, wide_in), f32),
        "inverse": pltpu.VMEM((nodes, LANES), f32),
        "mix": pltpu.VMEM((2, 2, width, width), f32),
        "direct": pltpu.VMEM((nodes, width), f32),
        "back": pltpu.VMEM((nodes, width), f32),
        "d_pre": pltpu.VMEM((nodes, width), f32),
        "agg": pltpu.VMEM((layers, nodes, width), f32),
        "hid": pltpu.VMEM((layers + 1, nodes, width), f32),
        "pre": pltpu.VMEM((layers, nodes, width), f32),
        "outer": pltpu.VMEM((2, width, width), f32),
        "ready": pltpu.SemaphoreType.REGULAR((3 * layers - 3,)),
        "forward": forward_sems(dims, in_chunks),
        "backward": backward_sems(dims, chunks),
        "sums": pltpu.VMEM((4 * stat_rows, wide_in), f32),
        "sum_in": pltpu.VMEM((partners, stat_rows, wide_in), f32),
        "sum_out": dma((partners,)),
        "sum_came": dma((partners,)),
        "marks": pltpu.VMEM((8, LANES), f32),
        "reduce_bufs": bufs,
        "reduce_sems": sems,
    }
    for layer in range(layers):
        refs["every%d" % layer] = pltpu.VMEM(dims + ((3 if layer == 0 else 2) * block, width), f32)
        refs["spread%d" % layer] = spread_sems(dims)
    return pl.pallas_call(
        functools.partial(train_kernel, dims, in_width, classes),
        out_shape=(
            jax.ShapeDtypeStruct((7 * block, width), f32),
            jax.ShapeDtypeStruct((stat_rows, wide_in), f32),
        ),
        in_specs=[pl.BlockSpec(memory_space=pl.ANY)] + [vmem] * 10,
        out_specs=(vmem, vmem),
        scratch_shapes=[refs],
        compiler_params=pltpu.CompilerParams(
            collective_id=name_id, has_side_effects=True, vmem_limit_bytes=63 * 2**20
        ),
    )(adjacency, feats, info, w_in_t, w_side, w_proj, w_out, col_in, row_side, row_proj, row_out)


def update_on_device(in_width, classes, *arrays):
    w_side, w_out = arrays[3], arrays[5]
    layers, block, width = w_side.shape
    shapes = [
        (1, 1),
        (1, 1),
        (block // 2, in_width),
        w_side.shape,
        w_side.shape,
        w_out.shape,
        (block // 2, in_width),
        w_side.shape,
        w_side.shape,
        w_out.shape,
        (1, in_width),
        (1, block // 2),
        (layers, block),
        (layers, width),
        (layers, block),
        (layers, width),
        (1, block // 2),
        (1, classes),
    ]
    vmem = pl.BlockSpec(memory_space=pltpu.VMEM)
    return pl.pallas_call(
        functools.partial(update_kernel, in_width, classes),
        out_shape=[jax.ShapeDtypeStruct(shape, f32) for shape in shapes],
        in_specs=[vmem] * len(arrays),
        out_specs=[vmem] * len(shapes),
    )(*arrays)


def dot(left, right, over=((1,), (0,))):
    return lax.dot_general(
        left, right, (over, ((), ())), precision=lax.Precision.HIGH, preferred_element_type=f32
    )


def left_t(left, right):
    return dot(left, right, ((0,), (0,)))


def right_t(left, right):
    return dot(left, right, ((1,), (1,)))


def pad_lanes(value, lanes):
    return jnp.pad(value, ((0, 0), (0, lanes - value.shape[1])))


def fits_on_chip(adjacency):
    return 2 * adjacency.shape[0] * adjacency.shape[1] <= 4 * 2**20


def step_fused(
    dims,
    features,
    adjacency,
    labels,
    labelled,
    node_count,
    w_in,
    w_side,
    w_proj,
    w_out,
    row_in,
    col_in,
    row_side,
    col_side,
    row_proj,
    col_proj,
    row_out,
    col_out,
):
    nodes, in_width = features.shape
    classes = w_out.shape[1]
    wide_in = -(-(in_width + 1) // LANES) * LANES
    counts = node_count.astype(f32)
    mask = labelled.astype(f32)
    lane = lax.broadcasted_iota(jnp.int32, (nodes, LANES), 1)
    facts = jnp.where(
        lane == 0,
        (2.0 / (1.0 + counts))[:, None],
        jnp.where(lane == 1, (mask * lax.rsqrt(counts))[:, None], jnp.where(lane == 2, mask[:, None], 0.0)),
    )
    info = jnp.concatenate([pad_lanes(labels.astype(f32), LANES), facts], 1)
    w_in_t = pad_lanes(w_in.T, wide_in)
    local = (w_in_t, w_side, w_proj, w_out)
    red, stat = train_on_device(
        dims, 1, in_width, classes, adjacency, pad_lanes(features, wide_in), info, *local,
        col_in[None], row_side, row_proj, row_out[None],
    )
    done = update_on_device(
        in_width, classes, red, stat, *local,
        row_in[None], col_in[None], row_side, col_side, row_proj, col_proj, row_out[None], col_out[None],
    )
    (loss, count, g_in, g_side, g_proj, g_out, n_in, n_side, n_proj, n_out,
     s_row_in, s_col_in, s_row_side, s_col_side, s_row_proj, s_col_proj, s_row_out, s_col_out) = done
    return (
        loss[0, 0],
        count[0, 0],
        g_in.T,
        g_side,
        g_proj,
        g_out,
        n_in.T,
        n_side,
        n_proj,
        n_out,
        s_row_in[0],
        s_col_in[0],
        s_row_side,
        s_col_side,
        s_row_proj,
        s_col_proj,
        s_row_out[0],
        s_col_out[0],
    )


def step_apart(
    dims,
    features,
    adjacency,
    labels,
    labelled,
    node_count,
    w_in,
    w_side,
    w_proj,
    w_out,
    row_in,
    col_in,
    row_side,
    col_side,
    row_proj,
    col_proj,
    row_out,
    col_out,
):
    layers = w_side.shape[0]
    width = w_side.shape[2]
    in_width = features.shape[1]
    classes = w_out.shape[1]
    nodes = features.shape[0]
    both = ("wide", "narrow")
    adj = adjacency.astype(bf16)
    counts = node_count.astype(f32)
    alpha = 2.0 / (1.0 + counts)
    lam = lax.rsqrt(counts)
    target = labels.astype(f32)
    weight_mask = labelled.astype(f32)

    spare = -(in_width + 1) % LANES
    sent = jnp.concatenate(
        [alpha[:, None] * features, jnp.ones((nodes, 1), f32), jnp.zeros((nodes, spare), f32)], 1
    )
    summed = aggregate(dims, 1, adj, sent)
    inverse = 1.0 / (1.0 + summed[:, in_width : in_width + 1])
    agg_features = summed[:, :in_width] * inverse

    full_in, full_side, full_proj, full_out = (
        lax.all_gather(w_in, both, axis=1, tiled=True),
        lax.all_gather(w_side, both, axis=1, tiled=True),
        lax.all_gather(w_proj, both, axis=1, tiled=True),
        lax.all_gather(w_out, both, axis=0, tiled=True),
    )
    mix_self = [dot(full_side[l, :width], full_proj[l, :width]) for l in range(layers)]
    mix_neigh = [dot(full_side[l, width:], full_proj[l, width:]) for l in range(layers)]

    kept = []
    hidden = dot(features, full_in)
    agg = dot(agg_features, full_in)
    for layer in range(layers):
        if layer > 0:
            agg = aggregate(dims, 1 + layer, adj, alpha[:, None] * hidden) * inverse
        pre_act = dot(hidden, mix_self[layer]) + dot(agg, mix_neigh[layer])
        kept.append((hidden, agg, pre_act))
        act = jax.nn.silu(pre_act)
        hidden = act * lax.rsqrt(jnp.mean(act * act, -1, keepdims=True) + norm_eps)

    logits = dot(hidden, full_out)
    per = jnp.sum(jax.nn.softplus(logits) - target * logits, -1)
    loss_sum, label_count = lax.psum(
        (jnp.sum(weight_mask * lam * per), jnp.sum(weight_mask)), both
    )
    d_logits = (weight_mask * lam / label_count)[:, None] * (jax.nn.sigmoid(logits) - target)
    g_out = left_t(hidden, d_logits)
    d_out = right_t(d_logits, full_out)
    side_grads = [None] * layers
    proj_grads = [None] * layers
    for layer in reversed(range(layers)):
        hidden, agg, pre_act = kept[layer]
        sig = jax.nn.sigmoid(pre_act)
        act = pre_act * sig
        scale = lax.rsqrt(jnp.mean(act * act, -1, keepdims=True) + norm_eps)
        normed = act * scale
        d_act = scale * (d_out - normed * jnp.mean(d_out * normed, -1, keepdims=True))
        d_pre = d_act * sig * (1.0 + pre_act * (1.0 - sig))
        outer_self = left_t(hidden, d_pre)
        outer_neigh = left_t(agg, d_pre)
        side, proj = full_side[layer], full_proj[layer]
        side_grads[layer] = jnp.concatenate(
            [right_t(outer_self, proj[:width]), right_t(outer_neigh, proj[width:])], 0
        )
        proj_grads[layer] = jnp.concatenate(
            [left_t(side[:width], outer_self), left_t(side[width:], outer_neigh)], 0
        )
        d_self = right_t(d_pre, mix_self[layer])
        if layer > 0:
            back = aggregate(dims, 3 + layer, adj, d_pre * inverse, backward=True)
            d_out = d_self + right_t(alpha[:, None] * back, mix_neigh[layer])
        else:
            g_in = left_t(features, d_self) + left_t(agg_features, right_t(d_pre, mix_neigh[layer]))
    red_in, red_side, red_proj, red_out = (
        lax.psum_scatter(g_in, both, scatter_dimension=1, tiled=True),
        lax.psum_scatter(jnp.stack(side_grads), both, scatter_dimension=1, tiled=True),
        lax.psum_scatter(jnp.stack(proj_grads), both, scatter_dimension=1, tiled=True),
        lax.psum_scatter(g_out, both, scatter_dimension=0, tiled=True),
    )
    sq_in = red_in * red_in
    sq_side = red_side * red_side
    sq_proj = red_proj * red_proj
    sq_out = red_out * red_out
    new_col_in = 0.5 * col_in + 0.5 * (jnp.mean(sq_in, 0) + stat_eps)
    new_row_side = 0.5 * row_side + 0.5 * (jnp.mean(sq_side, 2) + stat_eps)
    new_row_proj = 0.5 * row_proj + 0.5 * (jnp.mean(sq_proj, 2) + stat_eps)
    new_row_out = 0.5 * row_out + 0.5 * (jnp.mean(sq_out, 1) + stat_eps)
    (
        sum_row_in,
        sum_col_side,
        sum_col_proj,
        sum_col_out,
        total_side,
        total_proj,
        total_out,
        over_in,
        over_side,
        over_proj,
        over_out,
    ) = lax.psum(
        (
            jnp.sum(sq_in, 1),
            jnp.sum(sq_side, 1),
            jnp.sum(sq_proj, 1),
            jnp.sum(sq_out, 0),
            jnp.sum(new_row_side, 1),
            jnp.sum(new_row_proj, 1),
            jnp.sum(new_row_out),
            jnp.sum(sq_in / new_col_in[None, :], 1),
            jnp.sum(sq_side / new_row_side[:, :, None], 1),
            jnp.sum(sq_proj / new_row_proj[:, :, None], 1),
            jnp.sum(sq_out / new_row_out[:, None], 0),
        ),
        both,
    )
    new_row_in = 0.5 * row_in + 0.5 * (sum_row_in / width + stat_eps)
    new_col_side = 0.5 * col_side + 0.5 * (sum_col_side / (2 * width) + stat_eps)
    new_col_proj = 0.5 * col_proj + 0.5 * (sum_col_proj / (2 * width) + stat_eps)
    new_col_out = 0.5 * col_out + 0.5 * (sum_col_out / width + stat_eps)
    mean_in = jnp.mean(new_row_in)
    mean_side = total_side / (2 * width)
    mean_proj = total_proj / (2 * width)
    mean_out = total_out / width
    up_in = red_in * lax.rsqrt(new_row_in[:, None] * new_col_in[None, :] / mean_in)
    up_side = red_side * lax.rsqrt(
        new_row_side[:, :, None] * new_col_side[:, None, :] / mean_side[:, None, None]
    )
    up_proj = red_proj * lax.rsqrt(
        new_row_proj[:, :, None] * new_col_proj[:, None, :] / mean_proj[:, None, None]
    )
    up_out = red_out * lax.rsqrt(new_row_out[:, None] * new_col_out[None, :] / mean_out)
    ms_in = mean_in * jnp.sum(over_in / new_row_in) / (in_width * width)
    ms_side = mean_side * jnp.sum(over_side / new_col_side, 1) / (2 * width * width)
    ms_proj = mean_proj * jnp.sum(over_proj / new_col_proj, 1) / (2 * width * width)
    ms_out = mean_out * jnp.sum(over_out / new_col_out) / (width * classes)
    fac_in = 1.0 / jnp.maximum(1.0, jnp.sqrt(ms_in) / clip_level)
    fac_side = 1.0 / jnp.maximum(1.0, jnp.sqrt(ms_side) / clip_level)
    fac_proj = 1.0 / jnp.maximum(1.0, jnp.sqrt(ms_proj) / clip_level)
    fac_out = 1.0 / jnp.maximum(1.0, jnp.sqrt(ms_out) / clip_level)
    new_in = w_in - step_rate * (up_in * fac_in)
    new_side = w_side - step_rate * (up_side * fac_side[:, None, None])
    new_proj = w_proj - step_rate * (up_proj * fac_proj[:, None, None])
    new_out = w_out - step_rate * (up_out * fac_out)
    return (
        loss_sum,
        label_count,
        red_in,
        red_side,
        red_proj,
        red_out,
        new_in,
        new_side,
        new_proj,
        new_out,
        new_row_in,
        new_col_in,
        new_row_side,
        new_col_side,
        new_row_proj,
        new_col_proj,
        new_row_out,
        new_col_out,
    )


def step_on_device(dims, features, adjacency, *others):
    step = step_fused if dims[0] == 4 and fits_on_chip(adjacency) else step_apart
    return step(dims, features, adjacency, *others)


def solution(mesh):
    in_specs = (
        P(("wide", "narrow"), None),
        P("wide", "narrow"),
        P(("wide", "narrow"), None),
        P(("wide", "narrow")),
        P(("wide", "narrow")),
        P(None, ("wide", "narrow")),
        P(None, ("wide", "narrow"), None),
        P(None, ("wide", "narrow"), None),
        P(("wide", "narrow"), None),
        P(),
        P(("wide", "narrow")),
        P(None, ("wide", "narrow")),
        P(),
        P(None, ("wide", "narrow")),
        P(),
        P(("wide", "narrow")),
        P(),
    )
    out_specs = (
        P(),
        P(),
        P(None, ("wide", "narrow")),
        P(None, ("wide", "narrow"), None),
        P(None, ("wide", "narrow"), None),
        P(("wide", "narrow"), None),
        P(None, ("wide", "narrow")),
        P(None, ("wide", "narrow"), None),
        P(None, ("wide", "narrow"), None),
        P(("wide", "narrow"), None),
        P(),
        P(("wide", "narrow")),
        P(None, ("wide", "narrow")),
        P(),
        P(None, ("wide", "narrow")),
        P(),
        P(("wide", "narrow")),
        P(),
    )
    shards = functools.partial(step_on_device, grid_of(mesh))
    return jax.shard_map(shards, mesh=mesh, in_specs=in_specs, out_specs=out_specs, check_vma=False)
```

```python
import functools
import jax
import jax.numpy as jnp
from jax import lax
from jax.experimental import pallas as pl
from jax.experimental.pallas import tpu as pltpu
from jax.sharding import PartitionSpec as P

MESH = pl.DeviceIdType.MESH
LANES = 128
CORES = 2
f32 = jnp.float32
bf16 = jnp.bfloat16


norm_eps = 1e-06
stat_eps = 1e-30
clip_level = 0.5
step_rate = 0.04


def grid_of(mesh):
    wide, narrow = mesh.shape["wide"], mesh.shape["narrow"]
    far = 4 if wide % 4 == 0 else wide
    return far, wide // far, narrow // CORES, CORES


def place(dims):
    far, near, across, cores = dims
    wide, narrow = lax.axis_index("wide"), lax.axis_index("narrow")
    return wide // near, lax.rem(wide, near), narrow // cores, lax.rem(narrow, cores)


def device(dims, far_at, near_at, across_at, core_at):
    return (far_at * dims[1] + near_at, across_at * dims[3] + core_at)


def send(src, dst, send_sem, recv_sem, target):
    pltpu.make_async_remote_copy(
        src_ref=src,
        dst_ref=dst,
        send_sem=send_sem,
        recv_sem=recv_sem,
        device_id=target,
        device_id_type=MESH,
    ).start()


def arrived(dst, recv_sem):
    pltpu.make_async_copy(dst, dst, recv_sem).wait()


def left_source(src, send_sem):
    pltpu.make_async_copy(src, src, send_sem).wait()


def halves(value):
    high = value.astype(bf16)
    return high, (value - high.astype(f32)).astype(bf16)


def neighbours(dims, at):
    far, near, across, cores = dims
    p, q, x, c = at
    always = [(p, lax.rem(q + step, near), x, c) for step in range(1, near)]
    always += [(p, q, lax.rem(x + step, across), c) for step in range(1, across)]
    always += [(p, q, x, 1 - c)]
    return always


def line_peers(dims, at):
    far = dims[0]
    p, q, x, c = at
    return [(lax.rem(p + step, far), q, x, c) for step in range(1, far)]


def entry_barrier(dims, at):
    barrier = pltpu.get_barrier_semaphore()
    everyone = neighbours(dims, at) + line_peers(dims, at)
    for other in everyone:
        pl.semaphore_signal(barrier, inc=1, device_id=device(dims, *other), device_id_type=MESH)
    pl.semaphore_wait(barrier, len(everyone))


def chunk(ref, k):
    return ref.at[:, pl.ds(k * LANES, LANES)]


class SpreadAll:
    def __init__(self, dims, at, every, right_out, left_out, near_out, across_out, core_out, came):
        self.dims, self.at, self.every = dims, at, every
        self.right_out, self.left_out, self.near_out = right_out, left_out, near_out
        self.across_out, self.core_out, self.came = across_out, core_out, came

    def away(self, distance):
        far, p = self.dims[0], self.at[0]
        if distance == 0:
            return [(p, None)]
        return [(p - distance, p >= distance), (p + distance, p + distance < far)]

    def when(self, flag, act):
        if flag is None:
            act()
        else:
            pl.when(flag)(act)

    def on_line(self, pp, src):
        far, near, across, cores = self.dims
        p, q, x, c = self.at
        dst = self.every.at[pp, q, x, c]
        sem = self.came.at[pp, q, x, c]

        @pl.when(jnp.logical_and(p < far - 1, pp <= p))
        def _():
            send(src, dst, self.right_out.at[pp], sem, device(self.dims, p + 1, q, x, c))

        @pl.when(jnp.logical_and(p > 0, pp >= p))
        def _():
            send(src, dst, self.left_out.at[pp], sem, device(self.dims, p - 1, q, x, c))

        for step in range(1, near):
            send(src, dst, self.near_out.at[pp, step - 1], sem, device(self.dims, p, lax.rem(q + step, near), x, c))

    def on_plane(self, pp, qq, src):
        far, near, across, cores = self.dims
        p, q, x, c = self.at
        dst, sem = self.every.at[pp, qq, x, c], self.came.at[pp, qq, x, c]
        for step in range(1, across):
            send(src, dst, self.across_out.at[pp, qq, step - 1], sem, device(self.dims, p, q, lax.rem(x + step, across), c))
        self.to_core(pp, qq, x, src)

    def to_core(self, pp, qq, xx, src):
        p, q, x, c = self.at
        send(src, self.every.at[pp, qq, xx, c], self.core_out.at[pp, qq, xx], self.came.at[pp, qq, xx, c], device(self.dims, p, q, x, 1 - c))

    def wait(self, *where):
        arrived(self.every.at[where], self.came.at[where])

    def begin(self):
        p, q, x, c = self.at
        own = self.every.at[p, q, x, c]
        self.on_line(p, own)
        self.on_plane(p, q, own)

    def from_line(self, distance):
        p, q, x, c = self.at
        for pp, flag in self.away(distance):
            def act(pp=pp):
                self.wait(pp, q, x, c)
                self.on_line(pp, self.every.at[pp, q, x, c])
                self.on_plane(pp, q, self.every.at[pp, q, x, c])
            self.when(flag, act)

    def from_near(self, distance):
        far, near, across, cores = self.dims
        p, q, x, c = self.at
        for pp, flag in self.away(distance):
            def act(pp=pp):
                for step in range(1, near):
                    qq = lax.rem(q + step, near)
                    self.wait(pp, qq, x, c)
                    self.on_plane(pp, qq, self.every.at[pp, qq, x, c])
            self.when(flag, act)

    def from_across(self, distance):
        far, near, across, cores = self.dims
        p, q, x, c = self.at
        for pp, flag in self.away(distance):
            def act(pp=pp):
                for qq in range(near):
                    for step in range(1, across):
                        xx = lax.rem(x + step, across)
                        self.wait(pp, qq, xx, c)
                        self.to_core(pp, qq, xx, self.every.at[pp, qq, xx, c])
            self.when(flag, act)

    def step(self, distance):
        self.from_line(distance)
        self.from_near(distance - 1)
        if distance >= 2:
            self.from_across(distance - 2)

    def drain(self):
        far = self.dims[0]
        self.from_near(far - 1)
        if far >= 2:
            self.from_across(far - 2)

    def end(self):
        far, near, across, cores = self.dims
        p, q, x, c = self.at
        self.from_across(far - 1)
        for pp in range(far):
            for qq in range(near):
                for xx in range(across):
                    self.wait(pp, qq, xx, 1 - c)
        for pp in range(far):
            block = self.every.at[pp, q, x, c]

            @pl.when(jnp.logical_and(p < far - 1, pp <= p))
            def _(pp=pp, block=block):
                left_source(block, self.right_out.at[pp])

            @pl.when(jnp.logical_and(p > 0, pp >= p))
            def _(pp=pp, block=block):
                left_source(block, self.left_out.at[pp])

            for step in range(1, near):
                left_source(block, self.near_out.at[pp, step - 1])
            for qq in range(near):
                for step in range(1, across):
                    left_source(block, self.across_out.at[pp, qq, step - 1])
                for xx in range(across):
                    left_source(block, self.core_out.at[pp, qq, xx])


def spread_sems(dims):
    far, near, across, cores = dims
    dma = pltpu.SemaphoreType.DMA
    return [
        dma((far,)),
        dma((far,)),
        dma((far, max(near - 1, 1))),
        dma((far, near, max(across - 1, 1))),
        dma((far, near, across)),
        dma((far, near, across, cores)),
    ]


class Blocks:
    def __init__(self, pool, base, *shape):
        self.pool, self.base, self.shape = pool, base, shape

    @property
    def count(self):
        total = 1
        for size in self.shape:
            total *= size
        return total

    def flat(self, where):
        index = 0
        for size, at in zip(self.shape, where):
            index = index * size + at
        left = 1
        for size in self.shape[len(where) :]:
            left *= size
        return self.base + index * left, left

    def ref(self, *where):
        start, _ = self.flat(where)
        return self.pool.at[start]

    def run(self, *where):
        start, left = self.flat(where)
        return self.pool.at[pl.ds(start, left)]

    def add(self, where, other):
        ref = self.ref(*where)
        ref[...] = ref[...] + other[...]


def take(pool, *shapes):
    base, made = 0, []
    for shape in shapes:
        made.append(Blocks(pool, base, *shape))
        base += made[-1].count
    return made


def forward_blocks(dims, chunks):
    far, near, across, cores = dims
    return (
        (chunks, far, near),
        (chunks, cores, across),
        (chunks, across),
        (chunks, across),
    )


def backward_blocks(dims, chunks):
    far, near, across, cores = dims
    return (
        (chunks, across, cores),
        (chunks, far, near),
        (far, near),
        (chunks, far),
        (near,),
        (chunks,),
        (chunks, far, near),
    )


def blocks_of(shapes):
    total = 0
    for shape in shapes:
        size = 1
        for extent in shape:
            size *= extent
        total += size
    return total


def counted(dims, at):
    p, far = at[0], dims[0]
    ends = jnp.where(p > 0, 1, 0) + jnp.where(p < far - 1, 1, 0)
    return len(neighbours(dims, at)) + ends


def announce(dims, at, sem):
    far = dims[0]
    p, q, x, c = at
    for other in neighbours(dims, at):
        pl.semaphore_signal(sem, inc=1, device_id=device(dims, *other), device_id_type=MESH)

    @pl.when(p > 0)
    def _():
        pl.semaphore_signal(sem, inc=1, device_id=device(dims, p - 1, q, x, c), device_id_type=MESH)

    @pl.when(p < far - 1)
    def _():
        pl.semaphore_signal(sem, inc=1, device_id=device(dims, p + 1, q, x, c), device_id_type=MESH)


def await_all(dims, at, sem):
    pl.semaphore_wait(sem, counted(dims, at))


class Hooks:
    def __init__(self, **acts):
        self.acts = acts

    def run(self, name):
        for act in self.acts.get(name, ()):
            act()


def forward_pass(dims, at, chunks, adj, sent, out, pair, pool, sems, hooks):
    to_right, to_left, to_near, came, core_sems, across_out, across_in = sems
    gathered, part, from_core, from_across = take(pool, *forward_blocks(dims, chunks))
    far, near, across, cores = dims
    p, q, x, c = at
    nodes = sent.shape[0]
    early = chunks - 1
    right, left = device(dims, p + 1, q, x, c), device(dims, p - 1, q, x, c)
    others = [lax.rem(q + step, near) for step in range(1, near)]

    def go_right(k, pp, qq, src):
        @pl.when(p < far - 1)
        def _():
            send(src, gathered.ref(k, pp, qq), to_right.at[k, pp, qq], came.at[k, pp, qq], right)

    def go_left(k, pp, qq, src):
        @pl.when(p > 0)
        def _():
            send(src, gathered.ref(k, pp, qq), to_left.at[k, pp, qq], came.at[k, pp, qq], left)

    def go_near(k, pp, src):
        for step, qq in enumerate(others):
            send(src, gathered.ref(k, pp, q), to_near.at[k, pp, step], came.at[k, pp, q], device(dims, p, qq, x, c))

    hooks.run("begin")
    for k in [early] + list(range(chunks - 1)):
        src = chunk(sent, k)
        go_near(k, p, src)
        go_right(k, p, q, src)
        go_left(k, p, q, src)
    for k in range(chunks):
        gathered.ref(k, p, q)[...] = sent[:, k * LANES : (k + 1) * LANES]
    hooks.run("sent")
    for qq in others:
        arrived(gathered.ref(early, p, qq), came.at[early, p, qq])
        go_right(early, p, qq, gathered.ref(early, p, qq))
        go_left(early, p, qq, gathered.ref(early, p, qq))
    group = near * nodes

    def accumulate(k, pp, fresh):
        high, low = halves(gathered.run(k, pp)[...].reshape(group, LANES))
        pair[:group, :LANES] = high
        pair[:group, LANES:] = low
        columns = pl.ds(pl.multiple_of(pp * group, group), group)

        def product(index, carry):
            cc = lax.rem(index // across + 1 + c, cores)
            xx = lax.rem(index, across)
            rows = pl.multiple_of((xx * cores + cc) * nodes, nodes)
            both = jnp.dot(adj[pl.ds(rows, nodes), columns], pair[:group, :], preferred_element_type=f32)
            both = both[:, :LANES] + both[:, LANES:]
            into = part.ref(k, cc, xx)
            into[...] = both if fresh else into[...] + both
            return carry

        lax.fori_loop(0, cores * across, product, 0)

    def from_near(k, pp):
        if isinstance(k, int) and k == early:
            return

        def act():
            for qq in others:
                arrived(gathered.ref(k, pp, qq), came.at[k, pp, qq])

        if isinstance(k, int):
            act()
        else:
            pl.when(k != early)(act)

    def sides(distance):
        if distance == 0:
            return [(p, p >= 0)]
        return [(p - distance, p >= distance), (p + distance, p + distance < far)]

    def from_line(step, k):
        for pp, flag in sides(step):

            @pl.when(flag)
            def _(pp=pp):
                for qq in [q] + (others if k == early else []):
                    block = gathered.ref(k, pp, qq)
                    arrived(block, came.at[k, pp, qq])

                    @pl.when(pp < p)
                    def _():
                        go_right(k, pp, qq, block)

                    @pl.when(pp > p)
                    def _():
                        go_left(k, pp, qq, block)

                if k != early:
                    go_near(k, pp, gathered.ref(k, pp, q))

    def take_in(k, distance):
        for pp, flag in sides(distance):

            @pl.when(flag)
            def _(pp=pp):
                from_near(k, pp)
                accumulate(k, pp, distance == 0)

    def every_chunk(distance):
        def act(k, carry):
            take_in(k, distance)
            return carry

        lax.fori_loop(0, chunks, act, 0)

    def reduce_across(k):
        arrived(from_core.run(k), core_sems.at[1, k])
        for step in range(1, across):
            xx = lax.rem(x + step, across)
            part.add((k, c, xx), from_core.ref(k, xx))
            send(part.ref(k, c, xx), from_across.ref(k, x), across_out.at[k, xx], across_in.at[k, x], device(dims, p, q, xx, c))

    def finish(k):
        total = part.ref(k, c, x)[...] + from_core.ref(k, x)[...]
        for step in range(1, across):
            xx = lax.rem(x + step, across)
            arrived(from_across.ref(k, xx), across_in.at[k, xx])
            total = total + from_across.ref(k, xx)[...]
        out[:, k * LANES : (k + 1) * LANES] = total

    def complete(k):
        take_in(k, last)
        send(part.run(k, 1 - c), from_core.run(k), core_sems.at[0, k], core_sems.at[1, k], device(dims, p, q, x, 1 - c))

    last = far - 1
    for step in range(1, last):
        hooks.run("step%d" % step)
        for k in range(chunks):
            from_line(step, k)
        every_chunk(step - 1)
    hooks.run("step%d" % last)
    for k in range(early):
        if k >= 2:
            reduce_across(k - 2)
        from_line(last, k)
        take_in(k, last - 1)
        if k >= 1:
            complete(k - 1)
    if early >= 2:
        reduce_across(early - 2)
    take_in(early, last - 1)
    hooks.run("drain")
    if early >= 1:
        complete(early - 1)
    for k in range(early - 2):
        finish(k)
    if early >= 1:
        reduce_across(early - 1)
    from_line(last, early)
    complete(early)
    if early >= 2:
        finish(early - 2)
    hooks.run("product")
    reduce_across(early)
    if early >= 1:
        finish(early - 1)
    hooks.run("shadow")
    finish(chunks - 1)
    hooks.run("last")

    for k in range(chunks):
        left_source(part.run(k, 1 - c), core_sems.at[0, k])
        for step in range(1, across):
            xx = lax.rem(x + step, across)
            left_source(part.ref(k, c, xx), across_out.at[k, xx])
        for pp in range(far):
            for qq in [q] + (others if k == early else []):
                block = gathered.ref(k, pp, qq)

                @pl.when(jnp.logical_and(p < far - 1, pp <= p))
                def _(k=k, pp=pp, qq=qq, block=block):
                    left_source(block, to_right.at[k, pp, qq])

                @pl.when(jnp.logical_and(p > 0, pp >= p))
                def _(k=k, pp=pp, qq=qq, block=block):
                    left_source(block, to_left.at[k, pp, qq])

            def near_sent(k=k, pp=pp):
                for step in range(near - 1):
                    left_source(gathered.ref(k, pp, q), to_near.at[k, pp, step])

            if k == early:
                pl.when(pp == p)(near_sent)
            else:
                near_sent()


def forward_sems(dims, chunks):
    far, near, across, cores = dims
    dma = pltpu.SemaphoreType.DMA
    return [dma((chunks, far, near))] * 4 + [dma((2, chunks)), dma((chunks, across)), dma((chunks, across))]


def backward_pass(dims, at, chunks, adj, sent, out, pair, pool, sems, hooks):
    row_out, row_in, near_out, near_in, right_out, left_out, left_in, right_in = sems
    rows, part, line_early, line_rest, right_early, right_rest, from_near = take(
        pool, *backward_blocks(dims, chunks)
    )
    far, near, across, cores = dims
    p, q, x, c = at
    nodes = sent.shape[0]
    total_rows = across * cores * nodes
    early = 0
    right, left = device(dims, p + 1, q, x, c), device(dims, p - 1, q, x, c)
    others = [lax.rem(q + step, near) for step in range(1, near)]
    crossing = [lax.rem(x + step, across) for step in range(1, across)]

    at_end = jnp.logical_or(p == 0, p == far - 1)

    def on_line(k, pp, qq):
        return line_early.ref(pp, qq) if k == early else line_rest.ref(k, pp)

    def from_right_own(k, qq):
        return right_early.ref(qq) if k == early else right_rest.ref(k)

    for k in range(chunks):
        src = chunk(sent, k)
        for xx in crossing:
            send(src, rows.ref(k, x, c), row_out.at[k, xx], row_in.at[k, x, c], device(dims, p, q, xx, c))
        send(src, rows.ref(k, x, c), row_out.at[k, across + x], row_in.at[k, x, c], device(dims, p, q, x, 1 - c))
    for k in range(chunks):
        rows.ref(k, x, c)[...] = sent[:, k * LANES : (k + 1) * LANES]
    hooks.run("sent")

    def dest(i):
        rights = far - 1 - p
        low = jnp.where(i < rights, far - 1 - i, jnp.where(i < far - 1, i - rights, p))
        high = jnp.where(i < p, i, jnp.where(i < far - 1, far - 1 - (i - p), p))
        return jnp.where(p < far // 2, low, high)

    def along(k, pp, qq):
        @pl.when(pp > p)
        def _():
            @pl.when(p > 0)
            def _():
                arrived(on_line(k, pp, qq), left_in.at[k, pp, qq])
                part.add((k, pp, qq), on_line(k, pp, qq))

            send(part.ref(k, pp, qq), on_line(k, pp, qq), right_out.at[k, pp, qq], left_in.at[k, pp, qq], right)

        @pl.when(pp < p)
        def _():
            @pl.when(p < far - 1)
            def _():
                arrived(on_line(k, pp, qq), right_in.at[k, pp, qq])
                part.add((k, pp, qq), on_line(k, pp, qq))

            @pl.when(pp < p - 1)
            def _():
                send(part.ref(k, pp, qq), on_line(k, pp, qq), left_out.at[k, pp, qq], right_in.at[k, pp, qq], left)

            @pl.when(pp == p - 1)
            def _():
                send(part.ref(k, pp, qq), from_right_own(k, qq), left_out.at[k, pp, qq], right_in.at[k, pp, qq], left)

    def settle(k, qq):
        @pl.when(p > 0)
        def _():
            arrived(on_line(k, p, qq), left_in.at[k, p, qq])
            part.add((k, p, qq), on_line(k, p, qq))

        @pl.when(p < far - 1)
        def _():
            arrived(from_right_own(k, qq), right_in.at[k, p, qq])
            part.add((k, p, qq), from_right_own(k, qq))

    def line(k):
        def step(i, carry):
            pp = dest(i)
            if k == early:
                @pl.when(jnp.logical_not(at_end))
                def _():
                    for qq in others + [q]:
                        along(k, pp, qq)
            else:
                for qq in others:
                    arrived(from_near.ref(k, pp, qq), near_in.at[k, pp, qq])
                    part.add((k, pp, q), from_near.ref(k, pp, qq))
                along(k, pp, q)
            return carry

        lax.fori_loop(0, far, step, 0)

    def early_end():
        for step, qq in enumerate(others):
            settle(early, qq)
            send(part.ref(early, p, qq), from_near.ref(early, p, q), near_out.at[early, p, step], near_in.at[early, p, q], device(dims, p, qq, x, c))

    for k in range(chunks):
        for xx in crossing:
            arrived(rows.ref(k, xx, c), row_in.at[k, xx, c])
            send(rows.ref(k, xx, c), rows.ref(k, xx, c), row_out.at[k, across + xx], row_in.at[k, xx, c], device(dims, p, q, x, 1 - c))
        for xx in range(across):
            arrived(rows.ref(k, xx, 1 - c), row_in.at[k, xx, 1 - c])
        high, low = halves(rows.run(k)[...].reshape(total_rows, LANES))
        pair[:total_rows, :LANES] = high
        pair[:total_rows, LANES:] = low

        def product(i, carry, k=k):
            pp = dest(i // near)
            qq = lax.rem(q + 1 + lax.rem(i, near), near)
            start = pl.multiple_of((pp * near + qq) * nodes, nodes)
            both = lax.dot_general(adj[:, pl.ds(start, nodes)], pair[:total_rows, :], (((0,), (0,)), ((), ())), preferred_element_type=f32)
            part.ref(k, pp, qq)[...] = both[:, :LANES] + both[:, LANES:]
            if k == early:
                @pl.when(at_end)
                def _():
                    pl.when(pp != p)(lambda: along(k, pp, qq))
            else:
                @pl.when(qq != q)
                def _():
                    send(part.ref(k, pp, qq), from_near.ref(k, pp, q), near_out.at[k, pp, lax.rem(qq - q - 1 + near, near)], near_in.at[k, pp, q], device(dims, p, qq, x, c))

            return carry

        lax.fori_loop(0, far * near, product, 0)
        if k >= 1:
            line(k - 1)
        hooks.run("chunk%d" % k)
    early_end()
    hooks.run("early")
    line(chunks - 1)
    hooks.run("line")
    for k in range(chunks):
        settle(k, q)
        total = part.ref(k, p, q)[...]
        if k == early:
            for qq in others:
                arrived(from_near.ref(k, p, qq), near_in.at[k, p, qq])
                total = total + from_near.ref(k, p, qq)[...]
        out[:, k * LANES : (k + 1) * LANES] = total

    for k in range(chunks):
        for xx in crossing:
            left_source(rows.ref(k, x, c), row_out.at[k, xx])
        for xx in range(across):
            left_source(rows.ref(k, xx, c), row_out.at[k, across + xx])
        for pp in range(far):
            for qq in [q] + (others if k == early else []):
                @pl.when(pp > p)
                def _(k=k, pp=pp, qq=qq):
                    left_source(part.ref(k, pp, qq), right_out.at[k, pp, qq])

                @pl.when(pp < p)
                def _(k=k, pp=pp, qq=qq):
                    left_source(part.ref(k, pp, qq), left_out.at[k, pp, qq])

            def near_sent(k=k, pp=pp):
                for step in range(near - 1):
                    left_source(part.ref(k, pp, q), near_out.at[k, pp, step])

            if k == early:
                pl.when(pp == p)(near_sent)
            else:
                near_sent()


def backward_sems(dims, chunks):
    far, near, across, cores = dims
    dma = pltpu.SemaphoreType.DMA
    return [dma((chunks, 2 * across)), dma((chunks, across, cores))] + [dma((chunks, far, near))] * 6


class Part:
    def __init__(self, index, piece, offset, depth, own_row, out_row, turned):
        self.index, self.piece, self.offset, self.depth = index, piece, offset, depth
        self.own_row, self.out_row, self.turned = own_row, out_row, turned


class ReduceAll:
    def __init__(self, dims, at, own, out, bufs, sems):
        self.dims, self.at, self.own, self.out = dims, at, own, out
        self.halfway, self.first_buf, self.next_buf, self.left_buf, self.right_buf = bufs
        self.core_sems, self.first_out, self.first_in, self.next_out, self.next_in = sems[:5]
        self.right_out, self.left_out, self.left_in, self.right_in = sems[5:]

    def own_rows(self, part):
        return pl.ds(part.own_row, part.depth)

    def half(self, part, *where):
        lead = (part.piece,) + where + (slice(None),) * (3 - len(where))
        return self.halfway.at[lead + (pl.ds(part.offset, part.depth),)]

    def from_first(self, part, i):
        return self.first_buf.at[part.piece, i, :, :, pl.ds(part.offset, part.depth)]

    def from_next(self, part, i):
        return self.next_buf.at[part.piece, i, :, pl.ds(part.offset, part.depth)]

    def from_left(self, part, pp):
        return self.left_buf.at[part.piece, pp, pl.ds(part.offset, part.depth)]

    def from_right(self, part, pp):
        return self.right_buf.at[part.piece, pp, pl.ds(part.offset, part.depth)]

    def add(self, ref, other):
        ref[...] = ref[...] + other[...]

    def peers(self, turned):
        far, near, across, cores = self.dims
        p, q, x, c = self.at
        if turned:
            return [(lax.rem(q + step, near), device(self.dims, p, lax.rem(q + step, near), x, c)) for step in range(1, near)]
        return [(lax.rem(x + step, across), device(self.dims, p, q, lax.rem(x + step, across), c)) for step in range(1, across)]

    def core_stage(self, part):
        p, q, x, c = self.at
        send(self.own.at[:, :, :, 1 - c, self.own_rows(part)], self.half(part), self.core_sems.at[0, part.index], self.core_sems.at[1, part.index], device(self.dims, p, q, x, 1 - c))

    def across_stage(self, part):
        p, q, x, c = self.at
        arrived(self.half(part), self.core_sems.at[1, part.index])
        self.add(self.half(part), self.own.at[:, :, :, c, self.own_rows(part)])
        for i, (other, target) in enumerate(self.peers(part.turned)):
            src = self.half(part, slice(None), other) if part.turned else self.half(part, slice(None), slice(None), other)
            send(src, self.from_first(part, i), self.first_out.at[part.index, i], self.first_in.at[part.index, i], target)

    def near_stage(self, part):
        p, q, x, c = self.at
        mine = self.half(part, slice(None), q) if part.turned else self.half(part, slice(None), slice(None), x)
        for i, _ in enumerate(self.peers(part.turned)):
            arrived(self.from_first(part, i), self.first_in.at[part.index, i])
            self.add(mine, self.from_first(part, i))
        for i, (other, target) in enumerate(self.peers(not part.turned)):
            src = self.half(part, slice(None), q, other) if part.turned else self.half(part, slice(None), other, x)
            send(src, self.from_next(part, i), self.next_out.at[part.index, i], self.next_in.at[part.index, i], target)

    def line_stage(self, part):
        far, near, across, cores = self.dims
        p, q, x, c = self.at
        for i, _ in enumerate(self.peers(not part.turned)):
            arrived(self.from_next(part, i), self.next_in.at[part.index, i])
            self.add(self.half(part, slice(None), q, x), self.from_next(part, i))
        for distance in range(far - 1, 0, -1):
            pp = p + distance

            @pl.when(pp < far)
            def _(pp=pp):
                @pl.when(p > 0)
                def _():
                    arrived(self.from_left(part, pp), self.left_in.at[part.index, pp])
                    self.add(self.half(part, pp, q, x), self.from_left(part, pp))

                send(self.half(part, pp, q, x), self.from_left(part, pp), self.right_out.at[part.index, pp], self.left_in.at[part.index, pp], device(self.dims, p + 1, q, x, c))

            pm = p - distance

            @pl.when(pm >= 0)
            def _(pm=pm):
                @pl.when(p < far - 1)
                def _():
                    arrived(self.from_right(part, pm), self.right_in.at[part.index, pm])
                    self.add(self.half(part, pm, q, x), self.from_right(part, pm))

                send(self.half(part, pm, q, x), self.from_right(part, pm), self.left_out.at[part.index, pm], self.right_in.at[part.index, pm], device(self.dims, p - 1, q, x, c))

    def last_stage(self, part):
        far, near, across, cores = self.dims
        p, q, x, c = self.at
        into = self.out.at[pl.ds(part.out_row, part.depth)]
        into[...] = self.half(part, p, q, x)[...]

        @pl.when(p > 0)
        def _():
            arrived(self.from_left(part, p), self.left_in.at[part.index, p])
            self.add(into, self.from_left(part, p))

        @pl.when(p < far - 1)
        def _():
            arrived(self.from_right(part, p), self.right_in.at[part.index, p])
            self.add(into, self.from_right(part, p))

    def end(self, part):
        far, near, across, cores = self.dims
        p, q, x, c = self.at
        left_source(self.half(part), self.core_sems.at[0, part.index])
        for i, _ in enumerate(self.peers(part.turned)):
            left_source(self.from_first(part, i), self.first_out.at[part.index, i])
        for i, _ in enumerate(self.peers(not part.turned)):
            left_source(self.from_next(part, i), self.next_out.at[part.index, i])
        for pp in range(far):
            @pl.when(pp > p)
            def _(pp=pp):
                left_source(self.from_left(part, pp), self.right_out.at[part.index, pp])

            @pl.when(pp < p)
            def _(pp=pp):
                left_source(self.from_right(part, pp), self.left_out.at[part.index, pp])


def reduce_scratch(dims, pieces, parts, depth, width):
    far, near, across, cores = dims
    dma = pltpu.SemaphoreType.DMA
    bufs = [
        pltpu.VMEM((pieces, far, near, across, depth, width), f32),
        pltpu.VMEM((pieces, max(across - 1, 1), far, near, depth, width), f32),
        pltpu.VMEM((pieces, max(near - 1, 1), far, depth, width), f32),
        pltpu.VMEM((pieces, far, depth, width), f32),
        pltpu.VMEM((pieces, far, depth, width), f32),
    ]
    sems = [
        dma((2, parts)),
        dma((parts, max(across - 1, 1))),
        dma((parts, max(across - 1, 1))),
        dma((parts, max(near - 1, 1))),
        dma((parts, max(near - 1, 1))),
    ] + [dma((parts, far))] * 4
    return bufs, sems


def forward_kernel(dims, chunks, adj, sent, out, pair, pool, *sems):
    at = place(dims)
    entry_barrier(dims, at)
    forward_pass(dims, at, chunks, adj, sent, out, pair, pool, sems, Hooks())


def backward_kernel(dims, chunks, adj, sent, out, pair, pool, *sems):
    at = place(dims)
    entry_barrier(dims, at)
    backward_pass(dims, at, chunks, adj, sent, out, pair, pool, sems, Hooks())


def aggregate(dims, name_id, adj, sent, backward=False):
    far, near, across, cores = dims
    nodes, width = sent.shape
    chunks = width // LANES
    kernel = backward_kernel if backward else forward_kernel
    blocks = backward_blocks if backward else forward_blocks
    sems = backward_sems if backward else forward_sems
    depth = (across * cores if backward else far * near) * nodes
    return pl.pallas_call(
        functools.partial(kernel, dims, chunks),
        out_shape=jax.ShapeDtypeStruct((nodes, width), f32),
        in_specs=[pl.BlockSpec(memory_space=pltpu.VMEM)] * 2,
        out_specs=pl.BlockSpec(memory_space=pltpu.VMEM),
        scratch_shapes=[
            pltpu.VMEM((depth, 2 * LANES), bf16),
            pltpu.VMEM((blocks_of(blocks(dims, chunks)), nodes, LANES), f32),
        ]
        + sems(dims, chunks),
        compiler_params=pltpu.CompilerParams(
            collective_id=name_id, has_side_effects=True, vmem_limit_bytes=60 * 2**20
        ),
    )(adj, sent)


def contract(left, right, over):
    first, second = halves(left), halves(right)

    def go(a, b):
        return lax.dot_general(a, b, (over, ((), ())), preferred_element_type=f32)

    return go(first[0], second[0]) + (go(first[0], second[1]) + go(first[1], second[0]))


def plain(left, right):
    return contract(left, right, ((1,), (0,)))


def left_flip(left, right):
    return contract(left, right, ((0,), (0,)))


def right_flip(left, right):
    return contract(left, right, ((1,), (1,)))


def rows_of(every, half, start, size):
    far = every.shape[0]
    value = every[half * (far // 2) : (half + 1) * (far // 2), :, :, :, start : start + size, :]
    return value.reshape(-1, value.shape[-1])


def put_rows(every, half, start, size, value):
    far = every.shape[0]
    shape = (far // 2,) + every.shape[1:4] + (size, value.shape[-1])
    every[half * (far // 2) : (half + 1) * (far // 2), :, :, :, start : start + size, :] = value.reshape(shape)


def activation(pre_act):
    sig = jax.nn.sigmoid(pre_act)
    act = pre_act * sig
    return sig, act, lax.rsqrt(jnp.mean(act * act, -1, keepdims=True) + norm_eps)


def column_of(row):
    size = row.shape[1]
    same = lax.broadcasted_iota(jnp.int32, (size, size), 0) == lax.broadcasted_iota(jnp.int32, (size, size), 1)
    return jnp.sum(jnp.where(same, jnp.broadcast_to(row, (size, size)), 0.0), 1, keepdims=True)


def row_of(column):
    size = column.shape[0]
    same = lax.broadcasted_iota(jnp.int32, (size, size), 0) == lax.broadcasted_iota(jnp.int32, (size, size), 1)
    return jnp.sum(jnp.where(same, jnp.broadcast_to(column, (size, size)), 0.0), 0, keepdims=True)


def blend(old, mean_square):
    return 0.5 * old + 0.5 * (mean_square + stat_eps)


def row_statistic(grad, old, count):
    square = grad * grad
    return square, blend(old, jnp.sum(square, 1, keepdims=True) / count)


def train_kernel(dims, in_width, classes, adj_hbm, feats, info, w_in_t, w_side, w_proj, w_out, col_in, row_side, row_proj, row_out, red, stat, refs):
    far, near, across, cores = dims
    at = place(dims)
    nodes, wide_in = feats.shape
    layers, block, width = w_side.shape
    every = [refs["every%d" % layer] for layer in range(layers)]
    adj, stage, stage_sems = refs["adj"], refs["stage"], refs["stage_sems"]
    pair, pool, sent = refs["pair"], refs["pool"], refs["sent"]
    raw, inverse, mix, direct, back = refs["raw"], refs["inverse"], refs["mix"], refs["direct"], refs["back"]
    agg, hid, pre, outer, ready = refs["agg"], refs["hid"], refs["pre"], refs["outer"], refs["ready"]
    in_chunks, chunks = wide_in // LANES, width // LANES
    head = 2 * block
    tail = wide_in - width + LANES

    strip = stage.shape[1]

    def strip_copy(i):
        return pltpu.make_async_copy(adj_hbm.at[pl.ds(i * strip, strip)], stage.at[i % 2], stage_sems.at[i % 2])

    strips = adj.shape[0] // strip
    strip_copy(0).start()
    strip_copy(1).start()
    for layer in range(layers):
        mine = every[layer].at[at]
        mine[:block] = w_side[layer]
        mine[block : 2 * block] = w_proj[layer]
    mine = every[0].at[at]
    mine[head : head + block // 2] = w_in_t[:, :width]
    mine[head + block // 2 : head + block, : wide_in - width] = w_in_t[:, width:]
    mine[head + block // 2 : head + block, wide_in - width : tail] = jnp.zeros((block // 2, LANES), f32)
    mine[head + block // 2 : head + block, wide_in - width : wide_in - width + classes] = w_out[...]
    marked = jnp.sum(info[:, LANES + 2 : LANES + 3], 0, keepdims=True)
    mine[head + block // 2 : head + block, tail:] = jnp.broadcast_to(marked, (block // 2, width - tail))
    entry_barrier(dims, at)
    target = info[:, :LANES]
    alpha = info[:, LANES : LANES + 1]
    weight = info[:, LANES + 1 : LANES + 2]
    lane = lax.broadcasted_iota(jnp.int32, (nodes, wide_in), 1)
    sent[...] = jnp.where(lane == in_width, 1.0, feats[...] * alpha)

    def load_adjacency():
        for i in range(strips):
            strip_copy(i).wait()
            adj[i * strip : (i + 1) * strip, :] = stage[i % 2].astype(f32).astype(bf16)
            if i + 2 < strips:
                strip_copy(i + 2).start()

    spreads = [SpreadAll(dims, at, every[l], *refs["spread%d" % l]) for l in range(layers)]

    def mixing(layer):
        for half in range(2):
            side = rows_of(every[layer], half, 0, block)
            proj = rows_of(every[layer], half, block, block)
            mix[layer % 2, half] = plain(side, proj)

    def input_weights():
        def both(start):
            return jnp.concatenate([rows_of(every[0], half, start, block // 2) for half in range(2)], 0)

        first, second = both(head), both(head + block // 2)
        return jnp.concatenate([first, second[:, : wide_in - width]], 1)

    def ahead(layer):
        spreads[layer].end()
        mixing(layer)
        if layer == 0:
            hid[0] = right_flip(feats[...], input_weights())
        direct[...] = plain(hid[layer], mix[layer % 2, 0])

    rounds = iter(range(ready.shape[0]))
    for layer in range(layers):
        acts = {}
        now = spreads[layer]
        if layer == 0:
            acts = {"begin": [now.begin], "sent": [load_adjacency], "step1": [functools.partial(now.step, 1)], "step2": [functools.partial(now.step, 2)], "step3": [functools.partial(now.step, 3)], "drain": [now.drain], "shadow": [functools.partial(ahead, 0)]}
        else:
            acts = {"sent": [functools.partial(now.step, 2)], "step2": [functools.partial(now.step, 3)], "step3": [now.drain, functools.partial(ahead, layer)]}
        if layer + 1 < layers:
            after = spreads[layer + 1]
            for name, act in [("drain", after.begin), ("last", functools.partial(after.step, 1))]:
                acts[name] = acts.get(name, []) + [act]
        if layer == 0:
            forward_pass(dims, at, in_chunks, adj, sent, raw, pair, pool, refs["forward"], Hooks(**acts))
            turn = ready.at[next(rounds)]
            announce(dims, at, turn)
            inverse[...] = jnp.broadcast_to(1.0 / (1.0 + raw[:, in_width : in_width + 1]), inverse.shape)
            raw[...] = jnp.where(lane < in_width, raw[...] * inverse[:, 0:1], 0.0)
            agg[0] = right_flip(raw[...], input_weights())
        else:
            forward_pass(dims, at, chunks, adj, sent, agg.at[layer], pair, pool, refs["forward"], Hooks(**acts))
            turn = ready.at[next(rounds)]
            announce(dims, at, turn)
            agg[layer] = agg[layer] * inverse[:, 0:1]
        pre_act = direct[...] + plain(agg[layer], mix[layer % 2, 1])
        pre[layer] = pre_act
        _, act, scale = activation(pre_act)
        after = act * scale
        hid[layer + 1] = after
        if layer + 1 < layers:
            sent[:, :width] = after * alpha
        await_all(dims, at, turn)

    def output_weights():
        at_lane = wide_in - width
        return jnp.concatenate(
            [rows_of(every[0], half, head + block // 2, block // 2)[:, at_lane : at_lane + LANES] for half in range(2)], 0
        )

    labelled = jnp.sum(every[0][:, :, :, :, head + block // 2 : head + block // 2 + 8, tail : tail + LANES].reshape(-1, 8, LANES), 0)[0:1, 0:1]
    refs["marks"][...] = jnp.broadcast_to(labelled, refs["marks"].shape)
    head_weights = output_weights()
    logits = plain(hid[layers], head_weights)
    column = lax.broadcasted_iota(jnp.int32, logits.shape, 1)
    soft = jnp.maximum(logits, 0.0) + jnp.log(1.0 + jnp.exp(-jnp.abs(logits)))
    each = jnp.where(column < classes, soft - target * logits, 0.0)
    loss = jnp.sum(weight * jnp.sum(each, -1, keepdims=True), 0, keepdims=True)
    d_logits = jnp.where(column < classes, (weight / labelled) * (jax.nn.sigmoid(logits) - target), 0.0)
    g_out = left_flip(hid[layers], d_logits)
    d_out = right_flip(d_logits, head_weights)
    start = head + block // 2
    half_rows = width // 2
    for half in range(2):
        piece = jnp.concatenate(
            [
                jnp.zeros((half_rows, wide_in - width), f32),
                g_out[half * half_rows : (half + 1) * half_rows],
                jnp.broadcast_to(loss, (half_rows, width - tail)),
            ],
            1,
        )
        put_rows(every[0], half, start, block // 2, piece)

    reduces = [ReduceAll(dims, at, every[l], red, refs["reduce_bufs"], refs["reduce_sems"]) for l in range(layers)]

    def slope(layer, d_out):
        pre_act = pre[layer]
        sig, act, scale = activation(pre_act)
        normed = act * scale
        d_act = scale * (d_out - normed * jnp.mean(d_out * normed, -1, keepdims=True))
        return d_act * sig * (1.0 + pre_act * (1.0 - sig))

    def outers(layer, d_pre):
        outer[0] = left_flip(hid[layer], d_pre)
        outer[1] = left_flip(agg[layer], d_pre)

    def weight_grads(layer, half):
        side = rows_of(every[layer], half, 0, block)
        proj = rows_of(every[layer], half, block, block)
        g_side = right_flip(outer[half], proj)
        g_proj = left_flip(side, outer[half])
        put_rows(every[layer], half, 0, block, g_side)
        put_rows(every[layer], half, block, block, g_proj)

    base = [0, 3 * block, 5 * block]
    sums = refs["sums"]
    sums[...] = jnp.zeros_like(sums)
    spot = lax.broadcasted_iota(jnp.int32, (1, wide_in), 1)
    slot = 2 * layers

    def note_total(index, new_row):
        total = jnp.sum(new_row, 0, keepdims=True)
        sums[slot + 1 : slot + 2] = sums[slot + 1 : slot + 2] + jnp.where(spot == LANES + index, total, 0.0)

    def note_layer(layer):
        for kind, old in enumerate((row_side, row_proj)):
            start = base[layer] + kind * block
            square, new_row = row_statistic(red[start : start + block], column_of(old[layer : layer + 1]), width)
            index = kind * layers + layer
            sums[index : index + 1, :width] = jnp.sum(square, 0, keepdims=True)
            sums[slot + 2 + index : slot + 3 + index, :width] = jnp.sum(square / new_row, 0, keepdims=True)
            note_total(index, new_row)

    def note_head():
        first, second = red[head : head + block // 2], red[head + block // 2 : head + block]
        square = jnp.concatenate([first * first, second[:, : wide_in - width] * second[:, : wide_in - width]], 1)
        new_col = blend(column_of(col_in[...]), jnp.sum(square, 1, keepdims=True) / in_width)
        sums[slot : slot + 1] = jnp.sum(square, 0, keepdims=True)
        sums[2 * slot + 2 : 2 * slot + 3] = jnp.sum(square / new_col, 0, keepdims=True)
        square, new_row = row_statistic(second[:, wide_in - width : tail], column_of(row_out[...]), classes)
        sums[slot + 1 : slot + 2, :LANES] = jnp.sum(square, 0, keepdims=True)
        sums[2 * slot + 3 : 2 * slot + 4, :LANES] = jnp.sum(square / new_row, 0, keepdims=True)
        note_total(slot, new_row)

    def sum_everywhere(stat):
        far, near, across, cores = dims
        p, q, x, c = at
        came_in, out_sems, in_sems = refs["sum_in"], refs["sum_out"], refs["sum_came"]
        groups = [
            [device(dims, p, q, x, 1 - c)],
            [device(dims, p, q, lax.rem(x + step, across), c) for step in range(1, across)],
            [device(dims, p, lax.rem(q + step, near), x, c) for step in range(1, near)],
            [device(dims, *other) for other in line_peers(dims, at)],
        ]
        base_slot = 0
        for turn, group in enumerate(groups):
            for i, target in enumerate(group):
                at_slot = base_slot + i
                send(sums.at[pl.ds(turn * stat.shape[0], stat.shape[0])], came_in.at[at_slot], out_sems.at[at_slot], in_sems.at[at_slot], target)
            total = sums[turn * stat.shape[0] : (turn + 1) * stat.shape[0]]
            for i in range(len(group)):
                at_slot = base_slot + i
                arrived(came_in.at[at_slot], in_sems.at[at_slot])
                total = total + came_in[at_slot]
            base_slot += len(group)
            if turn + 1 < len(groups):
                sums[(turn + 1) * stat.shape[0] : (turn + 2) * stat.shape[0]] = total
            else:
                stat[...] = total
                stat[2 * slot + 4 : 2 * slot + 5, :LANES] = jnp.broadcast_to(refs["marks"][0:1, 0:1], (1, LANES))
        for at_slot in range(base_slot):
            left_source(came_in.at[at_slot], out_sems.at[at_slot])


    def finish_reduce(layer, parts):
        for part in parts:
            reduces[layer].last_stage(part)
        for part in parts:
            reduces[layer].end(part)
        note_layer(layer)

    d_pre_ref = refs["d_pre"]
    carried, freed = [], []
    for layer in range(layers - 1, 0, -1):
        d_pre_ref[...] = slope(layer, d_out)
        sent[:, :width] = d_pre_ref[...] * inverse[:, 0:1]
        first = 2 * ((layers - 1 - layer) % 2)
        parts = [
            Part(first + kind, first + kind, 0, block, kind * block, base[layer] + kind * block, False) for kind in range(2)
        ]

        def begin_grads(layer=layer):
            outers(layer, d_pre_ref[...])
            weight_grads(layer, 0)

        def more_grads(layer=layer, parts=parts):
            weight_grads(layer, 1)
            for part in parts:
                reduces[layer].core_stage(part)

        def direct_part(layer=layer):
            direct[...] = right_flip(d_pre_ref[...], mix[layer % 2, 0])

        def stage(name, layer=layer, parts=parts):
            for part in parts:
                getattr(reduces[layer], name)(part)

        acts = {
            "sent": carried[:1] + [begin_grads],
            "chunk0": carried[1:],
            "chunk1": [more_grads],
            "chunk2": [direct_part, functools.partial(stage, "across_stage")],
            "early": [functools.partial(mixing, 0)] if layer == 1 else [],
            "line": [functools.partial(stage, "near_stage")],
        }
        backward_pass(dims, at, chunks, adj, sent, back, pair, pool, refs["backward"], Hooks(**acts))
        if layer > 1:
            turn = ready.at[next(rounds)]
            announce(dims, at, turn)
        d_out = direct[...] + right_flip(back[...] * alpha, mix[layer % 2, 1])
        if layer > 1:
            await_all(dims, at, turn)

        def close(layer=layer, parts=parts):
            finish_reduce(layer, parts)
            if layer == layers - 1 or layer == 1:
                freed.append(ready.at[next(rounds)])
                announce(dims, at, freed[-1])

        carried = [functools.partial(stage, "line_stage"), close]

    d_pre = slope(0, d_out)
    d_pre_ref[...] = d_pre
    d_self = right_flip(d_pre, mix[0, 0])
    d_neigh = right_flip(d_pre, mix[0, 1])
    g_in = left_flip(d_self, feats[...]) + left_flip(d_neigh, raw[...])
    for half in range(2):
        top = slice(half * half_rows, (half + 1) * half_rows)
        put_rows(every[0], half, head, block // 2, g_in[top, :width])
        where = (slice(half * (far // 2), (half + 1) * (far // 2)),) + (slice(None),) * 3
        value = g_in[top, width:]
        every[0][where + (slice(head + block // 2, head + block), slice(0, wide_in - width))] = value.reshape(
            (far // 2, near, across, cores, block // 2, wide_in - width)
        )
    await_all(dims, at, freed.pop(0))
    final = reduces[0]
    depth = block // 2
    order = [
        Part(index + turned, piece, turned * depth, depth, kind * block + turned * depth, kind * block + turned * depth, turned == 1 and near == across)
        for kind, piece, index in ((2, 0, 0), (0, 1, 4), (1, 2, 2))
        for turned in range(2)
    ]

    def go(name, parts):
        for part in parts:
            getattr(final, name)(part)

    go("core_stage", order[:2])
    carried[0]()
    outers(0, d_pre)
    go("across_stage", order[:2])
    weight_grads(0, 0)
    go("near_stage", order[:2])
    weight_grads(0, 1)
    go("core_stage", order[2:4])
    carried[1]()
    go("across_stage", order[2:4])
    await_all(dims, at, freed.pop(0))
    go("core_stage", order[4:])
    go("line_stage", order[:2])
    go("across_stage", order[4:])
    go("near_stage", order[2:])
    go("line_stage", order[2:])
    finish_reduce(0, order)
    note_head()
    sum_everywhere(stat)


def update_kernel(in_width, classes, red, stat, w_in_t, w_side, w_proj, w_out, row_in, col_in, row_side, col_side, row_proj, col_proj, row_out, col_out, loss, count, g_in, g_side, g_proj, g_out, n_in, n_side, n_proj, n_out, s_row_in, s_col_in, s_row_side, s_col_side, s_row_proj, s_col_proj, s_row_out, s_col_out):
    layers, block, width = w_side.shape
    head = 2 * block
    wide_in = w_in_t.shape[1]
    tail = wide_in - width + LANES
    slot = 2 * layers
    base = [0, 3 * block, 5 * block]

    def step_of(weight, grad, new_row, new_col, mean, over, size):
        update = grad * lax.rsqrt(new_row * new_col / mean)
        factor = 1.0 / jnp.maximum(1.0, jnp.sqrt(mean * over / size) / clip_level)
        return weight - step_rate * (update * factor)

    def total_of(index):
        return stat[slot + 1 : slot + 2, LANES + index : LANES + index + 1]

    kinds = (
        (w_side, row_side, col_side, g_side, n_side, s_row_side, s_col_side),
        (w_proj, row_proj, col_proj, g_proj, n_proj, s_row_proj, s_col_proj),
    )
    for layer in range(layers):
        for kind, (weight, row, col, g, n, s_row, s_col) in enumerate(kinds):
            start = base[layer] + kind * block
            index = kind * layers + layer
            grad = red[start : start + block]
            _, new_row = row_statistic(grad, column_of(row[layer : layer + 1]), width)
            new_col = blend(col[layer : layer + 1], stat[index : index + 1, :width] / (2 * width))
            over = jnp.sum(stat[slot + 2 + index : slot + 3 + index, :width] / new_col, 1, keepdims=True)
            g[layer] = grad
            n[layer] = step_of(weight[layer], grad, new_row, new_col, total_of(index) / (2 * width), over, 2 * width * width)
            s_row[layer : layer + 1] = row_of(new_row)
            s_col[layer : layer + 1] = new_col
    first, second = red[head : head + block // 2], red[head + block // 2 : head + block]
    grad = jnp.concatenate([first, second[:, : wide_in - width]], 1)[:, :in_width]
    new_col = blend(column_of(col_in[...]), jnp.sum(grad * grad, 1, keepdims=True) / in_width)
    new_row = blend(row_in[...], stat[slot : slot + 1, :in_width] / width)
    mean = jnp.sum(new_row, 1, keepdims=True) / in_width
    over = jnp.sum(stat[2 * slot + 2 : 2 * slot + 3, :in_width] / new_row, 1, keepdims=True)
    g_in[...] = grad
    n_in[...] = step_of(w_in_t[:, :in_width], grad, new_col, new_row, mean, over, in_width * width)
    s_row_in[...] = new_row
    s_col_in[...] = row_of(new_col)
    grad = second[:, wide_in - width : wide_in - width + classes]
    _, new_row = row_statistic(grad, column_of(row_out[...]), classes)
    new_col = blend(col_out[...], stat[slot + 1 : slot + 2, :classes] / width)
    over = jnp.sum(stat[2 * slot + 3 : 2 * slot + 4, :classes] / new_col, 1, keepdims=True)
    g_out[...] = grad
    n_out[...] = step_of(w_out[...], grad, new_row, new_col, total_of(slot) / width, over, width * classes)
    s_row_out[...] = row_of(new_row)
    s_col_out[...] = new_col
    loss[...] = second[0:1, tail : tail + 1]
    count[...] = stat[2 * slot + 4 : 2 * slot + 5, 0:1]


def train_on_device(dims, name_id, in_width, classes, adjacency, feats, info, w_in_t, w_side, w_proj, w_out, col_in, row_side, row_proj, row_out):
    far, near, across, cores = dims
    nodes, wide_in = feats.shape
    layers, block, width = w_side.shape
    in_chunks, chunks = wide_in // LANES, width // LANES
    dma = pltpu.SemaphoreType.DMA
    pool = max(blocks_of(forward_blocks(dims, in_chunks)), blocks_of(backward_blocks(dims, chunks)))
    bufs, sems = reduce_scratch(dims, 4, 6, block, width)
    strip = 128
    stat_rows = 24
    partners = 1 + (across - 1) + (near - 1) + (far - 1)
    vmem = pl.BlockSpec(memory_space=pltpu.VMEM)
    refs = {
        "adj": pltpu.VMEM(adjacency.shape, bf16),
        "stage": pltpu.VMEM((2, strip, adjacency.shape[1]), jnp.int32),
        "stage_sems": dma((2,)),
        "pair": pltpu.VMEM((max(far * near, across * cores) * nodes, 2 * LANES), bf16),
        "pool": pltpu.VMEM((pool, nodes, LANES), f32),
        "sent": pltpu.VMEM((nodes, wide_in), f32),
        "raw": pltpu.VMEM((nodes, wide_in), f32),
        "inverse": pltpu.VMEM((nodes, LANES), f32),
        "mix": pltpu.VMEM((2, 2, width, width), f32),
        "direct": pltpu.VMEM((nodes, width), f32),
        "back": pltpu.VMEM((nodes, width), f32),
        "d_pre": pltpu.VMEM((nodes, width), f32),
        "agg": pltpu.VMEM((layers, nodes, width), f32),
        "hid": pltpu.VMEM((layers + 1, nodes, width), f32),
        "pre": pltpu.VMEM((layers, nodes, width), f32),
        "outer": pltpu.VMEM((2, width, width), f32),
        "ready": pltpu.SemaphoreType.REGULAR((3 * layers - 3,)),
        "forward": forward_sems(dims, in_chunks),
        "backward": backward_sems(dims, chunks),
        "sums": pltpu.VMEM((4 * stat_rows, wide_in), f32),
        "sum_in": pltpu.VMEM((partners, stat_rows, wide_in), f32),
        "sum_out": dma((partners,)),
        "sum_came": dma((partners,)),
        "marks": pltpu.VMEM((8, LANES), f32),
        "reduce_bufs": bufs,
        "reduce_sems": sems,
    }
    for layer in range(layers):
        refs["every%d" % layer] = pltpu.VMEM(dims + ((3 if layer == 0 else 2) * block, width), f32)
        refs["spread%d" % layer] = spread_sems(dims)
    return pl.pallas_call(
        functools.partial(train_kernel, dims, in_width, classes),
        out_shape=(
            jax.ShapeDtypeStruct((7 * block, width), f32),
            jax.ShapeDtypeStruct((stat_rows, wide_in), f32),
        ),
        in_specs=[pl.BlockSpec(memory_space=pl.ANY)] + [vmem] * 10,
        out_specs=(vmem, vmem),
        scratch_shapes=[refs],
        compiler_params=pltpu.CompilerParams(
            collective_id=name_id, has_side_effects=True, vmem_limit_bytes=63 * 2**20
        ),
    )(adjacency, feats, info, w_in_t, w_side, w_proj, w_out, col_in, row_side, row_proj, row_out)


def update_on_device(in_width, classes, *arrays):
    w_side, w_out = arrays[3], arrays[5]
    layers, block, width = w_side.shape
    shapes = [
        (1, 1),
        (1, 1),
        (block // 2, in_width),
        w_side.shape,
        w_side.shape,
        w_out.shape,
        (block // 2, in_width),
        w_side.shape,
        w_side.shape,
        w_out.shape,
        (1, in_width),
        (1, block // 2),
        (layers, block),
        (layers, width),
        (layers, block),
        (layers, width),
        (1, block // 2),
        (1, classes),
    ]
    vmem = pl.BlockSpec(memory_space=pltpu.VMEM)
    return pl.pallas_call(
        functools.partial(update_kernel, in_width, classes),
        out_shape=[jax.ShapeDtypeStruct(shape, f32) for shape in shapes],
        in_specs=[vmem] * len(arrays),
        out_specs=[vmem] * len(shapes),
    )(*arrays)


def dot(left, right, over=((1,), (0,))):
    return lax.dot_general(
        left, right, (over, ((), ())), precision=lax.Precision.HIGH, preferred_element_type=f32
    )


def left_t(left, right):
    return dot(left, right, ((0,), (0,)))


def right_t(left, right):
    return dot(left, right, ((1,), (1,)))


def pad_lanes(value, lanes):
    return jnp.pad(value, ((0, 0), (0, lanes - value.shape[1])))


def fits_on_chip(adjacency):
    return 2 * adjacency.shape[0] * adjacency.shape[1] <= 4 * 2**20


def step_fused(
    dims,
    features,
    adjacency,
    labels,
    labelled,
    node_count,
    w_in,
    w_side,
    w_proj,
    w_out,
    row_in,
    col_in,
    row_side,
    col_side,
    row_proj,
    col_proj,
    row_out,
    col_out,
):
    nodes, in_width = features.shape
    classes = w_out.shape[1]
    wide_in = -(-(in_width + 1) // LANES) * LANES
    counts = node_count.astype(f32)
    mask = labelled.astype(f32)
    lane = lax.broadcasted_iota(jnp.int32, (nodes, LANES), 1)
    facts = jnp.where(
        lane == 0,
        (2.0 / (1.0 + counts))[:, None],
        jnp.where(lane == 1, (mask * lax.rsqrt(counts))[:, None], jnp.where(lane == 2, mask[:, None], 0.0)),
    )
    info = jnp.concatenate([pad_lanes(labels.astype(f32), LANES), facts], 1)
    w_in_t = pad_lanes(w_in.T, wide_in)
    local = (w_in_t, w_side, w_proj, w_out)
    red, stat = train_on_device(
        dims, 1, in_width, classes, adjacency, pad_lanes(features, wide_in), info, *local,
        col_in[None], row_side, row_proj, row_out[None],
    )
    done = update_on_device(
        in_width, classes, red, stat, *local,
        row_in[None], col_in[None], row_side, col_side, row_proj, col_proj, row_out[None], col_out[None],
    )
    (loss, count, g_in, g_side, g_proj, g_out, n_in, n_side, n_proj, n_out,
     s_row_in, s_col_in, s_row_side, s_col_side, s_row_proj, s_col_proj, s_row_out, s_col_out) = done
    return (
        loss[0, 0],
        count[0, 0],
        g_in.T,
        g_side,
        g_proj,
        g_out,
        n_in.T,
        n_side,
        n_proj,
        n_out,
        s_row_in[0],
        s_col_in[0],
        s_row_side,
        s_col_side,
        s_row_proj,
        s_col_proj,
        s_row_out[0],
        s_col_out[0],
    )


def step_apart(
    dims,
    features,
    adjacency,
    labels,
    labelled,
    node_count,
    w_in,
    w_side,
    w_proj,
    w_out,
    row_in,
    col_in,
    row_side,
    col_side,
    row_proj,
    col_proj,
    row_out,
    col_out,
):
    layers = w_side.shape[0]
    width = w_side.shape[2]
    in_width = features.shape[1]
    classes = w_out.shape[1]
    nodes = features.shape[0]
    both = ("wide", "narrow")
    adj = adjacency.astype(bf16)
    counts = node_count.astype(f32)
    alpha = 2.0 / (1.0 + counts)
    lam = lax.rsqrt(counts)
    target = labels.astype(f32)
    weight_mask = labelled.astype(f32)

    spare = -(in_width + 1) % LANES
    sent = jnp.concatenate(
        [alpha[:, None] * features, jnp.ones((nodes, 1), f32), jnp.zeros((nodes, spare), f32)], 1
    )
    summed = aggregate(dims, 1, adj, sent)
    inverse = 1.0 / (1.0 + summed[:, in_width : in_width + 1])
    agg_features = summed[:, :in_width] * inverse

    full_in, full_side, full_proj, full_out = (
        lax.all_gather(w_in, both, axis=1, tiled=True),
        lax.all_gather(w_side, both, axis=1, tiled=True),
        lax.all_gather(w_proj, both, axis=1, tiled=True),
        lax.all_gather(w_out, both, axis=0, tiled=True),
    )
    mix_self = [dot(full_side[l, :width], full_proj[l, :width]) for l in range(layers)]
    mix_neigh = [dot(full_side[l, width:], full_proj[l, width:]) for l in range(layers)]

    kept = []
    hidden = dot(features, full_in)
    agg = dot(agg_features, full_in)
    for layer in range(layers):
        if layer > 0:
            agg = aggregate(dims, 1 + layer, adj, alpha[:, None] * hidden) * inverse
        pre_act = dot(hidden, mix_self[layer]) + dot(agg, mix_neigh[layer])
        kept.append((hidden, agg, pre_act))
        act = jax.nn.silu(pre_act)
        hidden = act * lax.rsqrt(jnp.mean(act * act, -1, keepdims=True) + norm_eps)

    logits = dot(hidden, full_out)
    per = jnp.sum(jax.nn.softplus(logits) - target * logits, -1)
    loss_sum, label_count = lax.psum(
        (jnp.sum(weight_mask * lam * per), jnp.sum(weight_mask)), both
    )
    d_logits = (weight_mask * lam / label_count)[:, None] * (jax.nn.sigmoid(logits) - target)
    g_out = left_t(hidden, d_logits)
    d_out = right_t(d_logits, full_out)
    side_grads = [None] * layers
    proj_grads = [None] * layers
    for layer in reversed(range(layers)):
        hidden, agg, pre_act = kept[layer]
        sig = jax.nn.sigmoid(pre_act)
        act = pre_act * sig
        scale = lax.rsqrt(jnp.mean(act * act, -1, keepdims=True) + norm_eps)
        normed = act * scale
        d_act = scale * (d_out - normed * jnp.mean(d_out * normed, -1, keepdims=True))
        d_pre = d_act * sig * (1.0 + pre_act * (1.0 - sig))
        outer_self = left_t(hidden, d_pre)
        outer_neigh = left_t(agg, d_pre)
        side, proj = full_side[layer], full_proj[layer]
        side_grads[layer] = jnp.concatenate(
            [right_t(outer_self, proj[:width]), right_t(outer_neigh, proj[width:])], 0
        )
        proj_grads[layer] = jnp.concatenate(
            [left_t(side[:width], outer_self), left_t(side[width:], outer_neigh)], 0
        )
        d_self = right_t(d_pre, mix_self[layer])
        if layer > 0:
            back = aggregate(dims, 3 + layer, adj, d_pre * inverse, backward=True)
            d_out = d_self + right_t(alpha[:, None] * back, mix_neigh[layer])
        else:
            g_in = left_t(features, d_self) + left_t(agg_features, right_t(d_pre, mix_neigh[layer]))
    red_in, red_side, red_proj, red_out = (
        lax.psum_scatter(g_in, both, scatter_dimension=1, tiled=True),
        lax.psum_scatter(jnp.stack(side_grads), both, scatter_dimension=1, tiled=True),
        lax.psum_scatter(jnp.stack(proj_grads), both, scatter_dimension=1, tiled=True),
        lax.psum_scatter(g_out, both, scatter_dimension=0, tiled=True),
    )
    sq_in = red_in * red_in
    sq_side = red_side * red_side
    sq_proj = red_proj * red_proj
    sq_out = red_out * red_out
    new_col_in = 0.5 * col_in + 0.5 * (jnp.mean(sq_in, 0) + stat_eps)
    new_row_side = 0.5 * row_side + 0.5 * (jnp.mean(sq_side, 2) + stat_eps)
    new_row_proj = 0.5 * row_proj + 0.5 * (jnp.mean(sq_proj, 2) + stat_eps)
    new_row_out = 0.5 * row_out + 0.5 * (jnp.mean(sq_out, 1) + stat_eps)
    (
        sum_row_in,
        sum_col_side,
        sum_col_proj,
        sum_col_out,
        total_side,
        total_proj,
        total_out,
        over_in,
        over_side,
        over_proj,
        over_out,
    ) = lax.psum(
        (
            jnp.sum(sq_in, 1),
            jnp.sum(sq_side, 1),
            jnp.sum(sq_proj, 1),
            jnp.sum(sq_out, 0),
            jnp.sum(new_row_side, 1),
            jnp.sum(new_row_proj, 1),
            jnp.sum(new_row_out),
            jnp.sum(sq_in / new_col_in[None, :], 1),
            jnp.sum(sq_side / new_row_side[:, :, None], 1),
            jnp.sum(sq_proj / new_row_proj[:, :, None], 1),
            jnp.sum(sq_out / new_row_out[:, None], 0),
        ),
        both,
    )
    new_row_in = 0.5 * row_in + 0.5 * (sum_row_in / width + stat_eps)
    new_col_side = 0.5 * col_side + 0.5 * (sum_col_side / (2 * width) + stat_eps)
    new_col_proj = 0.5 * col_proj + 0.5 * (sum_col_proj / (2 * width) + stat_eps)
    new_col_out = 0.5 * col_out + 0.5 * (sum_col_out / width + stat_eps)
    mean_in = jnp.mean(new_row_in)
    mean_side = total_side / (2 * width)
    mean_proj = total_proj / (2 * width)
    mean_out = total_out / width
    up_in = red_in * lax.rsqrt(new_row_in[:, None] * new_col_in[None, :] / mean_in)
    up_side = red_side * lax.rsqrt(
        new_row_side[:, :, None] * new_col_side[:, None, :] / mean_side[:, None, None]
    )
    up_proj = red_proj * lax.rsqrt(
        new_row_proj[:, :, None] * new_col_proj[:, None, :] / mean_proj[:, None, None]
    )
    up_out = red_out * lax.rsqrt(new_row_out[:, None] * new_col_out[None, :] / mean_out)
    ms_in = mean_in * jnp.sum(over_in / new_row_in) / (in_width * width)
    ms_side = mean_side * jnp.sum(over_side / new_col_side, 1) / (2 * width * width)
    ms_proj = mean_proj * jnp.sum(over_proj / new_col_proj, 1) / (2 * width * width)
    ms_out = mean_out * jnp.sum(over_out / new_col_out) / (width * classes)
    fac_in = 1.0 / jnp.maximum(1.0, jnp.sqrt(ms_in) / clip_level)
    fac_side = 1.0 / jnp.maximum(1.0, jnp.sqrt(ms_side) / clip_level)
    fac_proj = 1.0 / jnp.maximum(1.0, jnp.sqrt(ms_proj) / clip_level)
    fac_out = 1.0 / jnp.maximum(1.0, jnp.sqrt(ms_out) / clip_level)
    new_in = w_in - step_rate * (up_in * fac_in)
    new_side = w_side - step_rate * (up_side * fac_side[:, None, None])
    new_proj = w_proj - step_rate * (up_proj * fac_proj[:, None, None])
    new_out = w_out - step_rate * (up_out * fac_out)
    return (
        loss_sum,
        label_count,
        red_in,
        red_side,
        red_proj,
        red_out,
        new_in,
        new_side,
        new_proj,
        new_out,
        new_row_in,
        new_col_in,
        new_row_side,
        new_col_side,
        new_row_proj,
        new_col_proj,
        new_row_out,
        new_col_out,
    )


def step_on_device(dims, features, adjacency, *others):
    step = step_fused if dims[0] == 4 and fits_on_chip(adjacency) else step_apart
    return step(dims, features, adjacency, *others)


def solution(mesh):
    in_specs = (
        P(("wide", "narrow"), None),
        P("wide", "narrow"),
        P(("wide", "narrow"), None),
        P(("wide", "narrow")),
        P(("wide", "narrow")),
        P(None, ("wide", "narrow")),
        P(None, ("wide", "narrow"), None),
        P(None, ("wide", "narrow"), None),
        P(("wide", "narrow"), None),
        P(),
        P(("wide", "narrow")),
        P(None, ("wide", "narrow")),
        P(),
        P(None, ("wide", "narrow")),
        P(),
        P(("wide", "narrow")),
        P(),
    )
    out_specs = (
        P(),
        P(),
        P(None, ("wide", "narrow")),
        P(None, ("wide", "narrow"), None),
        P(None, ("wide", "narrow"), None),
        P(("wide", "narrow"), None),
        P(None, ("wide", "narrow")),
        P(None, ("wide", "narrow"), None),
        P(None, ("wide", "narrow"), None),
        P(("wide", "narrow"), None),
        P(),
        P(("wide", "narrow")),
        P(None, ("wide", "narrow")),
        P(),
        P(None, ("wide", "narrow")),
        P(),
        P(("wide", "narrow")),
        P(),
    )
    shards = functools.partial(step_on_device, grid_of(mesh))
    return jax.shard_map(shards, mesh=mesh, in_specs=in_specs, out_specs=out_specs, check_vma=False)
```
